32 devices in a mesh: heads: 4 (over y, x), blk: 8 (over z, core).
Axes of the slice: x: 2, y: 2, z: 4, core: 2. Of those that a mesh axis runs over, the one named last changes fastest.
Arguments:
- tokens: bfloat16 [2, 2048, 1024], P(None, ('blk', 'heads')), may hold values from -10.5 to 10.5
- cotangent: bfloat16 [2, 2048, 1024], P(None, ('blk', 'heads')), may hold values from -6 to 6
- doc_offsets: int32 [2, 16], replicated, may hold values from 0 to 2047, as said below
- valid_flags: int32 [2, 2048], replicated, may hold values 0 or 1
- w_query: bfloat16 [1024, 1024], P(('blk', 'heads')), may hold values from -0.1875 to 0.1875
- w_key: bfloat16 [1024, 1024], P(('blk', 'heads')), may hold values from -0.1875 to 0.1875
- w_value: bfloat16 [1024, 1024], P(('blk', 'heads')), may hold values from -0.1875 to 0.1875
- w_out: bfloat16 [1024, 1024], P(('blk', 'heads')), may hold values from -1.5 to 1.5
- w_fc1: bfloat16 [1024, 4096], P(('blk', 'heads')), may hold values from -0.1875 to 0.1875
- w_fc2: bfloat16 [4096, 1024], P(('blk', 'heads')), may hold values from -0.09375 to 0.09375
- b_query: bfloat16 [1024], P(('blk', 'heads')), may hold values from -3 to 3
- b_value: bfloat16 [1024], P(('blk', 'heads')), may hold values from -2 to 2
- b_out: bfloat16 [1024], P(('blk', 'heads')), may hold values from -2 to 2
- b_fc1: bfloat16 [4096], P(('blk', 'heads')), may hold values from -3 to 3
- b_fc2: bfloat16 [1024], P(('blk', 'heads')), may hold values from -2 to 2
- gain_attn: bfloat16 [1024], P(('blk', 'heads')), may hold values from 0.5 to 1.5
- bias_attn: bfloat16 [1024], P(('blk', 'heads')), may hold values from -2 to 2
- gain_ffn: bfloat16 [1024], P(('blk', 'heads')), may hold values from 0.5 to 1.5
- bias_ffn: bfloat16 [1024], P(('blk', 'heads')), may hold values from -2 to 2
Outputs:
- output: bfloat16 [2, 2048, 1024], P(None, ('blk', 'heads'))
- grad_tokens: float32 [2, 2048, 1024], P(None, ('blk', 'heads'))
- grad_w_query: float32 [1024, 1024], P(('blk', 'heads'))
- grad_w_key: float32 [1024, 1024], P(('blk', 'heads'))
- grad_w_value: float32 [1024, 1024], P(('blk', 'heads'))
- grad_w_out: float32 [1024, 1024], P(('blk', 'heads'))
- grad_w_fc1: float32 [1024, 4096], P(('blk', 'heads'))
- grad_w_fc2: float32 [4096, 1024], P(('blk', 'heads'))
- grad_b_query: float32 [1024], P(('blk', 'heads'))
- grad_b_value: float32 [1024], P(('blk', 'heads'))
- grad_b_out: float32 [1024], P(('blk', 'heads'))
- grad_b_fc1: float32 [4096], P(('blk', 'heads'))
- grad_b_fc2: float32 [1024], P(('blk', 'heads'))
- grad_gain_attn: float32 [1024], P(('blk', 'heads'))
- grad_bias_attn: float32 [1024], P(('blk', 'heads'))
- grad_gain_ffn: float32 [1024], P(('blk', 'heads'))
- grad_bias_ffn: float32 [1024], P(('blk', 'heads'))
- rms: float32 [4], replicated
The draws below stay inside these ranges and needn't reach their ends.
Inputs may be any that keep to these rules, and one draw needn't show every extreme that they name: `doc_offsets`: each row starts with 0 and rises strictly; entry j is where document j of that sequence begins, and the last document runs to the end of the sequence.
All inputs are finite; a program needn't handle non-finite values.
Results may differ from the reference program's by a relative error of at most 0.015.
Values may be sent and summed in bfloat16 or wider, within the bound.
No kernel may reach another device: no remote copies, remote signals or barrier semaphores. Data moves between devices by JAX's collectives and lax.ppermute only.
A program may use at most 128 MiB of HBM per device.

```python
import math
import jax
import jax.numpy as jnp
from jax import lax

D = 1024
HEADS = 16
HEAD_DIM = 64
FF = 4096
SEQS = 2
NDOC = 16
LEN = 2048
BLOCK_ROWS = 256


def draw_tokens(key, part):
    key = jax.random.fold_in(key, 5)
    ramp = 1.0 + 0.75 * jnp.arange(LEN, dtype=jnp.float32) / LEN
    base = jnp.clip(jax.random.normal(key, (SEQS, LEN, D), jnp.float32), -6.0, 6.0)
    return (base * ramp[None, :, None]).astype(jnp.bfloat16)


def draw_doc_offsets(key, part):
    key = jax.random.fold_in(key, 9)
    chosen = jax.random.randint(jax.random.fold_in(key, 1), (), 0, SEQS)
    rows_list = []
    for which in range(SEQS):
        sub_key = jax.random.fold_in(key, 100 + which)
        wide_cuts = jax.random.permutation(sub_key, LEN - 1)[:NDOC - 1] + 1
        near_cuts = jax.random.permutation(jax.random.fold_in(sub_key, 7), BLOCK_ROWS - 1)[:NDOC - 1] + 1
        cuts = jnp.sort(jnp.where(chosen == which, near_cuts, wide_cuts).astype(jnp.int32))
        rows_list.append(jnp.concatenate([jnp.zeros((1,), jnp.int32), cuts]))
    return jnp.stack(rows_list)


def set_ends(drawn, own_key, smallest, high):
    spot = [jax.random.randint(jax.random.fold_in(own_key, axis), (), 0, length) for axis, length in enumerate(drawn.shape)]
    main_axis = drawn.shape.index(max(drawn.shape))
    next_to = spot[:main_axis] + [(spot[main_axis] + 1) % drawn.shape[main_axis]] + spot[main_axis + 1:]
    return drawn.at[tuple(spot)].set(smallest).at[tuple(next_to)].set(high)


def steps_of(key, dims, split, low, high):
    level, own = 1.0, jax.random.fold_in(key, 6)
    for dim, shards_of in split:
        draws = jnp.exp(jax.random.uniform(jax.random.fold_in(own, dim), (shards_of,), jnp.float32, low / len(split), high / len(split)))
        level = level * jnp.repeat(draws, dims[dim] // shards_of).reshape([-1 if axis == dim else 1 for axis in range(len(dims))])
    return level


def noise(key, shape, deviation, limit, shards=(), kind=jnp.bfloat16):
    values = jax.random.normal(key, shape, jnp.float32) * deviation
    if len(shards) > 0:
        values = steps_of(key, shape, shards, -0.22, 0.18) * values
    return jnp.clip(values, min=-limit, max=limit).astype(kind)


def setup_inputs(seed: int = 0) -> dict:
    arg_keys = jax.random.split(jax.random.key(seed), 20)
    return {
        "tokens": draw_tokens(jax.random.fold_in(arg_keys[19], 71), 0),
        "cotangent": noise(arg_keys[1], (SEQS, LEN, D), 1.0, 6.0, ((1, 32),)),
        "doc_offsets": draw_doc_offsets(jax.random.fold_in(arg_keys[19], 71), 0),
        "valid_flags": set_ends((jax.random.randint(arg_keys[3], (SEQS, LEN), 0, 8) < 7).astype(jnp.int32), jax.random.fold_in(arg_keys[3], 1), 0, 1),
        "w_query": noise(arg_keys[4], (D, D), D ** -0.5, 0.1875, ((0, 32),)),
        "w_key": noise(arg_keys[5], (D, D), D ** -0.5, 0.1875, ((0, 32),)),
        "w_value": noise(arg_keys[6], (D, D), D ** -0.5, 0.1875, ((0, 32),)),
        "w_out": noise(arg_keys[7], (D, D), (D // 64) ** -0.5, 1.5, ((0, 32),)),
        "w_fc1": noise(arg_keys[8], (D, FF), D ** -0.5, 0.1875, ((0, 32),)),
        "w_fc2": noise(arg_keys[9], (FF, D), FF ** -0.5, 0.09375, ((0, 32),)),
        "b_query": noise(arg_keys[10], (D,), 0.5, 3.0, ((0, 32),)),
        "b_value": noise(arg_keys[11], (D,), 0.3, 2.0, ((0, 32),)),
        "b_out": noise(arg_keys[12], (D,), 0.3, 2.0, ((0, 32),)),
        "b_fc1": noise(arg_keys[13], (FF,), 0.5, 3.0, ((0, 32),)),
        "b_fc2": noise(arg_keys[14], (D,), 0.3, 2.0, ((0, 32),)),
        "gain_attn": jnp.clip(1.0 + 0.1 * jax.random.normal(arg_keys[15], (D,), jnp.float32), 0.5, 1.5).astype(jnp.bfloat16),
        "bias_attn": noise(arg_keys[16], (D,), 0.3, 2.0, ((0, 32),)),
        "gain_ffn": jnp.clip(1.0 + 0.1 * jax.random.normal(arg_keys[17], (D,), jnp.float32), 0.5, 1.5).astype(jnp.bfloat16),
        "bias_ffn": noise(arg_keys[18], (D,), 0.3, 2.0, ((0, 32),)),
    }


norm_eps = 1e-05
neg_large = -1e+30

@jax.custom_vjp
def low(v):
    return lax.optimization_barrier(v.astype(jnp.bfloat16)).astype(jnp.float32)

@jax.custom_vjp
def low_back(v):
    return v

def low_keep(v):
    return (low(v), None)

def low_pass(kept, grad):
    return (grad,)

def back_keep(v):
    return (v, None)

def back_low(kept, grad):
    return (low(grad),)
low.defvjp(low_keep, low_pass)
low_back.defvjp(back_keep, back_low)

def hdot(left, right):
    return jnp.dot(left, right, precision=lax.Precision.HIGHEST, preferred_element_type=jnp.float32)

def layer_norm(resid, norm_gain, norm_bias):
    center = resid - lax.optimization_barrier(jnp.mean(resid, axis=-1, keepdims=True))
    inv_std = lax.rsqrt(lax.optimization_barrier(jnp.mean(center * center, axis=-1, keepdims=True)) + norm_eps)
    return center * inv_std * norm_gain + norm_bias

def segments(offsets, places):
    return lax.optimization_barrier(jnp.sum((offsets[None, :] <= places[:, None]).astype(jnp.int32), axis=1)) - 1

def head_major(block):
    return jnp.transpose(block.reshape(LEN, HEADS, HEAD_DIM), (1, 0, 2))

def attend(queries, keys, values, offsets, flags):
    places = jnp.arange(LEN, dtype=jnp.int32)
    seg_all = segments(offsets, places)
    block = math.gcd(LEN, 512)
    block_count = LEN // block

    def one_head(head_args):
        query_head, key_head, value_head = head_args

        def one_block(block_args):
            query_block, seg_block, place_block = block_args
            scores = low_back(hdot(query_block, key_head.T))
            allowed = (seg_block[:, None] == seg_all[None, :]) & ((flags[None, :] > 0) | (place_block[:, None] == places[None, :]))
            scores = jnp.where(allowed, scores, neg_large)
            probs = jax.nn.softmax(scores, axis=-1)
            return hdot(low(probs), value_head)
        pieces = lax.map(jax.checkpoint(one_block), (query_head.reshape(block_count, block, HEAD_DIM), seg_all.reshape(block_count, block), places.reshape(block_count, block)))
        return pieces.reshape(LEN, HEAD_DIM)
    result = lax.map(jax.checkpoint(one_head), (head_major(queries), head_major(keys), head_major(values)))
    return jnp.transpose(result, (1, 0, 2)).reshape(LEN, D)

def reference(tokens, cotangent, doc_offsets, valid_flags, w_query, w_key, w_value, w_out, w_fc1, w_fc2, b_query, b_value, b_out, b_fc1, b_fc2, gain_attn, bias_attn, gain_ffn, bias_ffn):
    params = tuple((item.astype(jnp.float32) for item in (w_query, w_key, w_value, w_out, w_fc1, w_fc2, b_query, b_value, b_out, b_fc1, b_fc2, gain_attn, bias_attn, gain_ffn, bias_ffn)))
    inputs = tokens.astype(jnp.float32).reshape(SEQS * LEN, D)

    def forward(resid_in, *weights):
        mat_query, mat_key, mat_value, mat_out, mat_up, mat_down = weights[:6]
        vec_query, vec_value, vec_out, vec_up, vec_down, gain_one, bias_one, gain_two, bias_two = weights[6:]
        query_all = low(low_back((hdot(resid_in, mat_query) + vec_query) * HEAD_DIM ** (-0.5)))
        key_all = low(low_back(hdot(resid_in, mat_key)))
        value_all = low(low_back(hdot(resid_in, mat_value) + vec_value))
        pieces = []
        for which in range(SEQS):
            lower = which * LEN
            pieces.append(attend(query_all[lower:lower + LEN], key_all[lower:lower + LEN], value_all[lower:lower + LEN], doc_offsets[which], valid_flags[which]))
        attn_low = low(low_back(jnp.concatenate(pieces, axis=0)))
        branch = low_back(hdot(attn_low, mat_out) + vec_out)
        normed_one = layer_norm(resid_in + branch, gain_one, bias_one)
        hidden = low_back(hdot(low(normed_one), mat_up) + vec_up)
        act_low = low(jax.nn.gelu(hidden, approximate=False))
        ffn = low_back(hdot(act_low, mat_down) + vec_down)
        normed_two = layer_norm(normed_one + ffn, gain_two, bias_two)
        return (normed_two, (branch, normed_one, ffn))
    result, pullback, extras = jax.vjp(forward, inputs, *params, has_aux=True)
    grads = pullback(cotangent.astype(jnp.float32).reshape(SEQS * LEN, D))
    flags = valid_flags.reshape(SEQS * LEN).astype(jnp.float32)
    real_count = jnp.maximum(jnp.sum(flags), 1.0)
    sums = jnp.stack([jnp.sum(flags * lax.optimization_barrier(jnp.sum(item * item, axis=1))) for item in (inputs,) + tuple(extras)])
    rms = jnp.sqrt(sums / (real_count * D))
    return (result.reshape(SEQS, LEN, D).astype(jnp.bfloat16), grads[0].reshape(SEQS, LEN, D), grads[1], grads[2], grads[3], grads[4], grads[5], grads[6], grads[7], grads[8], grads[9], grads[10], grads[11], grads[12], grads[13], grads[14], grads[15], rms)
```

```python
import functools

import jax
import jax.numpy as jnp
from jax import lax
from jax.experimental import pallas as pl
from jax.experimental.pallas import tpu as pltpu
from jax.sharding import PartitionSpec as P

HEAD_DIM = 64
NORM_EPS = 1e-05
NEG_LARGE = -1e30
QUERY_ROWS = 256
BF16 = jnp.bfloat16
F32 = jnp.float32
ALL = ("blk", "heads")


def vmem_limit(length):
    return 8 * 1024 * 1024 + 6 * 1024 * length


def matmul(left, right):
    return jnp.dot(left, right, preferred_element_type=F32)


def matmul_tn(left, right):
    return lax.dot_general(left, right, (((0,), (0,)), ((), ())), preferred_element_type=F32)


def matmul_nt(left, right):
    return lax.dot_general(left, right, (((1,), (1,)), ((), ())), preferred_element_type=F32)


def swapped(block, axis, mask):
    count = lax.axis_size(axis)
    return lax.ppermute(block, axis, [(i, i ^ mask) for i in range(count)])


def gather_parts(block, axis):
    index = lax.axis_index(axis)
    every = lax.all_gather(block, axis, axis=0, tiled=False)
    return [
        lax.dynamic_index_in_dim(every, index ^ k, 0, False) for k in range(lax.axis_size(axis))
    ]


def scatter_parts(parts, axis):
    stacked = xor_order(jnp.stack(parts), 0, lax.axis_index(axis))
    return lax.psum_scatter(stacked, axis, scatter_dimension=0, tiled=False)


def xor_order(array, dim, index):
    pieces = [
        lax.dynamic_index_in_dim(array, index ^ k, dim, True) for k in range(array.shape[dim])
    ]
    return jnp.concatenate(pieces, axis=dim)


def gather_blk(block):
    return lax.all_gather(block, "blk", axis=0, tiled=False)


def scatter_blk(blocks):
    return lax.psum_scatter(blocks.astype(F32), "blk", scatter_dimension=0, tiled=False)


def layer_norm(resid, norm_gain, norm_bias):
    center = resid - jnp.mean(resid, axis=-1, keepdims=True)
    inv_std = lax.rsqrt(jnp.mean(center * center, axis=-1, keepdims=True) + NORM_EPS)
    normed = center * inv_std
    return (normed * norm_gain + norm_bias, normed, inv_std)


def norm_back(upstream, normed, inv_std, norm_gain):
    scaled = upstream * norm_gain
    return inv_std * (
        scaled
        - jnp.mean(scaled, axis=-1, keepdims=True)
        - normed * jnp.mean(scaled * normed, axis=-1, keepdims=True)
    )


def gelu_slope(hidden):
    cdf_part = 0.5 * (1.0 + lax.erf(hidden * 0.7071067811865476))
    pdf_part = jnp.exp(-0.5 * hidden * hidden) * 0.3989422804014327
    return cdf_part + hidden * pdf_part


def two_halves(values):
    high = lax.reduce_precision(values, 8, 7)
    return jnp.stack([high, values - high], axis=-1).astype(BF16)


def left_lanes(block):
    lane = lax.broadcasted_iota(jnp.int32, block.shape, 1)
    return jnp.where(lane < HEAD_DIM, block, 0.0)


def masked_scores(seg_key, seg_query, scores):
    width = scores.shape[1] // seg_key.shape[1]
    same = jnp.concatenate([seg_key] * width, axis=1) == seg_query
    return jnp.where(same, scores, NEG_LARGE)


def own_scores(seg_key, seg_query, scores):
    width = scores.shape[1] // seg_key.shape[1]
    same = jnp.concatenate([seg_key] * width, axis=1) == seg_query
    rows = lax.broadcasted_iota(jnp.int32, scores.shape, 0)
    columns = lax.broadcasted_iota(jnp.int32, scores.shape, 1)
    return jnp.where(same | (rows == columns), scores, NEG_LARGE)


def score_all(turn, seg_query, seg_key_ref, qkv_ref, query_t, scores):
    sources, rows = qkv_ref.shape[0], qkv_ref.shape[1] * 2 // 3
    per_source = rows // QUERY_ROWS
    query_now = query_t[turn]
    for b in range(sources):
        spot = slice(b * rows, (b + 1) * rows)
        scores[spot, :] = masked_scores(
            seg_key_ref[spot, :], seg_query, matmul(qkv_ref[b, 0:rows, :], query_now)
        )
    own = pl.ds(pl.multiple_of(turn * QUERY_ROWS, QUERY_ROWS), QUERY_ROWS)
    inner = pl.ds(pl.multiple_of(turn % per_source * QUERY_ROWS, QUERY_ROWS), QUERY_ROWS)
    own_pair = qkv_ref[turn // per_source, inner, :]
    scores[own, :] = own_scores(seg_key_ref[own, :], seg_query, matmul(own_pair, query_now))
    return own, own_pair


def turn_queries(b, turned, query_t):
    per_source = turned.shape[1] // QUERY_ROWS
    low = jnp.concatenate([jnp.zeros_like(turned[0:HEAD_DIM]), turned[0:HEAD_DIM]], axis=0)
    for t in range(per_source):
        spot = slice(t * QUERY_ROWS, (t + 1) * QUERY_ROWS)
        query_t[b * per_source + t] = low[:, spot].astype(BF16)


def attend_kernel(
    part_ref, seg_row_ref, seg_key_ref, qkv_ref, low_ref, attn_ref, lse_ref,
    query_t, values_t, scores,
):
    step = pl.program_id(0)
    sources, rows = qkv_ref.shape[0], qkv_ref.shape[1] * 2 // 3
    half = rows // 2

    @pl.when(step == 0)
    def _():
        for b in range(sources):
            turn_queries(b, qkv_ref[b, 0:rows, :].astype(F32).T, query_t)
            turned = qkv_ref[b, rows : rows + half, :].astype(F32).T
            values_t[:, b * rows : b * rows + half] = turned[0:HEAD_DIM].astype(BF16)
            values_t[:, b * rows + half : (b + 1) * rows] = turned[
                HEAD_DIM : 2 * HEAD_DIM
            ].astype(BF16)

    turn = part_ref[0] + step
    score_all(turn, seg_row_ref[0], seg_key_ref, qkv_ref, query_t, scores)
    top = jnp.max(scores[...], axis=0, keepdims=True)
    total = jnp.zeros_like(top)
    result = jnp.zeros((HEAD_DIM, QUERY_ROWS), F32)
    for b in range(sources):
        spot = slice(b * rows, (b + 1) * rows)
        probs = jnp.exp(scores[spot, :] - top)
        total = total + jnp.sum(probs, axis=0, keepdims=True)
        result = result + matmul(values_t[:, spot], probs.astype(BF16))
    result = result / total
    attn_ref[...] = result
    lse_ref[0] = top + jnp.log(total)
    turned = result.T
    wide = low_ref.shape[1]
    for t in range(low_ref.shape[0]):
        left = turned[2 * t * wide : (2 * t + 1) * wide]
        right = turned[(2 * t + 1) * wide : (2 * t + 2) * wide]
        low_ref[t] = jnp.concatenate([left, right], axis=1).astype(BF16)


def attend(part, seg_row, seg_key, qkv, wide, query_length):
    sources, rows = qkv.shape[0], qkv.shape[1] * 2 // 3
    length = sources * rows
    steps = query_length // QUERY_ROWS
    blocks = QUERY_ROWS // (2 * wide)
    return pl.pallas_call(
        attend_kernel,
        grid_spec=pltpu.PrefetchScalarGridSpec(
            num_scalar_prefetch=1,
            grid=(steps,),
            in_specs=[
                pl.BlockSpec((1, 1, QUERY_ROWS), lambda i, part: (part[0] + i, 0, 0)),
                pl.BlockSpec(seg_key.shape, lambda i, part: (0, 0)),
                pl.BlockSpec(qkv.shape, lambda i, part: (0, 0, 0)),
            ],
            out_specs=[
                pl.BlockSpec((blocks, wide, 128), lambda i, part: (i, 0, 0)),
                pl.BlockSpec((HEAD_DIM, QUERY_ROWS), lambda i, part: (0, i)),
                pl.BlockSpec((1, 1, QUERY_ROWS), lambda i, part: (i, 0, 0)),
            ],
            scratch_shapes=[
                pltpu.VMEM((length // QUERY_ROWS, 128, QUERY_ROWS), BF16),
                pltpu.VMEM((HEAD_DIM, length), BF16),
                pltpu.VMEM((length, QUERY_ROWS), F32),
            ],
        ),
        out_shape=[
            jax.ShapeDtypeStruct((steps * blocks, wide, 128), BF16),
            jax.ShapeDtypeStruct((HEAD_DIM, query_length), F32),
            jax.ShapeDtypeStruct((steps, 1, QUERY_ROWS), F32),
        ],
        compiler_params=pltpu.CompilerParams(vmem_limit_bytes=vmem_limit(length)),
    )(part, seg_row, seg_key, qkv)


def attend_back_kernel(
    part_ref, seg_row_ref, seg_key_ref, qkv_ref, up_ref, attn_ref, lse_ref, grads_ref,
    query_t, keys_t, values, scores, grad_query, grad_key, grad_value,
):
    step = pl.program_id(0)
    sources, rows = qkv_ref.shape[0], qkv_ref.shape[1] * 2 // 3
    half = rows // 2
    lane = lax.broadcasted_iota(jnp.int32, (rows, 128), 1)

    @pl.when(step == 0)
    def _():
        for b in range(sources):
            turned = qkv_ref[b, 0:rows, :].astype(F32).T
            turn_queries(b, turned, query_t)
            keys_t[:, b * rows : (b + 1) * rows] = turned[HEAD_DIM : 2 * HEAD_DIM].astype(BF16)
            packed = qkv_ref[b, rows : rows + half, :].astype(F32)
            values[b * rows : b * rows + half, :] = left_lanes(packed).astype(BF16)
            values[b * rows + half : (b + 1) * rows, :] = left_lanes(
                pltpu.roll(packed, HEAD_DIM, 1)
            ).astype(BF16)
        grad_query[...] = jnp.zeros_like(grad_query)
        grad_key[...] = jnp.zeros_like(grad_key)
        grad_value[...] = jnp.zeros_like(grad_value)

    turn = part_ref[0] + step
    lse = lse_ref[0]
    pieces = []
    for t in range(up_ref.shape[0]):
        packed = up_ref[t].astype(F32)
        pieces.append(left_lanes(packed))
        pieces.append(left_lanes(pltpu.roll(packed, HEAD_DIM, 1)))
    up_now = jnp.concatenate(pieces, axis=0)
    up_turned = up_now.T
    delta = jnp.sum(up_turned[0:HEAD_DIM] * attn_ref[...], axis=0, keepdims=True)
    up_now = up_now.astype(BF16)
    up_turned = up_turned.astype(BF16)
    own, own_pair = score_all(turn, seg_row_ref[0], seg_key_ref, qkv_ref, query_t, scores)
    query_now = pltpu.roll(own_pair.astype(F32), HEAD_DIM, 1).astype(BF16)
    result = jnp.zeros((HEAD_DIM, QUERY_ROWS), F32)
    for b in range(sources):
        spot = slice(b * rows, (b + 1) * rows)
        probs = jnp.exp(scores[spot, :] - lse)
        grad_probs = matmul(values[spot, :], up_turned)
        grad_scores = (probs * (grad_probs - delta)).astype(BF16)
        grad_value[spot, :] += matmul(probs.astype(BF16), up_now)
        grad_key[spot, :] += matmul(grad_scores, query_now)
        result = result + matmul(keys_t[:, spot], grad_scores)
    grad_query[own, :] = jnp.concatenate([result, jnp.zeros_like(result)], axis=0).T

    @pl.when(step == pl.num_programs(0) - 1)
    def _():
        for b in range(sources):
            spot = slice(b * rows, (b + 1) * rows)
            grads_ref[b, 0:rows, :] = jnp.where(
                lane < HEAD_DIM, grad_query[spot, :], grad_key[spot, :]
            ).astype(BF16)
            upper = grad_value[b * rows : b * rows + half, :]
            lower = grad_value[b * rows + half : (b + 1) * rows, :]
            grads_ref[b, rows : rows + half, :] = (
                upper + pltpu.roll(lower, HEAD_DIM, 1)
            ).astype(BF16)


def attend_back(part, seg_row, seg_key, qkv, upstream, attn_t, lse):
    sources, rows = qkv.shape[0], qkv.shape[1] * 2 // 3
    length = sources * rows
    steps = lse.shape[0]
    wide = upstream.shape[1]
    blocks = QUERY_ROWS // (2 * wide)
    return pl.pallas_call(
        attend_back_kernel,
        grid_spec=pltpu.PrefetchScalarGridSpec(
            num_scalar_prefetch=1,
            grid=(steps,),
            in_specs=[
                pl.BlockSpec((1, 1, QUERY_ROWS), lambda i, part: (part[0] + i, 0, 0)),
                pl.BlockSpec(seg_key.shape, lambda i, part: (0, 0)),
                pl.BlockSpec(qkv.shape, lambda i, part: (0, 0, 0)),
                pl.BlockSpec((blocks, wide, 128), lambda i, part: (part[0] + i, 0, 0)),
                pl.BlockSpec((HEAD_DIM, QUERY_ROWS), lambda i, part: (0, i)),
                pl.BlockSpec((1, 1, QUERY_ROWS), lambda i, part: (i, 0, 0)),
            ],
            out_specs=pl.BlockSpec(qkv.shape, lambda i, part: (0, 0, 0)),
            scratch_shapes=[
                pltpu.VMEM((length // QUERY_ROWS, 128, QUERY_ROWS), BF16),
                pltpu.VMEM((HEAD_DIM, length), BF16),
                pltpu.VMEM((length, 128), BF16),
                pltpu.VMEM((length, QUERY_ROWS), F32),
                pltpu.VMEM((length, 128), F32),
                pltpu.VMEM((length, 128), F32),
                pltpu.VMEM((length, 128), F32),
            ],
        ),
        out_shape=jax.ShapeDtypeStruct(qkv.shape, BF16),
        compiler_params=pltpu.CompilerParams(vmem_limit_bytes=vmem_limit(length)),
    )(part, seg_row, seg_key, qkv, upstream, attn_t, lse)


def per_device(
    tokens,
    cotangent,
    doc_offsets,
    valid_flags,
    w_query,
    w_key,
    w_value,
    w_out,
    w_fc1,
    w_fc2,
    b_query,
    b_value,
    b_out,
    b_fc1,
    b_fc2,
    gain_attn,
    bias_attn,
    gain_ffn,
    bias_ffn,
):
    seqs, span, width = tokens.shape
    groups = lax.axis_size("heads")
    blocks = lax.axis_size("blk")
    devices = groups * blocks
    my_group = lax.axis_index("heads")
    my_block = lax.axis_index("blk")
    rows = seqs * span
    block_rows = span * groups
    length = block_rows * blocks
    heads = width // HEAD_DIM
    heads_here = heads // groups
    pairs = seqs * heads_here
    repeats = blocks // pairs
    parts_length = length // repeats
    width_here = heads_here * HEAD_DIM
    dim_rows = w_query.shape[0]
    unit_rows = w_fc2.shape[0]
    hidden_size = w_fc1.shape[1]
    units_here = hidden_size // groups
    qk_scale = HEAD_DIM ** (-0.5)
    half = block_rows // 2
    wide = span // 2

    w_three = jnp.concatenate(
        [w.reshape(dim_rows, groups, width_here) for w in (w_query, w_key, w_value)], axis=-1
    )
    w_three = jnp.transpose(w_three, (1, 0, 2))
    vectors = jnp.stack(
        [b_query, b_value, b_out, b_fc2, gain_attn, bias_attn, gain_ffn, bias_ffn], axis=1
    )
    vectors = jnp.concatenate([vectors, b_fc1.reshape(dim_rows, unit_rows // dim_rows)], axis=1)
    vector_count = vectors.shape[1]
    vectors = jnp.pad(vectors, ((0, 0), (0, 128 - vector_count)))
    first = jnp.concatenate(
        [w_three, jnp.broadcast_to(vectors[None], (groups,) + vectors.shape)], axis=-1
    )
    first = lax.all_to_all(first, "heads", split_axis=0, concat_axis=0, tiled=True)
    first = gather_blk(first.reshape(groups * dim_rows, first.shape[-1]))
    first = first.reshape(width, first.shape[-1])
    mat_three = first[:, : 3 * width_here]
    vectors = first[:, 3 * width_here : 3 * width_here + vector_count]
    (vec_query, vec_value, vec_out, vec_down, gain_one, bias_one, gain_two, bias_two) = [
        vectors[:, i].astype(F32) for i in range(8)
    ]
    vec_up = vectors[:, 8:].reshape(blocks, groups, unit_rows)
    vec_up = lax.dynamic_index_in_dim(vec_up, my_group, 1, False).reshape(units_here).astype(F32)
    w_up = w_fc1.reshape(dim_rows, blocks, groups, unit_rows)
    w_up = jnp.transpose(w_up, (2, 0, 1, 3)).reshape(groups, dim_rows, units_here)
    second = jnp.concatenate(
        [w_up, jnp.broadcast_to(w_out[None], (groups,) + w_out.shape)], axis=-1
    )
    second = lax.all_to_all(second, "heads", split_axis=0, concat_axis=0, tiled=True)
    second = lax.all_gather(
        second.reshape(groups * dim_rows, second.shape[-1]), "blk", axis=0, tiled=True
    )
    mat_up = second[:, :units_here]
    mat_out = second[:, units_here:]
    mat_down = lax.all_gather(w_fc2, "blk", axis=0, tiled=True)

    token_rows = tokens.reshape(rows, width)
    token_parts = gather_parts(token_rows, "heads")
    token_all = jnp.stack([part.reshape(tokens.shape) for part in token_parts], axis=1)
    token_all = token_all.reshape(seqs * block_rows, width)
    projected = matmul(token_all, mat_three)
    group_query = lax.dynamic_slice_in_dim(vec_query, my_group * width_here, width_here)
    group_value = lax.dynamic_slice_in_dim(vec_value, my_group * width_here, width_here)
    head_shape = (seqs, block_rows, heads_here, HEAD_DIM)
    query_tok = ((projected[:, :width_here] + group_query) * qk_scale).astype(BF16)
    key_tok = projected[:, width_here : 2 * width_here].astype(BF16)
    pair_tok = jnp.concatenate([query_tok.reshape(head_shape), key_tok.reshape(head_shape)], axis=3)
    pair_tok = jnp.transpose(pair_tok, (0, 2, 1, 3))
    value_tok = (projected[:, 2 * width_here :] + group_value).astype(BF16)
    value_tok = value_tok.reshape(seqs, 2, half, heads_here, HEAD_DIM)
    value_tok = jnp.transpose(value_tok, (0, 3, 2, 1, 4))
    value_tok = value_tok.reshape(seqs, heads_here, half, 2 * HEAD_DIM)
    sent = jnp.concatenate([pair_tok, value_tok], axis=2)
    sent = sent.reshape(pairs, 1, block_rows + half, 2 * HEAD_DIM)
    sent = jnp.broadcast_to(sent, (pairs, repeats) + sent.shape[2:])
    sent = sent.reshape(blocks, block_rows + half, 2 * HEAD_DIM)
    qkv = lax.all_to_all(sent, "blk", split_axis=0, concat_axis=0, tiled=True)

    my_pair = my_block // repeats
    my_part = my_block % repeats
    my_seq = my_pair // heads_here
    inner = jnp.arange(length, dtype=jnp.int32)
    place = (inner // block_rows) * block_rows + inner % span
    place = place + (((inner // span) % groups) ^ my_group) * span
    offsets = lax.dynamic_index_in_dim(doc_offsets, my_seq, 0, False)
    flags = lax.dynamic_index_in_dim(valid_flags, my_seq, 0, False)
    flags = xor_order(flags.reshape(blocks, groups, span), 1, my_group).reshape(length)
    segment = jnp.sum((offsets[None, :] <= place[:, None]).astype(jnp.int32), axis=1) - 1
    seg_row = segment.reshape(length // QUERY_ROWS, 1, QUERY_ROWS)
    seg_key = jnp.where(flags > 0, segment, -1)
    seg_key = jnp.broadcast_to(seg_key[:, None], (length, 128))
    first_turn = (my_part * (parts_length // QUERY_ROWS)).reshape(1).astype(jnp.int32)
    attn_low, attn_t, lse = attend(first_turn, seg_row, seg_key, qkv, wide, parts_length)

    part_blocks = blocks // repeats
    sent = attn_low.reshape(part_blocks, groups, wide, 2 * HEAD_DIM)
    sent = xor_order(sent, 1, my_group)
    sent = jnp.broadcast_to(sent[None], (repeats,) + sent.shape)
    sent = sent.reshape(devices, wide, 2 * HEAD_DIM)
    got = lax.all_to_all(sent, ALL, split_axis=0, concat_axis=0, tiled=True)
    got = got.reshape(seqs, heads_here, repeats, groups, wide, 2, HEAD_DIM)
    got = lax.dynamic_index_in_dim(got, my_block // part_blocks, 2, False)
    attn_tok = jnp.transpose(got, (0, 4, 3, 2, 1, 5)).reshape(rows, width)

    resid_in = token_rows.astype(F32)
    branch = matmul(attn_tok, mat_out) + vec_out
    normed_one, unit_one, inv_one = layer_norm(resid_in + branch, gain_one, bias_one)
    normed_low = normed_one.astype(BF16)
    normed_all = jnp.concatenate(gather_parts(normed_low, "heads"), axis=0)
    hidden = matmul(normed_all, mat_up) + vec_up
    act_low = jax.nn.gelu(hidden, approximate=False).astype(BF16)
    ffn_all = matmul(act_low, mat_down)
    ffn = scatter_parts(jnp.split(ffn_all, groups), "heads") + vec_down
    normed_two, unit_two, inv_two = layer_norm(normed_one + ffn, gain_two, bias_two)
    output = normed_two.astype(BF16).reshape(tokens.shape)
    my_span = my_block * groups + my_group
    local_flags = lax.dynamic_slice_in_dim(valid_flags, my_span * span, span, 1)
    local_flags = local_flags.reshape(rows).astype(F32)
    squares = jnp.stack(
        [
            jnp.sum(local_flags * jnp.sum(item * item, axis=1))
            for item in (resid_in, branch, normed_one, ffn)
        ]
    )

    upstream = cotangent.reshape(rows, width).astype(F32)
    grad_gain_two = jnp.sum(upstream * unit_two, axis=0)
    grad_bias_two = jnp.sum(upstream, axis=0)
    grad_resid_two = norm_back(upstream, unit_two, inv_two, gain_two)
    grad_ffn = grad_resid_two.astype(BF16)
    grad_vec_down = jnp.sum(grad_ffn.astype(F32), axis=0)
    grad_ffn_all = jnp.concatenate(gather_parts(grad_ffn, "heads"), axis=0)
    grad_hidden = (matmul_nt(grad_ffn_all, mat_down) * gelu_slope(hidden)).astype(BF16)
    grad_vec_up = jnp.sum(grad_hidden.astype(F32), axis=0)
    grad_normed_all = matmul_nt(grad_hidden, mat_up)
    grad_normed_one = grad_resid_two + scatter_parts(jnp.split(grad_normed_all, groups), "heads")
    grad_mat_down = matmul_tn(act_low, grad_ffn_all).astype(BF16)
    grad_mat_up = matmul_tn(normed_all, grad_hidden).astype(BF16)
    ffn_grads = jnp.concatenate(
        [
            grad_mat_down.reshape(blocks, unit_rows, width),
            grad_mat_up.reshape(blocks, -1, width),
        ],
        axis=1,
    )
    ffn_grads = lax.psum_scatter(
        ffn_grads.reshape(-1, width), "blk", scatter_dimension=0, tiled=True
    )
    shard_down = ffn_grads[:unit_rows].astype(F32)
    shard_up = lax.all_to_all(
        ffn_grads[unit_rows:].reshape(groups, dim_rows, units_here),
        "heads",
        split_axis=0,
        concat_axis=0,
        tiled=True,
    )
    shard_up = jnp.transpose(
        shard_up.reshape(groups, dim_rows, blocks, unit_rows), (1, 2, 0, 3)
    ).reshape(dim_rows, hidden_size)
    shard_up = shard_up.astype(F32)

    grad_gain_one = jnp.sum(grad_normed_one * unit_one, axis=0)
    grad_bias_one = jnp.sum(grad_normed_one, axis=0)
    grad_resid_one = norm_back(grad_normed_one, unit_one, inv_one, gain_one)
    grad_branch = grad_resid_one.astype(BF16)
    grad_vec_out = jnp.sum(grad_branch.astype(F32), axis=0)
    grad_attn = matmul_nt(grad_branch, mat_out).astype(BF16)

    sent = grad_attn.reshape(seqs, 2, wide, groups, heads_here, HEAD_DIM)
    sent = jnp.transpose(sent, (0, 4, 3, 2, 1, 5))
    sent = sent.reshape(pairs, 1, groups, wide, 2 * HEAD_DIM)
    sent = jnp.broadcast_to(sent, (pairs, repeats) + sent.shape[2:])
    sent = sent.reshape(devices, wide, 2 * HEAD_DIM)
    small = jnp.stack(
        [grad_vec_out, grad_vec_down, grad_gain_one, grad_bias_one, grad_gain_two, grad_bias_two]
    )
    small = jnp.transpose(small.reshape(6, devices, dim_rows), (1, 0, 2)).reshape(devices, -1)
    up_sums = jnp.zeros((blocks, groups, unit_rows), F32)
    up_sums = lax.dynamic_update_slice_in_dim(
        up_sums, grad_vec_up.reshape(blocks, 1, unit_rows), my_group, 1
    ).reshape(devices, unit_rows)
    small = jnp.concatenate(
        [small, up_sums, jnp.broadcast_to(squares[None], (devices, 4))], axis=1
    )
    small_count = small.shape[1]
    small = two_halves(small).reshape(devices, 2 * small_count)
    extra = 16 * (-(-2 * small_count // 2048))
    small = jnp.pad(small, ((0, 0), (0, extra * 128 - 2 * small_count)))
    sent = jnp.concatenate([sent, small.reshape(devices, extra, 128)], axis=1)
    got = lax.all_to_all(sent, ALL, split_axis=0, concat_axis=0, tiled=True)
    up_heads = got[:, :wide].reshape(blocks, groups, wide, 2 * HEAD_DIM)
    up_heads = xor_order(up_heads, 1, my_group).reshape(devices, wide, 2 * HEAD_DIM)
    small = jnp.sum(got[:, wide:].reshape(devices, extra * 128).astype(F32), axis=0)
    small = jnp.sum(small[: 2 * small_count].reshape(small_count, 2), axis=1)
    vector_sums = small[: 6 * dim_rows].reshape(6, dim_rows)
    shard_vec_up = small[6 * dim_rows : 6 * dim_rows + unit_rows]
    totals = small[6 * dim_rows + unit_rows :]
    real_count = jnp.maximum(jnp.sum(valid_flags.astype(F32)), 1.0)
    rms = jnp.sqrt(totals / (real_count * width))

    attn_columns = jnp.transpose(
        attn_tok.reshape(rows, blocks, groups, dim_rows), (2, 0, 1, 3)
    ).reshape(groups, rows, blocks * dim_rows)
    attn_columns = lax.all_to_all(
        attn_columns, "heads", split_axis=0, concat_axis=0, tiled=True
    )
    attn_columns = xor_order(attn_columns, 0, my_group)
    branch_parts = gather_parts(grad_branch, "heads")
    grad_mat_out = matmul_tn(
        attn_columns.reshape(groups * rows, blocks * dim_rows),
        jnp.concatenate(branch_parts, axis=0),
    ).astype(BF16)
    shard_out = scatter_blk(grad_mat_out.reshape(blocks, dim_rows, width))

    grads = attend_back(first_turn, seg_row, seg_key, qkv, up_heads, attn_t, lse)
    got = lax.all_to_all(grads, "blk", split_axis=0, concat_axis=0, tiled=True)
    got = got.reshape(pairs, repeats, block_rows + half, 2 * HEAD_DIM)
    got = jnp.sum(got.astype(F32), axis=1).astype(BF16) if repeats > 1 else got[:, 0]
    got = got.reshape(seqs, heads_here, block_rows + half, 2 * HEAD_DIM)
    grad_pair = got[:, :, :block_rows].reshape(seqs, heads_here, block_rows, 2, HEAD_DIM)
    grad_pair = jnp.transpose(grad_pair, (3, 0, 2, 1, 4))
    grad_pair = grad_pair.reshape(2, seqs * block_rows, width_here)
    grad_value = got[:, :, block_rows:].reshape(seqs, heads_here, half, 2, HEAD_DIM)
    grad_value = jnp.transpose(grad_value, (0, 3, 2, 1, 4)).reshape(seqs * block_rows, width_here)
    grad_query = grad_pair[0] * jnp.asarray(qk_scale, BF16)
    grad_three = jnp.concatenate([grad_query, grad_pair[1], grad_value], axis=1)
    grad_input = matmul_nt(grad_three, mat_three)
    grad_input = grad_input.reshape(seqs, groups, span, width)
    grad_input = scatter_parts([grad_input[:, k].reshape(rows, width) for k in range(groups)], "heads")
    grad_input = (grad_resid_one + grad_input).reshape(tokens.shape)
    grad_mat_three = matmul_tn(token_all, grad_three)
    sums = jnp.sum(grad_three.astype(F32), axis=0)
    query_sums = sums[:width_here]
    value_sums = sums[2 * width_here :]
    chunks = blocks // groups
    sums = jnp.concatenate(
        [
            query_sums.reshape(chunks, groups * dim_rows),
            value_sums.reshape(chunks, groups * dim_rows),
            jnp.zeros((chunks, 3 * width_here - 2 * groups * dim_rows), F32),
        ],
        axis=1,
    )
    sums = jnp.concatenate([sums] * groups, axis=0)
    is_owner = jnp.arange(blocks, dtype=jnp.int32) // chunks == my_group
    sums = jnp.where(is_owner[:, None], sums, 0.0)
    row = lax.broadcasted_iota(jnp.int32, (1, 16, 1), 1)
    sum_rows = jnp.where(row == 0, sums[:, None, :], 0.0)
    three_grads = jnp.concatenate(
        [grad_mat_three.reshape(blocks, groups * dim_rows, 3 * width_here), sum_rows], axis=1
    ).astype(BF16)
    three_grads = scatter_blk(three_grads)
    own_rows = three_grads[: groups * dim_rows].reshape(groups, dim_rows, 3 * width_here)
    own_sums = three_grads[groups * dim_rows, : 2 * groups * dim_rows]
    own_sums = jnp.transpose(own_sums.reshape(2, groups, dim_rows), (1, 0, 2))
    own_sums = jnp.concatenate(
        [
            own_sums.reshape(groups, 2 * dim_rows),
            jnp.zeros((groups, 3 * width_here - 2 * dim_rows), F32),
        ],
        axis=1,
    )
    own_sums = jnp.where(row == 0, own_sums[:, None, :], 0.0)
    own = jnp.concatenate([own_rows, own_sums], axis=1).astype(BF16)
    own = lax.all_to_all(own, "heads", split_axis=0, concat_axis=0, tiled=True).astype(F32)
    shard_sums = jnp.sum(own[:, dim_rows, : 2 * dim_rows], axis=0)
    shards_three = [
        jnp.transpose(
            own[:, :dim_rows, which * width_here : (which + 1) * width_here], (1, 0, 2)
        ).reshape(dim_rows, width)
        for which in range(3)
    ]

    return (
        output,
        grad_input,
        shards_three[0],
        shards_three[1],
        shards_three[2],
        shard_out,
        shard_up,
        shard_down,
        shard_sums[:dim_rows],
        shard_sums[dim_rows:],
        vector_sums[0],
        shard_vec_up,
        vector_sums[1],
        vector_sums[2],
        vector_sums[3],
        vector_sums[4],
        vector_sums[5],
        rms,
    )


def solution(mesh):
    token_spec = P(None, ALL, None)
    matrix_spec = P(ALL, None)
    vector_spec = P(ALL)
    return jax.shard_map(
        per_device,
        mesh=mesh,
        in_specs=(token_spec,) * 2 + (P(),) * 2 + (matrix_spec,) * 6 + (vector_spec,) * 9,
        out_specs=(token_spec,) * 2 + (matrix_spec,) * 6 + (vector_spec,) * 9 + (P(),),
        check_vma=False,
    )
```

```python
import functools

import jax
import jax.numpy as jnp
from jax import lax
from jax.experimental import pallas as pl
from jax.experimental.pallas import tpu as pltpu
from jax.sharding import PartitionSpec as P

HEAD_DIM = 64
NORM_EPS = 1e-05
NEG_LARGE = -1e30
QUERY_ROWS = 256
BF16 = jnp.bfloat16
F32 = jnp.float32
ALL = ("blk", "heads")


def vmem_limit(length):
    return 8 * 1024 * 1024 + 6 * 1024 * length


def matmul(left, right):
    return jnp.dot(left, right, preferred_element_type=F32)


def matmul_tn(left, right):
    return lax.dot_general(left, right, (((0,), (0,)), ((), ())), preferred_element_type=F32)


def matmul_nt(left, right):
    return lax.dot_general(left, right, (((1,), (1,)), ((), ())), preferred_element_type=F32)


def swapped(block, axis, mask):
    count = lax.axis_size(axis)
    return lax.ppermute(block, axis, [(i, i ^ mask) for i in range(count)])


def gather_parts(block, axis):
    return [block] + [swapped(block, axis, k) for k in range(1, lax.axis_size(axis))]


def scatter_parts(parts, axis):
    total = parts[0].astype(F32)
    for k in range(1, len(parts)):
        total = total + swapped(parts[k].astype(BF16), axis, k).astype(F32)
    return total


def xor_order(array, dim, index):
    pieces = [
        lax.dynamic_index_in_dim(array, index ^ k, dim, True) for k in range(array.shape[dim])
    ]
    return jnp.concatenate(pieces, axis=dim)


def gather_blk(block):
    count = lax.axis_size("blk")
    index = lax.axis_index("blk")
    parts = [block] + [swapped(block, "blk", k) for k in range(2, count, 2)]
    mine = jnp.stack(parts)
    other = swapped(mine, "blk", 1)
    both = jnp.stack([mine, other], axis=1).reshape((count,) + block.shape)
    return xor_order(both, 0, index)


def scatter_blk(blocks):
    index = lax.axis_index("blk")
    ordered = xor_order(blocks, 0, index)
    pairs = ordered.reshape((ordered.shape[0] // 2, 2) + ordered.shape[1:])
    total = pairs[:, 0].astype(F32) + swapped(pairs[:, 1], "blk", 1).astype(F32)
    low = total.astype(BF16)
    result = total[0]
    for k in range(1, low.shape[0]):
        result = result + swapped(low[k], "blk", 2 * k).astype(F32)
    return result


def layer_norm(resid, norm_gain, norm_bias):
    center = resid - jnp.mean(resid, axis=-1, keepdims=True)
    inv_std = lax.rsqrt(jnp.mean(center * center, axis=-1, keepdims=True) + NORM_EPS)
    normed = center * inv_std
    return (normed * norm_gain + norm_bias, normed, inv_std)


def norm_back(upstream, normed, inv_std, norm_gain):
    scaled = upstream * norm_gain
    return inv_std * (
        scaled
        - jnp.mean(scaled, axis=-1, keepdims=True)
        - normed * jnp.mean(scaled * normed, axis=-1, keepdims=True)
    )


def gelu_slope(hidden):
    cdf_part = 0.5 * (1.0 + lax.erf(hidden * 0.7071067811865476))
    pdf_part = jnp.exp(-0.5 * hidden * hidden) * 0.3989422804014327
    return cdf_part + hidden * pdf_part


def two_halves(values):
    high = lax.reduce_precision(values, 8, 7)
    return jnp.stack([high, values - high], axis=-1).astype(BF16)


def left_lanes(block):
    lane = lax.broadcasted_iota(jnp.int32, block.shape, 1)
    return jnp.where(lane < HEAD_DIM, block, 0.0)


def masked_scores(seg_key, seg_query, scores):
    width = scores.shape[1] // seg_key.shape[1]
    same = jnp.concatenate([seg_key] * width, axis=1) == seg_query
    return jnp.where(same, scores, NEG_LARGE)


def own_scores(seg_key, seg_query, scores):
    width = scores.shape[1] // seg_key.shape[1]
    same = jnp.concatenate([seg_key] * width, axis=1) == seg_query
    rows = lax.broadcasted_iota(jnp.int32, scores.shape, 0)
    columns = lax.broadcasted_iota(jnp.int32, scores.shape, 1)
    return jnp.where(same | (rows == columns), scores, NEG_LARGE)


def score_all(turn, seg_query, seg_key_ref, qkv_ref, query_t, scores):
    sources, rows = qkv_ref.shape[0], qkv_ref.shape[1] * 2 // 3
    per_source = rows // QUERY_ROWS
    query_now = query_t[turn]
    for b in range(sources):
        spot = slice(b * rows, (b + 1) * rows)
        scores[spot, :] = masked_scores(
            seg_key_ref[spot, :], seg_query, matmul(qkv_ref[b, 0:rows, :], query_now)
        )
    own = pl.ds(pl.multiple_of(turn * QUERY_ROWS, QUERY_ROWS), QUERY_ROWS)
    inner = pl.ds(pl.multiple_of(turn % per_source * QUERY_ROWS, QUERY_ROWS), QUERY_ROWS)
    own_pair = qkv_ref[turn // per_source, inner, :]
    scores[own, :] = own_scores(seg_key_ref[own, :], seg_query, matmul(own_pair, query_now))
    return own, own_pair


def turn_queries(b, turned, query_t):
    per_source = turned.shape[1] // QUERY_ROWS
    low = jnp.concatenate([jnp.zeros_like(turned[0:HEAD_DIM]), turned[0:HEAD_DIM]], axis=0)
    for t in range(per_source):
        spot = slice(t * QUERY_ROWS, (t + 1) * QUERY_ROWS)
        query_t[b * per_source + t] = low[:, spot].astype(BF16)


def attend_kernel(
    part_ref, seg_row_ref, seg_key_ref, qkv_ref, low_ref, attn_ref, lse_ref,
    query_t, values_t, scores,
):
    step = pl.program_id(0)
    sources, rows = qkv_ref.shape[0], qkv_ref.shape[1] * 2 // 3
    half = rows // 2

    @pl.when(step == 0)
    def _():
        for b in range(sources):
            turn_queries(b, qkv_ref[b, 0:rows, :].astype(F32).T, query_t)
            turned = qkv_ref[b, rows : rows + half, :].astype(F32).T
            values_t[:, b * rows : b * rows + half] = turned[0:HEAD_DIM].astype(BF16)
            values_t[:, b * rows + half : (b + 1) * rows] = turned[
                HEAD_DIM : 2 * HEAD_DIM
            ].astype(BF16)

    turn = part_ref[0] + step
    score_all(turn, seg_row_ref[0], seg_key_ref, qkv_ref, query_t, scores)
    top = jnp.max(scores[...], axis=0, keepdims=True)
    total = jnp.zeros_like(top)
    result = jnp.zeros((HEAD_DIM, QUERY_ROWS), F32)
    for b in range(sources):
        spot = slice(b * rows, (b + 1) * rows)
        probs = jnp.exp(scores[spot, :] - top)
        total = total + jnp.sum(probs, axis=0, keepdims=True)
        result = result + matmul(values_t[:, spot], probs.astype(BF16))
    result = result / total
    attn_ref[...] = result
    lse_ref[0] = top + jnp.log(total)
    turned = result.T
    wide = low_ref.shape[1]
    for t in range(low_ref.shape[0]):
        left = turned[2 * t * wide : (2 * t + 1) * wide]
        right = turned[(2 * t + 1) * wide : (2 * t + 2) * wide]
        low_ref[t] = jnp.concatenate([left, right], axis=1).astype(BF16)


def attend(part, seg_row, seg_key, qkv, wide, query_length):
    sources, rows = qkv.shape[0], qkv.shape[1] * 2 // 3
    length = sources * rows
    steps = query_length // QUERY_ROWS
    blocks = QUERY_ROWS // (2 * wide)
    return pl.pallas_call(
        attend_kernel,
        grid_spec=pltpu.PrefetchScalarGridSpec(
            num_scalar_prefetch=1,
            grid=(steps,),
            in_specs=[
                pl.BlockSpec((1, 1, QUERY_ROWS), lambda i, part: (part[0] + i, 0, 0)),
                pl.BlockSpec(seg_key.shape, lambda i, part: (0, 0)),
                pl.BlockSpec(qkv.shape, lambda i, part: (0, 0, 0)),
            ],
            out_specs=[
                pl.BlockSpec((blocks, wide, 128), lambda i, part: (i, 0, 0)),
                pl.BlockSpec((HEAD_DIM, QUERY_ROWS), lambda i, part: (0, i)),
                pl.BlockSpec((1, 1, QUERY_ROWS), lambda i, part: (i, 0, 0)),
            ],
            scratch_shapes=[
                pltpu.VMEM((length // QUERY_ROWS, 128, QUERY_ROWS), BF16),
                pltpu.VMEM((HEAD_DIM, length), BF16),
                pltpu.VMEM((length, QUERY_ROWS), F32),
            ],
        ),
        out_shape=[
            jax.ShapeDtypeStruct((steps * blocks, wide, 128), BF16),
            jax.ShapeDtypeStruct((HEAD_DIM, query_length), F32),
            jax.ShapeDtypeStruct((steps, 1, QUERY_ROWS), F32),
        ],
        compiler_params=pltpu.CompilerParams(vmem_limit_bytes=vmem_limit(length)),
    )(part, seg_row, seg_key, qkv)


def attend_back_kernel(
    part_ref, seg_row_ref, seg_key_ref, qkv_ref, up_ref, attn_ref, lse_ref, grads_ref,
    query_t, keys_t, values, scores, grad_query, grad_key, grad_value,
):
    step = pl.program_id(0)
    sources, rows = qkv_ref.shape[0], qkv_ref.shape[1] * 2 // 3
    half = rows // 2
    lane = lax.broadcasted_iota(jnp.int32, (rows, 128), 1)

    @pl.when(step == 0)
    def _():
        for b in range(sources):
            turned = qkv_ref[b, 0:rows, :].astype(F32).T
            turn_queries(b, turned, query_t)
            keys_t[:, b * rows : (b + 1) * rows] = turned[HEAD_DIM : 2 * HEAD_DIM].astype(BF16)
            packed = qkv_ref[b, rows : rows + half, :].astype(F32)
            values[b * rows : b * rows + half, :] = left_lanes(packed).astype(BF16)
            values[b * rows + half : (b + 1) * rows, :] = left_lanes(
                pltpu.roll(packed, HEAD_DIM, 1)
            ).astype(BF16)
        grad_query[...] = jnp.zeros_like(grad_query)
        grad_key[...] = jnp.zeros_like(grad_key)
        grad_value[...] = jnp.zeros_like(grad_value)

    turn = part_ref[0] + step
    lse = lse_ref[0]
    pieces = []
    for t in range(up_ref.shape[0]):
        packed = up_ref[t].astype(F32)
        pieces.append(left_lanes(packed))
        pieces.append(left_lanes(pltpu.roll(packed, HEAD_DIM, 1)))
    up_now = jnp.concatenate(pieces, axis=0)
    up_turned = up_now.T
    delta = jnp.sum(up_turned[0:HEAD_DIM] * attn_ref[...], axis=0, keepdims=True)
    up_now = up_now.astype(BF16)
    up_turned = up_turned.astype(BF16)
    own, own_pair = score_all(turn, seg_row_ref[0], seg_key_ref, qkv_ref, query_t, scores)
    query_now = pltpu.roll(own_pair.astype(F32), HEAD_DIM, 1).astype(BF16)
    result = jnp.zeros((HEAD_DIM, QUERY_ROWS), F32)
    for b in range(sources):
        spot = slice(b * rows, (b + 1) * rows)
        probs = jnp.exp(scores[spot, :] - lse)
        grad_probs = matmul(values[spot, :], up_turned)
        grad_scores = (probs * (grad_probs - delta)).astype(BF16)
        grad_value[spot, :] += matmul(probs.astype(BF16), up_now)
        grad_key[spot, :] += matmul(grad_scores, query_now)
        result = result + matmul(keys_t[:, spot], grad_scores)
    grad_query[own, :] = jnp.concatenate([result, jnp.zeros_like(result)], axis=0).T

    @pl.when(step == pl.num_programs(0) - 1)
    def _():
        for b in range(sources):
            spot = slice(b * rows, (b + 1) * rows)
            grads_ref[b, 0:rows, :] = jnp.where(
                lane < HEAD_DIM, grad_query[spot, :], grad_key[spot, :]
            ).astype(BF16)
            upper = grad_value[b * rows : b * rows + half, :]
            lower = grad_value[b * rows + half : (b + 1) * rows, :]
            grads_ref[b, rows : rows + half, :] = (
                upper + pltpu.roll(lower, HEAD_DIM, 1)
            ).astype(BF16)


def attend_back(part, seg_row, seg_key, qkv, upstream, attn_t, lse):
    sources, rows = qkv.shape[0], qkv.shape[1] * 2 // 3
    length = sources * rows
    steps = lse.shape[0]
    wide = upstream.shape[1]
    blocks = QUERY_ROWS // (2 * wide)
    return pl.pallas_call(
        attend_back_kernel,
        grid_spec=pltpu.PrefetchScalarGridSpec(
            num_scalar_prefetch=1,
            grid=(steps,),
            in_specs=[
                pl.BlockSpec((1, 1, QUERY_ROWS), lambda i, part: (part[0] + i, 0, 0)),
                pl.BlockSpec(seg_key.shape, lambda i, part: (0, 0)),
                pl.BlockSpec(qkv.shape, lambda i, part: (0, 0, 0)),
                pl.BlockSpec((blocks, wide, 128), lambda i, part: (part[0] + i, 0, 0)),
                pl.BlockSpec((HEAD_DIM, QUERY_ROWS), lambda i, part: (0, i)),
                pl.BlockSpec((1, 1, QUERY_ROWS), lambda i, part: (i, 0, 0)),
            ],
            out_specs=pl.BlockSpec(qkv.shape, lambda i, part: (0, 0, 0)),
            scratch_shapes=[
                pltpu.VMEM((length // QUERY_ROWS, 128, QUERY_ROWS), BF16),
                pltpu.VMEM((HEAD_DIM, length), BF16),
                pltpu.VMEM((length, 128), BF16),
                pltpu.VMEM((length, QUERY_ROWS), F32),
                pltpu.VMEM((length, 128), F32),
                pltpu.VMEM((length, 128), F32),
                pltpu.VMEM((length, 128), F32),
            ],
        ),
        out_shape=jax.ShapeDtypeStruct(qkv.shape, BF16),
        compiler_params=pltpu.CompilerParams(vmem_limit_bytes=vmem_limit(length)),
    )(part, seg_row, seg_key, qkv, upstream, attn_t, lse)


def per_device(
    tokens,
    cotangent,
    doc_offsets,
    valid_flags,
    w_query,
    w_key,
    w_value,
    w_out,
    w_fc1,
    w_fc2,
    b_query,
    b_value,
    b_out,
    b_fc1,
    b_fc2,
    gain_attn,
    bias_attn,
    gain_ffn,
    bias_ffn,
):
    seqs, span, width = tokens.shape
    groups = lax.axis_size("heads")
    blocks = lax.axis_size("blk")
    devices = groups * blocks
    my_group = lax.axis_index("heads")
    my_block = lax.axis_index("blk")
    rows = seqs * span
    block_rows = span * groups
    length = block_rows * blocks
    heads = width // HEAD_DIM
    heads_here = heads // groups
    pairs = seqs * heads_here
    repeats = blocks // pairs
    parts_length = length // repeats
    width_here = heads_here * HEAD_DIM
    dim_rows = w_query.shape[0]
    unit_rows = w_fc2.shape[0]
    hidden_size = w_fc1.shape[1]
    units_here = hidden_size // groups
    qk_scale = HEAD_DIM ** (-0.5)
    half = block_rows // 2
    wide = span // 2

    w_three = jnp.concatenate(
        [w.reshape(dim_rows, groups, width_here) for w in (w_query, w_key, w_value)], axis=-1
    )
    w_three = jnp.transpose(w_three, (1, 0, 2))
    vectors = jnp.stack(
        [b_query, b_value, b_out, b_fc2, gain_attn, bias_attn, gain_ffn, bias_ffn], axis=1
    )
    vectors = jnp.concatenate([vectors, b_fc1.reshape(dim_rows, unit_rows // dim_rows)], axis=1)
    vector_count = vectors.shape[1]
    vectors = jnp.pad(vectors, ((0, 0), (0, 128 - vector_count)))
    first = jnp.concatenate(
        [w_three, jnp.broadcast_to(vectors[None], (groups,) + vectors.shape)], axis=-1
    )
    first = lax.all_to_all(first, "heads", split_axis=0, concat_axis=0, tiled=True)
    first = gather_blk(first.reshape(groups * dim_rows, first.shape[-1]))
    first = first.reshape(width, first.shape[-1])
    mat_three = first[:, : 3 * width_here]
    vectors = first[:, 3 * width_here : 3 * width_here + vector_count]
    (vec_query, vec_value, vec_out, vec_down, gain_one, bias_one, gain_two, bias_two) = [
        vectors[:, i].astype(F32) for i in range(8)
    ]
    vec_up = vectors[:, 8:].reshape(blocks, groups, unit_rows)
    vec_up = lax.dynamic_index_in_dim(vec_up, my_group, 1, False).reshape(units_here).astype(F32)
    w_up = w_fc1.reshape(dim_rows, blocks, groups, unit_rows)
    w_up = jnp.transpose(w_up, (2, 0, 1, 3)).reshape(groups, dim_rows, units_here)
    second = jnp.concatenate(
        [w_up, jnp.broadcast_to(w_out[None], (groups,) + w_out.shape)], axis=-1
    )
    second = lax.all_to_all(second, "heads", split_axis=0, concat_axis=0, tiled=True)
    second = lax.all_gather(
        second.reshape(groups * dim_rows, second.shape[-1]), "blk", axis=0, tiled=True
    )
    mat_up = second[:, :units_here]
    mat_out = second[:, units_here:]
    mat_down = lax.all_gather(w_fc2, "blk", axis=0, tiled=True)

    token_rows = tokens.reshape(rows, width)
    token_parts = gather_parts(token_rows, "heads")
    token_all = jnp.stack([part.reshape(tokens.shape) for part in token_parts], axis=1)
    token_all = token_all.reshape(seqs * block_rows, width)
    projected = matmul(token_all, mat_three)
    group_query = lax.dynamic_slice_in_dim(vec_query, my_group * width_here, width_here)
    group_value = lax.dynamic_slice_in_dim(vec_value, my_group * width_here, width_here)
    head_shape = (seqs, block_rows, heads_here, HEAD_DIM)
    query_tok = ((projected[:, :width_here] + group_query) * qk_scale).astype(BF16)
    key_tok = projected[:, width_here : 2 * width_here].astype(BF16)
    pair_tok = jnp.concatenate([query_tok.reshape(head_shape), key_tok.reshape(head_shape)], axis=3)
    pair_tok = jnp.transpose(pair_tok, (0, 2, 1, 3))
    value_tok = (projected[:, 2 * width_here :] + group_value).astype(BF16)
    value_tok = value_tok.reshape(seqs, 2, half, heads_here, HEAD_DIM)
    value_tok = jnp.transpose(value_tok, (0, 3, 2, 1, 4))
    value_tok = value_tok.reshape(seqs, heads_here, half, 2 * HEAD_DIM)
    sent = jnp.concatenate([pair_tok, value_tok], axis=2)
    sent = sent.reshape(pairs, 1, block_rows + half, 2 * HEAD_DIM)
    sent = jnp.broadcast_to(sent, (pairs, repeats) + sent.shape[2:])
    sent = sent.reshape(blocks, block_rows + half, 2 * HEAD_DIM)
    qkv = lax.all_to_all(sent, "blk", split_axis=0, concat_axis=0, tiled=True)

    my_pair = my_block // repeats
    my_part = my_block % repeats
    my_seq = my_pair // heads_here
    inner = jnp.arange(length, dtype=jnp.int32)
    place = (inner // block_rows) * block_rows + inner % span
    place = place + (((inner // span) % groups) ^ my_group) * span
    offsets = lax.dynamic_index_in_dim(doc_offsets, my_seq, 0, False)
    flags = lax.dynamic_index_in_dim(valid_flags, my_seq, 0, False)
    flags = xor_order(flags.reshape(blocks, groups, span), 1, my_group).reshape(length)
    segment = jnp.sum((offsets[None, :] <= place[:, None]).astype(jnp.int32), axis=1) - 1
    seg_row = segment.reshape(length // QUERY_ROWS, 1, QUERY_ROWS)
    seg_key = jnp.where(flags > 0, segment, -1)
    seg_key = jnp.broadcast_to(seg_key[:, None], (length, 128))
    first_turn = (my_part * (parts_length // QUERY_ROWS)).reshape(1).astype(jnp.int32)
    attn_low, attn_t, lse = attend(first_turn, seg_row, seg_key, qkv, wide, parts_length)

    part_blocks = blocks // repeats
    sent = attn_low.reshape(part_blocks, groups, wide, 2 * HEAD_DIM)
    sent = xor_order(sent, 1, my_group)
    sent = jnp.broadcast_to(sent[None], (repeats,) + sent.shape)
    sent = sent.reshape(devices, wide, 2 * HEAD_DIM)
    got = lax.all_to_all(sent, ALL, split_axis=0, concat_axis=0, tiled=True)
    got = got.reshape(seqs, heads_here, repeats, groups, wide, 2, HEAD_DIM)
    got = lax.dynamic_index_in_dim(got, my_block // part_blocks, 2, False)
    attn_tok = jnp.transpose(got, (0, 4, 3, 2, 1, 5)).reshape(rows, width)

    resid_in = token_rows.astype(F32)
    branch = matmul(attn_tok, mat_out) + vec_out
    normed_one, unit_one, inv_one = layer_norm(resid_in + branch, gain_one, bias_one)
    normed_low = normed_one.astype(BF16)
    normed_all = jnp.concatenate(gather_parts(normed_low, "heads"), axis=0)
    hidden = matmul(normed_all, mat_up) + vec_up
    act_low = jax.nn.gelu(hidden, approximate=False).astype(BF16)
    ffn_all = matmul(act_low, mat_down)
    ffn = scatter_parts(jnp.split(ffn_all, groups), "heads") + vec_down
    normed_two, unit_two, inv_two = layer_norm(normed_one + ffn, gain_two, bias_two)
    output = normed_two.astype(BF16).reshape(tokens.shape)
    my_span = my_block * groups + my_group
    local_flags = lax.dynamic_slice_in_dim(valid_flags, my_span * span, span, 1)
    local_flags = local_flags.reshape(rows).astype(F32)
    squares = jnp.stack(
        [
            jnp.sum(local_flags * jnp.sum(item * item, axis=1))
            for item in (resid_in, branch, normed_one, ffn)
        ]
    )

    upstream = cotangent.reshape(rows, width).astype(F32)
    grad_gain_two = jnp.sum(upstream * unit_two, axis=0)
    grad_bias_two = jnp.sum(upstream, axis=0)
    grad_resid_two = norm_back(upstream, unit_two, inv_two, gain_two)
    grad_ffn = grad_resid_two.astype(BF16)
    grad_vec_down = jnp.sum(grad_ffn.astype(F32), axis=0)
    grad_ffn_all = jnp.concatenate(gather_parts(grad_ffn, "heads"), axis=0)
    grad_hidden = (matmul_nt(grad_ffn_all, mat_down) * gelu_slope(hidden)).astype(BF16)
    grad_vec_up = jnp.sum(grad_hidden.astype(F32), axis=0)
    grad_normed_all = matmul_nt(grad_hidden, mat_up)
    grad_normed_one = grad_resid_two + scatter_parts(jnp.split(grad_normed_all, groups), "heads")
    grad_mat_down = matmul_tn(act_low, grad_ffn_all).astype(BF16)
    grad_mat_up = matmul_tn(normed_all, grad_hidden).astype(BF16)
    ffn_grads = jnp.concatenate(
        [
            grad_mat_down.reshape(blocks, unit_rows, width),
            grad_mat_up.reshape(blocks, -1, width),
        ],
        axis=1,
    )
    ffn_grads = lax.psum_scatter(
        ffn_grads.reshape(-1, width), "blk", scatter_dimension=0, tiled=True
    )
    shard_down = ffn_grads[:unit_rows].astype(F32)
    shard_up = lax.all_to_all(
        ffn_grads[unit_rows:].reshape(groups, dim_rows, units_here),
        "heads",
        split_axis=0,
        concat_axis=0,
        tiled=True,
    )
    shard_up = jnp.transpose(
        shard_up.reshape(groups, dim_rows, blocks, unit_rows), (1, 2, 0, 3)
    ).reshape(dim_rows, hidden_size)
    shard_up = shard_up.astype(F32)

    grad_gain_one = jnp.sum(grad_normed_one * unit_one, axis=0)
    grad_bias_one = jnp.sum(grad_normed_one, axis=0)
    grad_resid_one = norm_back(grad_normed_one, unit_one, inv_one, gain_one)
    grad_branch = grad_resid_one.astype(BF16)
    grad_vec_out = jnp.sum(grad_branch.astype(F32), axis=0)
    grad_attn = matmul_nt(grad_branch, mat_out).astype(BF16)

    sent = grad_attn.reshape(seqs, 2, wide, groups, heads_here, HEAD_DIM)
    sent = jnp.transpose(sent, (0, 4, 3, 2, 1, 5))
    sent = sent.reshape(pairs, 1, groups, wide, 2 * HEAD_DIM)
    sent = jnp.broadcast_to(sent, (pairs, repeats) + sent.shape[2:])
    sent = sent.reshape(devices, wide, 2 * HEAD_DIM)
    small = jnp.stack(
        [grad_vec_out, grad_vec_down, grad_gain_one, grad_bias_one, grad_gain_two, grad_bias_two]
    )
    small = jnp.transpose(small.reshape(6, devices, dim_rows), (1, 0, 2)).reshape(devices, -1)
    up_sums = jnp.zeros((blocks, groups, unit_rows), F32)
    up_sums = lax.dynamic_update_slice_in_dim(
        up_sums, grad_vec_up.reshape(blocks, 1, unit_rows), my_group, 1
    ).reshape(devices, unit_rows)
    small = jnp.concatenate(
        [small, up_sums, jnp.broadcast_to(squares[None], (devices, 4))], axis=1
    )
    small_count = small.shape[1]
    small = two_halves(small).reshape(devices, 2 * small_count)
    extra = 16 * (-(-2 * small_count // 2048))
    small = jnp.pad(small, ((0, 0), (0, extra * 128 - 2 * small_count)))
    sent = jnp.concatenate([sent, small.reshape(devices, extra, 128)], axis=1)
    got = lax.all_to_all(sent, ALL, split_axis=0, concat_axis=0, tiled=True)
    up_heads = got[:, :wide].reshape(blocks, groups, wide, 2 * HEAD_DIM)
    up_heads = xor_order(up_heads, 1, my_group).reshape(devices, wide, 2 * HEAD_DIM)
    small = jnp.sum(got[:, wide:].reshape(devices, extra * 128).astype(F32), axis=0)
    small = jnp.sum(small[: 2 * small_count].reshape(small_count, 2), axis=1)
    vector_sums = small[: 6 * dim_rows].reshape(6, dim_rows)
    shard_vec_up = small[6 * dim_rows : 6 * dim_rows + unit_rows]
    totals = small[6 * dim_rows + unit_rows :]
    real_count = jnp.maximum(jnp.sum(valid_flags.astype(F32)), 1.0)
    rms = jnp.sqrt(totals / (real_count * width))

    attn_columns = jnp.transpose(
        attn_tok.reshape(rows, blocks, groups, dim_rows), (2, 0, 1, 3)
    ).reshape(groups, rows, blocks * dim_rows)
    attn_columns = lax.all_to_all(
        attn_columns, "heads", split_axis=0, concat_axis=0, tiled=True
    )
    attn_columns = xor_order(attn_columns, 0, my_group)
    branch_parts = gather_parts(grad_branch, "heads")
    grad_mat_out = matmul_tn(
        attn_columns.reshape(groups * rows, blocks * dim_rows),
        jnp.concatenate(branch_parts, axis=0),
    ).astype(BF16)
    shard_out = scatter_blk(grad_mat_out.reshape(blocks, dim_rows, width))

    grads = attend_back(first_turn, seg_row, seg_key, qkv, up_heads, attn_t, lse)
    got = lax.all_to_all(grads, "blk", split_axis=0, concat_axis=0, tiled=True)
    got = got.reshape(pairs, repeats, block_rows + half, 2 * HEAD_DIM)
    got = jnp.sum(got.astype(F32), axis=1).astype(BF16) if repeats > 1 else got[:, 0]
    got = got.reshape(seqs, heads_here, block_rows + half, 2 * HEAD_DIM)
    grad_pair = got[:, :, :block_rows].reshape(seqs, heads_here, block_rows, 2, HEAD_DIM)
    grad_pair = jnp.transpose(grad_pair, (3, 0, 2, 1, 4))
    grad_pair = grad_pair.reshape(2, seqs * block_rows, width_here)
    grad_value = got[:, :, block_rows:].reshape(seqs, heads_here, half, 2, HEAD_DIM)
    grad_value = jnp.transpose(grad_value, (0, 3, 2, 1, 4)).reshape(seqs * block_rows, width_here)
    grad_query = grad_pair[0] * jnp.asarray(qk_scale, BF16)
    grad_three = jnp.concatenate([grad_query, grad_pair[1], grad_value], axis=1)
    grad_input = matmul_nt(grad_three, mat_three)
    grad_input = grad_input.reshape(seqs, groups, span, width)
    grad_input = scatter_parts([grad_input[:, k].reshape(rows, width) for k in range(groups)], "heads")
    grad_input = (grad_resid_one + grad_input).reshape(tokens.shape)
    grad_mat_three = matmul_tn(token_all, grad_three)
    sums = jnp.sum(grad_three.astype(F32), axis=0)
    query_sums = sums[:width_here]
    value_sums = sums[2 * width_here :]
    chunks = blocks // groups
    sums = jnp.concatenate(
        [
            query_sums.reshape(chunks, groups * dim_rows),
            value_sums.reshape(chunks, groups * dim_rows),
            jnp.zeros((chunks, 3 * width_here - 2 * groups * dim_rows), F32),
        ],
        axis=1,
    )
    sums = jnp.concatenate([sums] * groups, axis=0)
    is_owner = jnp.arange(blocks, dtype=jnp.int32) // chunks == my_group
    sums = jnp.where(is_owner[:, None], sums, 0.0)
    row = lax.broadcasted_iota(jnp.int32, (1, 16, 1), 1)
    sum_rows = jnp.where(row == 0, sums[:, None, :], 0.0)
    three_grads = jnp.concatenate(
        [grad_mat_three.reshape(blocks, groups * dim_rows, 3 * width_here), sum_rows], axis=1
    ).astype(BF16)
    three_grads = scatter_blk(three_grads)
    own_rows = three_grads[: groups * dim_rows].reshape(groups, dim_rows, 3 * width_here)
    own_sums = three_grads[groups * dim_rows, : 2 * groups * dim_rows]
    own_sums = jnp.transpose(own_sums.reshape(2, groups, dim_rows), (1, 0, 2))
    own_sums = jnp.concatenate(
        [
            own_sums.reshape(groups, 2 * dim_rows),
            jnp.zeros((groups, 3 * width_here - 2 * dim_rows), F32),
        ],
        axis=1,
    )
    own_sums = jnp.where(row == 0, own_sums[:, None, :], 0.0)
    own = jnp.concatenate([own_rows, own_sums], axis=1).astype(BF16)
    own = lax.all_to_all(own, "heads", split_axis=0, concat_axis=0, tiled=True).astype(F32)
    shard_sums = jnp.sum(own[:, dim_rows, : 2 * dim_rows], axis=0)
    shards_three = [
        jnp.transpose(
            own[:, :dim_rows, which * width_here : (which + 1) * width_here], (1, 0, 2)
        ).reshape(dim_rows, width)
        for which in range(3)
    ]

    return (
        output,
        grad_input,
        shards_three[0],
        shards_three[1],
        shards_three[2],
        shard_out,
        shard_up,
        shard_down,
        shard_sums[:dim_rows],
        shard_sums[dim_rows:],
        vector_sums[0],
        shard_vec_up,
        vector_sums[1],
        vector_sums[2],
        vector_sums[3],
        vector_sums[4],
        vector_sums[5],
        rms,
    )


def solution(mesh):
    token_spec = P(None, ALL, None)
    matrix_spec = P(ALL, None)
    vector_spec = P(ALL)
    return jax.shard_map(
        per_device,
        mesh=mesh,
        in_specs=(token_spec,) * 2 + (P(),) * 2 + (matrix_spec,) * 6 + (vector_spec,) * 9,
        out_specs=(token_spec,) * 2 + (matrix_spec,) * 6 + (vector_spec,) * 9 + (P(),),
        check_vma=False,
    )
```

```python
import functools

import jax
import jax.numpy as jnp
from jax import lax
from jax.experimental import pallas as pl
from jax.experimental.pallas import tpu as pltpu
from jax.sharding import PartitionSpec as P

HEAD_DIM = 64
NORM_EPS = 1e-05
NEG_LARGE = -1e30
QUERY_ROWS = 256
BF16 = jnp.bfloat16
F32 = jnp.float32
ALL = ("blk", "heads")


def vmem_limit(length):
    return 8 * 1024 * 1024 + 6 * 1024 * length


def matmul(left, right):
    return jnp.dot(left, right, preferred_element_type=F32)


def matmul_tn(left, right):
    return lax.dot_general(left, right, (((0,), (0,)), ((), ())), preferred_element_type=F32)


def matmul_nt(left, right):
    return lax.dot_general(left, right, (((1,), (1,)), ((), ())), preferred_element_type=F32)


def after(block, other):
    spot = lax.slice(other, (0,) * other.ndim, (1,) * other.ndim).reshape(())
    return block + (spot * 0).astype(block.dtype)


def swapped(block, axis, mask):
    count = lax.axis_size(axis)
    return lax.ppermute(block, axis, [(i, i ^ mask) for i in range(count)])


def gather_parts(block, axis):
    return [block] + [swapped(block, axis, k) for k in range(1, lax.axis_size(axis))]


def scatter_parts(parts, axis):
    total = parts[0].astype(F32)
    for k in range(1, len(parts)):
        total = total + swapped(parts[k].astype(BF16), axis, k).astype(F32)
    return total


def xor_order(array, dim, index):
    pieces = [
        lax.dynamic_index_in_dim(array, index ^ k, dim, True) for k in range(array.shape[dim])
    ]
    return jnp.concatenate(pieces, axis=dim)


def gather_blk_parts(block, first_needs):
    count = lax.axis_size("blk")
    mine = jnp.stack([block] + [swapped(block, "blk", k) for k in range(2, count, 2)])
    mine = after(mine, first_needs)
    return mine, swapped(mine, "blk", 1)


def gather_blk(block, first_needs):
    mine, other = gather_blk_parts(block, first_needs)
    both = jnp.stack([mine, other], axis=1).reshape((-1,) + block.shape)
    return xor_order(both, 0, lax.axis_index("blk"))


def scatter_blk(blocks):
    index = lax.axis_index("blk")
    ordered = xor_order(blocks, 0, index)
    pairs = ordered.reshape((ordered.shape[0] // 2, 2) + ordered.shape[1:])
    total = pairs[:, 0].astype(F32) + swapped(pairs[:, 1], "blk", 1).astype(F32)
    low = total.astype(BF16)
    result = total[0]
    for k in range(1, low.shape[0]):
        result = result + swapped(low[k], "blk", 2 * k).astype(F32)
    return result


def layer_norm(resid, norm_gain, norm_bias):
    center = resid - jnp.mean(resid, axis=-1, keepdims=True)
    inv_std = lax.rsqrt(jnp.mean(center * center, axis=-1, keepdims=True) + NORM_EPS)
    normed = center * inv_std
    return (normed * norm_gain + norm_bias, normed, inv_std)


def norm_back(upstream, normed, inv_std, norm_gain):
    scaled = upstream * norm_gain
    return inv_std * (
        scaled
        - jnp.mean(scaled, axis=-1, keepdims=True)
        - normed * jnp.mean(scaled * normed, axis=-1, keepdims=True)
    )


def gelu_slope(hidden):
    cdf_part = 0.5 * (1.0 + lax.erf(hidden * 0.7071067811865476))
    pdf_part = jnp.exp(-0.5 * hidden * hidden) * 0.3989422804014327
    return cdf_part + hidden * pdf_part


def two_halves(values):
    high = lax.reduce_precision(values, 8, 7)
    return jnp.stack([high, values - high], axis=-1).astype(BF16)


def left_lanes(block):
    lane = lax.broadcasted_iota(jnp.int32, block.shape, 1)
    return jnp.where(lane < HEAD_DIM, block, 0.0)


def masked_scores(seg_key, seg_query, scores):
    width = scores.shape[1] // seg_key.shape[1]
    same = jnp.concatenate([seg_key] * width, axis=1) == seg_query
    return jnp.where(same, scores, NEG_LARGE)


def own_scores(seg_key, seg_query, scores):
    width = scores.shape[1] // seg_key.shape[1]
    same = jnp.concatenate([seg_key] * width, axis=1) == seg_query
    rows = lax.broadcasted_iota(jnp.int32, scores.shape, 0)
    columns = lax.broadcasted_iota(jnp.int32, scores.shape, 1)
    return jnp.where(same | (rows == columns), scores, NEG_LARGE)


def score_all(turn, seg_query, seg_key_ref, qkv_ref, query_t, scores):
    sources, rows = qkv_ref.shape[0], qkv_ref.shape[1] * 2 // 3
    per_source = rows // QUERY_ROWS
    query_now = query_t[turn]
    for b in range(sources):
        spot = slice(b * rows, (b + 1) * rows)
        scores[spot, :] = masked_scores(
            seg_key_ref[spot, :], seg_query, matmul(qkv_ref[b, 0:rows, :], query_now)
        )
    own = pl.ds(pl.multiple_of(turn * QUERY_ROWS, QUERY_ROWS), QUERY_ROWS)
    inner = pl.ds(pl.multiple_of(turn % per_source * QUERY_ROWS, QUERY_ROWS), QUERY_ROWS)
    own_pair = qkv_ref[turn // per_source, inner, :]
    scores[own, :] = own_scores(seg_key_ref[own, :], seg_query, matmul(own_pair, query_now))
    return own, own_pair


def turn_queries(b, turned, query_t):
    per_source = turned.shape[1] // QUERY_ROWS
    low = jnp.concatenate([jnp.zeros_like(turned[0:HEAD_DIM]), turned[0:HEAD_DIM]], axis=0)
    for t in range(per_source):
        spot = slice(t * QUERY_ROWS, (t + 1) * QUERY_ROWS)
        query_t[b * per_source + t] = low[:, spot].astype(BF16)


def attend_kernel(
    spot_ref, seg_row_ref, seg_key_ref, qkv_ref, low_ref, attn_ref, lse_ref,
    query_t, values_t, scores,
):
    step = pl.program_id(0)
    sources, rows = qkv_ref.shape[0], qkv_ref.shape[1] * 2 // 3
    half = rows // 2

    @pl.when(step == 0)
    def _():
        for b in range(sources):
            turn_queries(b, qkv_ref[b, 0:rows, :].astype(F32).T, query_t)
            turned = qkv_ref[b, rows : rows + half, :].astype(F32).T
            values_t[:, b * rows : b * rows + half] = turned[0:HEAD_DIM].astype(BF16)
            values_t[:, b * rows + half : (b + 1) * rows] = turned[
                HEAD_DIM : 2 * HEAD_DIM
            ].astype(BF16)

    turn = spot_ref[2] + step
    score_all(turn, seg_row_ref[0], seg_key_ref, qkv_ref, query_t, scores)
    top = jnp.max(scores[...], axis=0, keepdims=True)
    total = jnp.zeros_like(top)
    result = jnp.zeros((HEAD_DIM, QUERY_ROWS), F32)
    for b in range(sources):
        spot = slice(b * rows, (b + 1) * rows)
        probs = jnp.exp(scores[spot, :] - top)
        total = total + jnp.sum(probs, axis=0, keepdims=True)
        result = result + matmul(values_t[:, spot], probs.astype(BF16))
    result = result / total
    attn_ref[...] = result
    lse_ref[0] = top + jnp.log(total)
    turned = result.T
    wide = low_ref.shape[1]
    spans = QUERY_ROWS // (2 * wide)
    first = turn % (rows // QUERY_ROWS) * spans
    for t in range(spans):
        left = turned[2 * t * wide : (2 * t + 1) * wide]
        right = turned[(2 * t + 1) * wide : (2 * t + 2) * wide]
        low_ref[spot_ref[1] ^ (first + t)] = jnp.concatenate([left, right], axis=1).astype(BF16)


def attend(spot, seg_row, seg_key, qkv, wide, query_length):
    sources, rows = qkv.shape[0], qkv.shape[1] * 2 // 3
    length = sources * rows
    steps = query_length // QUERY_ROWS
    spans = rows // (2 * wide)
    per_source = rows // QUERY_ROWS
    return pl.pallas_call(
        attend_kernel,
        grid_spec=pltpu.PrefetchScalarGridSpec(
            num_scalar_prefetch=1,
            grid=(steps,),
            in_specs=[
                pl.BlockSpec((1, 1, QUERY_ROWS), lambda i, spot: (spot[2] + i, 0, 0)),
                pl.BlockSpec(seg_key.shape, lambda i, spot: (0, 0)),
                pl.BlockSpec(qkv.shape, lambda i, spot: (0, 0, 0)),
            ],
            out_specs=[
                pl.BlockSpec((spans, wide, 128), lambda i, spot: (i // per_source, 0, 0)),
                pl.BlockSpec((HEAD_DIM, QUERY_ROWS), lambda i, spot: (0, i)),
                pl.BlockSpec((1, 1, QUERY_ROWS), lambda i, spot: (i, 0, 0)),
            ],
            scratch_shapes=[
                pltpu.VMEM((length // QUERY_ROWS, 128, QUERY_ROWS), BF16),
                pltpu.VMEM((HEAD_DIM, length), BF16),
                pltpu.VMEM((length, QUERY_ROWS), F32),
            ],
        ),
        out_shape=[
            jax.ShapeDtypeStruct((steps // per_source * spans, wide, 128), BF16),
            jax.ShapeDtypeStruct((HEAD_DIM, query_length), F32),
            jax.ShapeDtypeStruct((steps, 1, QUERY_ROWS), F32),
        ],
        compiler_params=pltpu.CompilerParams(vmem_limit_bytes=vmem_limit(length)),
    )(spot, seg_row, seg_key, qkv)


def attend_back_kernel(
    spot_ref, seg_row_ref, seg_key_ref, qkv_ref, up_ref, attn_ref, lse_ref, grads_ref,
    query_t, keys_t, values, scores, grad_query, grad_key, grad_value,
):
    step = pl.program_id(0)
    sources, rows = qkv_ref.shape[0], qkv_ref.shape[1] * 2 // 3
    half = rows // 2
    lane = lax.broadcasted_iota(jnp.int32, (rows, 128), 1)

    @pl.when(step == 0)
    def _():
        for b in range(sources):
            turned = qkv_ref[b, 0:rows, :].astype(F32).T
            turn_queries(b, turned, query_t)
            keys_t[:, b * rows : (b + 1) * rows] = turned[HEAD_DIM : 2 * HEAD_DIM].astype(BF16)
            packed = qkv_ref[b, rows : rows + half, :].astype(F32)
            values[b * rows : b * rows + half, :] = left_lanes(packed).astype(BF16)
            values[b * rows + half : (b + 1) * rows, :] = left_lanes(
                pltpu.roll(packed, HEAD_DIM, 1)
            ).astype(BF16)
        grad_query[...] = jnp.zeros_like(grad_query)
        grad_key[...] = jnp.zeros_like(grad_key)
        grad_value[...] = jnp.zeros_like(grad_value)

    turn = spot_ref[2] + step
    lse = lse_ref[0]
    pieces = []
    spans = QUERY_ROWS // (rows // up_ref.shape[0])
    first = turn % (rows // QUERY_ROWS) * spans
    for t in range(spans):
        packed = up_ref[spot_ref[1] ^ (first + t), 0 : rows // up_ref.shape[0] // 2, :].astype(F32)
        pieces.append(left_lanes(packed))
        pieces.append(left_lanes(pltpu.roll(packed, HEAD_DIM, 1)))
    up_now = jnp.concatenate(pieces, axis=0)
    up_turned = up_now.T
    delta = jnp.sum(up_turned[0:HEAD_DIM] * attn_ref[...], axis=0, keepdims=True)
    up_now = up_now.astype(BF16)
    up_turned = up_turned.astype(BF16)
    own, own_pair = score_all(turn, seg_row_ref[0], seg_key_ref, qkv_ref, query_t, scores)
    query_now = pltpu.roll(own_pair.astype(F32), HEAD_DIM, 1).astype(BF16)
    result = jnp.zeros((HEAD_DIM, QUERY_ROWS), F32)
    for b in range(sources):
        spot = slice(b * rows, (b + 1) * rows)
        probs = jnp.exp(scores[spot, :] - lse)
        grad_probs = matmul(values[spot, :], up_turned)
        grad_scores = (probs * (grad_probs - delta)).astype(BF16)
        grad_value[spot, :] += matmul(probs.astype(BF16), up_now)
        grad_key[spot, :] += matmul(grad_scores, query_now)
        result = result + matmul(keys_t[:, spot], grad_scores)
    grad_query[own, :] = jnp.concatenate([result, jnp.zeros_like(result)], axis=0).T

    @pl.when(step == pl.num_programs(0) - 1)
    def _():
        for b in range(sources):
            spot = slice(b * rows, (b + 1) * rows)
            grads_ref[b, 0:rows, :] = jnp.where(
                lane < HEAD_DIM, grad_query[spot, :], grad_key[spot, :]
            ).astype(BF16)
            upper = grad_value[b * rows : b * rows + half, :]
            lower = grad_value[b * rows + half : (b + 1) * rows, :]
            grads_ref[b, rows : rows + half, :] = (
                upper + pltpu.roll(lower, HEAD_DIM, 1)
            ).astype(BF16)


def attend_back(spot, seg_row, seg_key, qkv, upstream, attn_t, lse):
    sources, rows = qkv.shape[0], qkv.shape[1] * 2 // 3
    length = sources * rows
    steps = lse.shape[0]
    groups = upstream.shape[0] // sources
    per_source = rows // QUERY_ROWS
    return pl.pallas_call(
        attend_back_kernel,
        grid_spec=pltpu.PrefetchScalarGridSpec(
            num_scalar_prefetch=1,
            grid=(steps,),
            in_specs=[
                pl.BlockSpec((1, 1, QUERY_ROWS), lambda i, spot: (spot[2] + i, 0, 0)),
                pl.BlockSpec(seg_key.shape, lambda i, spot: (0, 0)),
                pl.BlockSpec(qkv.shape, lambda i, spot: (0, 0, 0)),
                pl.BlockSpec(
                    (groups,) + upstream.shape[1:],
                    lambda i, spot: ((spot[2] + i) // per_source, 0, 0),
                ),
                pl.BlockSpec((HEAD_DIM, QUERY_ROWS), lambda i, spot: (0, i)),
                pl.BlockSpec((1, 1, QUERY_ROWS), lambda i, spot: (i, 0, 0)),
            ],
            out_specs=pl.BlockSpec(qkv.shape, lambda i, spot: (0, 0, 0)),
            scratch_shapes=[
                pltpu.VMEM((length // QUERY_ROWS, 128, QUERY_ROWS), BF16),
                pltpu.VMEM((HEAD_DIM, length), BF16),
                pltpu.VMEM((length, 128), BF16),
                pltpu.VMEM((length, QUERY_ROWS), F32),
                pltpu.VMEM((length, 128), F32),
                pltpu.VMEM((length, 128), F32),
                pltpu.VMEM((length, 128), F32),
            ],
        ),
        out_shape=jax.ShapeDtypeStruct(qkv.shape, BF16),
        compiler_params=pltpu.CompilerParams(vmem_limit_bytes=vmem_limit(length)),
    )(spot, seg_row, seg_key, qkv, upstream, attn_t, lse)


def left_pair(first, second):
    lane = lax.broadcasted_iota(jnp.int32, first.shape, 1)
    return jnp.where(lane < HEAD_DIM, first, pltpu.roll(second, HEAD_DIM, 1))


def right_pair(first, second):
    lane = lax.broadcasted_iota(jnp.int32, first.shape, 1)
    return jnp.where(lane < HEAD_DIM, pltpu.roll(first, HEAD_DIM, 1), second)


def join_kernel(
    seqs, heads_here, repeats, spot_ref, got_ref, tokens_ref, flags_ref, mat_ref, vectors_ref,
    sent_ref, normed_ref, unit_ref, inv_ref, squares_ref, attn,
):
    my_group, part = spot_ref[1], spot_ref[3]
    groups = sent_ref.shape[0]
    wide = got_ref.shape[1]
    width = tokens_ref.shape[1]
    width_here = heads_here * HEAD_DIM
    for which in range(seqs):
        for group in range(groups):
            for head in range(0, heads_here, 2):
                first, second = [
                    got_ref[
                        ((which * heads_here + i) * repeats + part) * groups + group
                    ].astype(F32)
                    for i in (head, head + 1)
                ]
                start = group * width_here + head * HEAD_DIM
                top = 2 * which * wide
                attn[top : top + wide, start : start + 128] = left_pair(first, second).astype(BF16)
                attn[top + wide : top + 2 * wide, start : start + 128] = right_pair(
                    first, second
                ).astype(BF16)
    branch = matmul(attn[...], mat_ref[...]) + vectors_ref[0:1, :]
    resid_in = tokens_ref[...].astype(F32)
    normed, unit, inv_std = layer_norm(resid_in + branch, vectors_ref[2:3, :], vectors_ref[3:4, :])
    normed_ref[...] = normed
    unit_ref[...] = unit
    inv_ref[...] = jnp.broadcast_to(inv_std, inv_ref.shape)
    low = normed.astype(BF16)
    for k in range(groups):
        sent_ref[k, :, 0:width] = low
        for group in range(groups):

            @pl.when((my_group ^ k) == group)
            def _():
                sent_ref[k, :, width:] = attn[:, group * width_here : (group + 1) * width_here]

    lane = lax.broadcasted_iota(jnp.int32, squares_ref.shape, 1)
    total = jnp.zeros(squares_ref.shape, F32)
    for i, item in enumerate((resid_in, branch, normed)):
        size = flags_ref[...] * jnp.sum(item * item, axis=1, keepdims=True)
        total = total + jnp.where(lane == i, jnp.sum(size, axis=0, keepdims=True), 0.0)
    squares_ref[...] = total


def join(spot, got, tokens, flags, mat_out, vectors, seqs, heads_here, repeats):
    groups = tokens.shape[1] // (heads_here * HEAD_DIM)
    rows, width = tokens.shape
    vmem = pl.BlockSpec(memory_space=pltpu.VMEM)
    return pl.pallas_call(
        functools.partial(join_kernel, seqs, heads_here, repeats),
        in_specs=[pl.BlockSpec(memory_space=pltpu.SMEM)] + [vmem] * 5,
        out_specs=[vmem] * 5,
        out_shape=[
            jax.ShapeDtypeStruct((groups, rows, width + heads_here * HEAD_DIM), BF16),
            jax.ShapeDtypeStruct((rows, width), F32),
            jax.ShapeDtypeStruct((rows, width), F32),
            jax.ShapeDtypeStruct((rows, 128), F32),
            jax.ShapeDtypeStruct((1, 128), F32),
        ],
        scratch_shapes=[pltpu.VMEM((rows, width), BF16)],
        compiler_params=pltpu.CompilerParams(vmem_limit_bytes=32 * 1024 * 1024),
    )(spot, got, tokens, flags, mat_out, vectors)


def branch_back_kernel(
    seqs, heads_here, repeats, spot_ref, *refs,
):
    (own_ref, resid_ref, unit_ref, inv_ref, gain_ref, mat_ref, early_ref, up_sums_ref,
     squares_ref), others, (sent_ref, grad_ref, low_ref) = refs[:9], refs[9:-3], refs[-3:]
    my_group = spot_ref[1]
    groups = len(others) + 1
    rows, width = own_ref.shape
    span = rows // seqs
    wide = span // 2
    devices = sent_ref.shape[0]
    blocks = devices // groups
    grad_normed = own_ref[...]
    for other in others:
        grad_normed = grad_normed + other[...].astype(F32)
    grad_normed = grad_normed + resid_ref[...]
    unit = unit_ref[...]
    grad_resid = norm_back(grad_normed, unit, inv_ref[:, 0:1], gain_ref[...])
    grad_ref[...] = grad_resid
    low = grad_resid.astype(BF16)
    low_ref[...] = low
    grad_attn = matmul_nt(low, mat_ref[...])
    for which in range(seqs):
        top = which * span
        for group in range(groups):
            for head in range(0, heads_here, 2):
                start = (group * heads_here + head) * HEAD_DIM
                upper = grad_attn[top : top + wide, start : start + 128]
                lower = grad_attn[top + wide : top + span, start : start + 128]
                blocks_two = (left_pair(upper, lower), right_pair(upper, lower))
                for i in range(2):
                    for copy in range(repeats):
                        pair = which * heads_here + head + i
                        place = (pair * repeats + copy) * groups + group
                        sent_ref[place, 0:wide, :] = blocks_two[i].astype(BF16)
    sums = [
        jnp.sum(low.astype(F32), axis=0, keepdims=True),
        jnp.sum(grad_normed * unit, axis=0, keepdims=True),
        jnp.sum(grad_normed, axis=0, keepdims=True),
    ] + [early_ref[i : i + 1, :] for i in range(3)]
    row = lax.broadcasted_iota(jnp.int32, (8, 128), 0)
    dim_rows = width // devices
    unit_rows = up_sums_ref.shape[1] // blocks
    for tile in range(width // 128):
        base = jnp.where(row == 7, squares_ref[...], 0.0)
        for i in range(6):
            base = base + jnp.where(row == i, sums[i][:, tile * 128 : (tile + 1) * 128], 0.0)
        for place in range(tile * 128 // dim_rows, (tile + 1) * 128 // dim_rows):
            start = place // groups * unit_rows // 128 * 128
            mine = jnp.where(my_group == place % groups, up_sums_ref[:, start : start + 128], 0.0)
            block = base + jnp.where(row == 6, mine, 0.0)
            high = block.astype(BF16)
            rest = block - high.astype(F32)
            sent_ref[place, wide : wide + 16, :] = jnp.concatenate(
                [high.astype(F32), rest], axis=0
            ).astype(BF16)


def branch_back(spot, own, others, resid, unit, inv_std, gain, mat_out, early, up_sums, squares,
                seqs, heads_here, repeats, devices):
    rows, width = own.shape
    vmem = pl.BlockSpec(memory_space=pltpu.VMEM)
    return pl.pallas_call(
        functools.partial(branch_back_kernel, seqs, heads_here, repeats),
        in_specs=[pl.BlockSpec(memory_space=pltpu.SMEM)] + [vmem] * (9 + len(others)),
        out_specs=[vmem] * 3,
        out_shape=[
            jax.ShapeDtypeStruct((devices, rows // seqs // 2 + 16, 128), BF16),
            jax.ShapeDtypeStruct((rows, width), F32),
            jax.ShapeDtypeStruct((rows, width), BF16),
        ],
        compiler_params=pltpu.CompilerParams(vmem_limit_bytes=32 * 1024 * 1024),
    )(spot, own, resid, unit, inv_std, gain, mat_out, early, up_sums, squares, *others)


def project_kernel(groups, heads_here, repeats, spot_ref, *refs):
    tokens, (mine_ref, other_ref, sent_ref, all_ref, mat_ref, values) = refs[:groups], refs[groups:]
    my_block, my_group = spot_ref[0], spot_ref[1]
    halves, chip_rows, _ = mine_ref.shape
    blocks = 2 * halves
    dim_rows = chip_rows // groups
    rows, width = tokens[0].shape
    width_here = heads_here * HEAD_DIM
    seqs = sent_ref.shape[0] // (repeats * heads_here)
    span = rows // seqs
    block_rows = span * groups
    for k in range(groups):
        all_ref[k * rows : (k + 1) * rows, :] = tokens[k][...]
    for b in range(blocks):
        place = my_block ^ b
        spot = slice(b * chip_rows, (b + 1) * chip_rows)

        @pl.when(place % 2 == 0)
        def _():
            mat_ref[spot, :] = mine_ref[place // 2, :, 0 : 3 * width_here]

        @pl.when(place % 2 == 1)
        def _():
            mat_ref[spot, :] = other_ref[place // 2, :, 0 : 3 * width_here]

    lane = lax.broadcasted_iota(jnp.int32, (1, 128), 1)
    tiles = width_here // 128
    biases = [[jnp.zeros((1, 128), F32) for _ in range(tiles)] for _ in range(2)]
    for t in range(blocks):
        place = my_block ^ (my_group * (blocks // groups) + t // groups)
        piece = jnp.where(
            place % 2 == 0,
            mine_ref[place // 2, :, 3 * width_here :].astype(F32),
            other_ref[place // 2, :, 3 * width_here :].astype(F32),
        )
        piece = piece[t % groups * dim_rows : t % groups * dim_rows + 1]
        tile, start = t * dim_rows // 128, t * dim_rows % 128
        inside = (lane >= start) & (lane < start + dim_rows)
        for which in range(2):
            shift = (start - which * dim_rows) % 128
            moved = pltpu.roll(piece, shift, 1) if shift else piece
            biases[which][tile] = biases[which][tile] + jnp.where(inside, moved, 0.0)
    query_bias, value_bias = [jnp.concatenate(item, axis=1) for item in biases]
    result = matmul(all_ref[...], mat_ref[...])
    query = (result[:, :width_here] + query_bias) * HEAD_DIM ** (-0.5)
    key = result[:, width_here : 2 * width_here]
    values[...] = result[:, 2 * width_here :] + value_bias
    half_parts = groups // 2
    for pair in range(seqs * heads_here):
        which, head = pair // heads_here, pair % heads_here
        columns = slice(head * HEAD_DIM, (head + 1) * HEAD_DIM)
        for k in range(groups):
            spot = slice(k * rows + which * span, k * rows + (which + 1) * span)
            block = jnp.concatenate([query[spot, columns], key[spot, columns]], axis=1)
            for copy in range(repeats):
                sent_ref[pair * repeats + copy, k * span : (k + 1) * span, :] = block.astype(BF16)
        for k in range(half_parts):
            upper = slice(k * rows + which * span, k * rows + (which + 1) * span)
            lower = slice(upper.start + half_parts * rows, upper.stop + half_parts * rows)
            block = jnp.concatenate([values[upper, columns], values[lower, columns]], axis=1)
            for copy in range(repeats):
                sent_ref[
                    pair * repeats + copy, block_rows + k * span : block_rows + (k + 1) * span, :
                ] = block.astype(BF16)


def project(spot, token_parts, mine, other, seqs, heads_here, repeats):
    groups = len(token_parts)
    rows, width = token_parts[0].shape
    blocks = seqs * heads_here * repeats
    block_rows = rows // seqs * groups
    vmem = pl.BlockSpec(memory_space=pltpu.VMEM)
    return pl.pallas_call(
        functools.partial(project_kernel, groups, heads_here, repeats),
        in_specs=[pl.BlockSpec(memory_space=pltpu.SMEM)] + [vmem] * (groups + 2),
        out_specs=[vmem] * 3,
        out_shape=[
            jax.ShapeDtypeStruct((blocks, block_rows * 3 // 2, 128), BF16),
            jax.ShapeDtypeStruct((groups * rows, width), BF16),
            jax.ShapeDtypeStruct((width, 3 * heads_here * HEAD_DIM), BF16),
        ],
        scratch_shapes=[pltpu.VMEM((groups * rows, heads_here * HEAD_DIM), F32)],
        compiler_params=pltpu.CompilerParams(vmem_limit_bytes=40 * 1024 * 1024),
    )(spot, *token_parts, mine, other)


def input_kernel(
    groups, heads_here, repeats, spot_ref, got_ref, mat_ref, all_ref,
    own_ref, others_ref, keep_ref, send_ref, grads, mat_grads,
):
    my_block, my_group = spot_ref[0], spot_ref[1]
    blocks = got_ref.shape[0]
    seqs = blocks // (repeats * heads_here)
    rows = all_ref.shape[0] // groups
    span = rows // seqs
    block_rows = span * groups
    width_here = heads_here * HEAD_DIM
    chip_rows = keep_ref.shape[1] - 16
    half_parts = groups // 2

    def received(pair, start):
        spot = slice(start, start + span)
        total = got_ref[pair * repeats, spot, :].astype(F32)
        for copy in range(1, repeats):
            total = total + got_ref[pair * repeats + copy, spot, :].astype(F32)
        return total

    for which in range(seqs):
        for head in range(0, heads_here, 2):
            pair = which * heads_here + head
            start = head * HEAD_DIM
            for k in range(groups):
                spot = slice(k * rows + which * span, k * rows + (which + 1) * span)
                first, second = received(pair, k * span), received(pair + 1, k * span)
                grads[spot, start : start + 128] = (
                    left_pair(first, second) * HEAD_DIM ** (-0.5)
                ).astype(BF16)
                grads[spot, width_here + start : width_here + start + 128] = right_pair(
                    first, second
                ).astype(BF16)
                inner = block_rows + k % half_parts * span
                first, second = received(pair, inner), received(pair + 1, inner)
                grads[spot, 2 * width_here + start : 2 * width_here + start + 128] = (
                    left_pair(first, second) if k < half_parts else right_pair(first, second)
                ).astype(BF16)
    back = matmul_nt(grads[...], mat_ref[...])
    own_ref[...] = back[:rows]
    for k in range(1, groups):
        others_ref[k - 1] = back[k * rows : (k + 1) * rows].astype(BF16)
    mat_grads[...] = matmul_tn(all_ref[...], grads[...])
    query_sums = jnp.sum(grads[:, :width_here].astype(F32), axis=0, keepdims=True)
    value_sums = jnp.sum(grads[:, 2 * width_here :].astype(F32), axis=0, keepdims=True)
    chunks = blocks // groups
    chunk = width_here // chunks
    row = lax.broadcasted_iota(jnp.int32, (16, 128), 0)
    for k in range(blocks):
        owner = my_block ^ k
        spot = pl.ds(pl.multiple_of(owner * chip_rows, chip_rows), chip_rows)
        block = mat_grads[spot, :]
        sums = []
        for total in (query_sums, value_sums):
            chosen = jnp.zeros((1, chunk), F32)
            for i in range(chunks):
                piece = total[:, i * chunk : (i + 1) * chunk]
                chosen = chosen + jnp.where(owner == my_group * chunks + i, piece, 0.0)
            sums.append(jnp.concatenate([chosen, jnp.zeros((1, 128 - chunk), F32)], axis=1) if chunk < 128 else chosen)
        if k % 2 == 0:
            keep_ref[k // 2, 0:chip_rows, :] = block
        else:
            send_ref[k // 2, 0:chip_rows, :] = block.astype(BF16)
        for i in range(3 * width_here // 128):
            value = jnp.where(row == 0, sums[i], 0.0) if i < 2 else jnp.zeros((16, 128), F32)
            columns = slice(i * 128, (i + 1) * 128)
            if k % 2 == 0:
                keep_ref[k // 2, chip_rows : chip_rows + 16, columns] = value
            else:
                send_ref[k // 2, chip_rows : chip_rows + 16, columns] = value.astype(BF16)


def input_grads(spot, got, mat_three, token_all, heads_here, groups, repeats):
    blocks = got.shape[0]
    total_rows, width = token_all.shape
    rows = total_rows // groups
    chip_rows = width // blocks
    columns = mat_three.shape[1]
    vmem = pl.BlockSpec(memory_space=pltpu.VMEM)
    shape = (blocks // 2, chip_rows + 16, columns)
    return pl.pallas_call(
        functools.partial(input_kernel, groups, heads_here, repeats),
        in_specs=[pl.BlockSpec(memory_space=pltpu.SMEM)] + [vmem] * 3,
        out_specs=[vmem] * 4,
        out_shape=[
            jax.ShapeDtypeStruct((rows, width), F32),
            jax.ShapeDtypeStruct((groups - 1, rows, width), BF16),
            jax.ShapeDtypeStruct(shape, F32),
            jax.ShapeDtypeStruct(shape, BF16),
        ],
        scratch_shapes=[
            pltpu.VMEM((total_rows, columns), BF16),
            pltpu.VMEM((width, columns), F32),
        ],
        compiler_params=pltpu.CompilerParams(vmem_limit_bytes=40 * 1024 * 1024),
    )(spot, got, mat_three, token_all)


def per_device(
    tokens,
    cotangent,
    doc_offsets,
    valid_flags,
    w_query,
    w_key,
    w_value,
    w_out,
    w_fc1,
    w_fc2,
    b_query,
    b_value,
    b_out,
    b_fc1,
    b_fc2,
    gain_attn,
    bias_attn,
    gain_ffn,
    bias_ffn,
):
    seqs, span, width = tokens.shape
    groups = lax.axis_size("heads")
    blocks = lax.axis_size("blk")
    devices = groups * blocks
    my_group = lax.axis_index("heads")
    my_block = lax.axis_index("blk")
    rows = seqs * span
    block_rows = span * groups
    length = block_rows * blocks
    heads = width // HEAD_DIM
    heads_here = heads // groups
    pairs = seqs * heads_here
    repeats = blocks // pairs
    parts_length = length // repeats
    width_here = heads_here * HEAD_DIM
    dim_rows = w_query.shape[0]
    unit_rows = w_fc2.shape[0]
    hidden_size = w_fc1.shape[1]
    units_here = hidden_size // groups
    qk_scale = HEAD_DIM ** (-0.5)
    half = block_rows // 2
    wide = span // 2

    token_rows = tokens.reshape(rows, width)
    token_parts = gather_parts(token_rows, "heads")
    w_three = jnp.concatenate(
        [w.reshape(dim_rows, groups, width_here) for w in (w_query, w_key, w_value)], axis=-1
    )
    w_three = jnp.transpose(w_three, (1, 0, 2))
    def lanes_of(pieces):
        flat = jnp.concatenate(pieces)
        return jnp.pad(flat, (0, dim_rows * 128 - flat.shape[0])).reshape(dim_rows, 128)

    vectors = lanes_of([b_query, b_value])
    w_up = w_fc1.reshape(dim_rows, blocks, groups, unit_rows)
    w_up = jnp.transpose(w_up, (2, 0, 1, 3)).reshape(groups, dim_rows, units_here)
    first = jnp.concatenate(
        [w_three, jnp.broadcast_to(vectors[None], (groups,) + vectors.shape), w_up], axis=-1
    )
    first = lax.all_to_all(first, "heads", split_axis=0, concat_axis=0, tiled=True)
    first = first.reshape(groups * dim_rows, first.shape[-1])
    second = first[:, 3 * width_here + 128 :].reshape(-1, width)
    second = jnp.concatenate([second, w_fc2])
    third = lanes_of([b_out, b_fc2, gain_attn, bias_attn, gain_ffn, bias_ffn, b_fc1])
    third = after(jnp.concatenate([w_out, third], axis=1), first)
    third = lax.all_gather(third, ALL, axis=0, tiled=False)

    first = first[:, : 3 * width_here + 128]
    for part in token_parts[1:]:
        first = after(first, part)
    mine, other = gather_blk_parts(first, second)
    part_blocks = blocks // repeats
    first_turn = my_block % repeats * (parts_length // QUERY_ROWS)
    spot = jnp.stack([my_block, my_group, first_turn, my_block // part_blocks]).astype(jnp.int32)
    sent, token_all, mat_three = project(
        spot, token_parts, mine, other, seqs, heads_here, repeats
    )
    qkv = lax.all_to_all(sent, "blk", split_axis=0, concat_axis=0, tiled=True)


    mat_out = third[..., :width].reshape(width, width)
    vectors = third[..., width:].reshape(devices, dim_rows * 128)[:, : 6 * dim_rows + unit_rows]
    short = jnp.transpose(vectors[:, : 6 * dim_rows].reshape(devices, 6, dim_rows), (1, 0, 2))
    short = short.reshape(6, width).astype(F32)
    vec_out, vec_down, gain_one, bias_one, gain_two, bias_two = [short[i] for i in range(6)]
    vec_up = vectors[:, 6 * dim_rows :].reshape(blocks, groups, unit_rows)
    vec_up = lax.dynamic_index_in_dim(vec_up, my_group, 1, False).reshape(units_here).astype(F32)

    second = lax.all_gather(after(second, qkv), "blk", axis=0, tiled=False)
    up_rows = groups * dim_rows * units_here // width
    mat_up = second[:, :up_rows].reshape(width, units_here)
    mat_down = second[:, up_rows:].reshape(units_here, width)

    my_pair = my_block // repeats
    my_part = my_block % repeats
    my_seq = my_pair // heads_here
    inner = jnp.arange(length, dtype=jnp.int32)
    place = (inner // block_rows) * block_rows + inner % span
    place = place + (((inner // span) % groups) ^ my_group) * span
    offsets = lax.dynamic_index_in_dim(doc_offsets, my_seq, 0, False)
    flags = lax.dynamic_index_in_dim(valid_flags, my_seq, 0, False)
    flags = xor_order(flags.reshape(blocks, groups, span), 1, my_group).reshape(length)
    segment = jnp.sum((offsets[None, :] <= place[:, None]).astype(jnp.int32), axis=1) - 1
    seg_row = segment.reshape(length // QUERY_ROWS, 1, QUERY_ROWS)
    seg_key = jnp.where(flags > 0, segment, -1)
    seg_key = jnp.broadcast_to(seg_key[:, None], (length, 128))
    attn_low, attn_t, lse = attend(spot, seg_row, seg_key, qkv, wide, parts_length)

    sent = jnp.concatenate([attn_low] * repeats, axis=0) if repeats > 1 else attn_low
    got = lax.all_to_all(sent, ALL, split_axis=0, concat_axis=0, tiled=True)
    my_span = my_block * groups + my_group
    local_flags = lax.dynamic_slice_in_dim(valid_flags, my_span * span, span, 1)
    local_flags = local_flags.reshape(rows, 1).astype(F32)
    sent, normed_one, unit_one, inv_one, squares = join(
        spot, got, token_rows, local_flags, mat_out, short, seqs, heads_here, repeats
    )
    joint_parts = [sent[0]] + [swapped(sent[k], "heads", k) for k in range(1, groups)]
    normed_parts = [part[:, :width] for part in joint_parts]
    attn_parts = [part[:, width:] for part in joint_parts]
    hidden_parts = [matmul(part, mat_up) + vec_up for part in normed_parts]
    act_parts = [jax.nn.gelu(part, approximate=False).astype(BF16) for part in hidden_parts]
    ffn_parts = [matmul(part, mat_down) for part in act_parts]
    ffn = scatter_parts(ffn_parts, "heads") + vec_down
    normed_two, unit_two, inv_two = layer_norm(normed_one + ffn, gain_two, bias_two)
    output = normed_two.astype(BF16).reshape(tokens.shape)
    last = jnp.sum(local_flags * jnp.sum(ffn * ffn, axis=1, keepdims=True))
    squares = squares + jnp.where(jnp.arange(128) == 3, last, 0.0)[None]

    upstream = cotangent.reshape(rows, width).astype(F32)
    grad_gain_two = jnp.sum(upstream * unit_two, axis=0)
    grad_bias_two = jnp.sum(upstream, axis=0)
    grad_resid_two = norm_back(upstream, unit_two, inv_two, gain_two)
    grad_ffn = grad_resid_two.astype(BF16)
    grad_vec_down = jnp.sum(grad_ffn.astype(F32), axis=0)
    grad_ffn_parts = gather_parts(grad_ffn, "heads")
    grad_hidden_parts = [
        (matmul_nt(part, mat_down) * gelu_slope(hidden)).astype(BF16)
        for part, hidden in zip(grad_ffn_parts, hidden_parts)
    ]
    grad_normed_parts = [matmul_nt(part, mat_up) for part in grad_hidden_parts]
    grad_normed_others = [
        swapped(grad_normed_parts[k].astype(BF16), "heads", k) for k in range(1, groups)
    ]
    grad_ffn_all = jnp.concatenate(grad_ffn_parts, axis=0)
    grad_hidden = jnp.concatenate(grad_hidden_parts, axis=0)
    grad_vec_up = jnp.sum(grad_hidden.astype(F32), axis=0)
    act_low = jnp.concatenate(act_parts, axis=0)
    normed_all = jnp.concatenate(normed_parts, axis=0)
    grad_mat_down = matmul_tn(act_low, grad_ffn_all).astype(BF16)
    grad_mat_up = matmul_tn(normed_all, grad_hidden).astype(BF16)
    ffn_grads = jnp.concatenate(
        [
            grad_mat_down.reshape(blocks, unit_rows, width),
            grad_mat_up.reshape(blocks, -1, width),
        ],
        axis=1,
    )
    ffn_grads = lax.psum_scatter(
        ffn_grads.reshape(-1, width), "blk", scatter_dimension=0, tiled=True
    )
    shard_down = ffn_grads[:unit_rows].astype(F32)
    shard_up = lax.all_to_all(
        ffn_grads[unit_rows:].reshape(groups, dim_rows, units_here),
        "heads",
        split_axis=0,
        concat_axis=0,
        tiled=True,
    )
    shard_up = jnp.transpose(
        shard_up.reshape(groups, dim_rows, blocks, unit_rows), (1, 2, 0, 3)
    ).reshape(dim_rows, hidden_size)
    shard_up = shard_up.astype(F32)

    sent, grad_resid_one, grad_branch = branch_back(
        spot, grad_normed_parts[0], grad_normed_others, grad_resid_two, unit_one, inv_one,
        gain_one[None], mat_out, jnp.stack([grad_vec_down, grad_gain_two, grad_bias_two]),
        grad_vec_up[None], squares, seqs, heads_here, repeats, devices,
    )
    got = lax.all_to_all(sent, ALL, split_axis=0, concat_axis=0, tiled=True)
    small = jnp.sum(got[:, wide:].astype(F32), axis=0)
    small = small[:8] + small[8:]
    vector_sums = lax.dynamic_slice_in_dim(small[:6], my_span * dim_rows % 128, dim_rows, 1)
    shard_vec_up = lax.dynamic_slice_in_dim(small[6], my_block * unit_rows % 128, unit_rows, 0)
    real_count = jnp.maximum(jnp.sum(valid_flags.astype(F32)), 1.0)
    rms = jnp.sqrt(small[7, :4] / (real_count * width))

    branch_parts = gather_parts(grad_branch, "heads")
    grad_mat_out = matmul_tn(
        jnp.concatenate(attn_parts, axis=0), jnp.concatenate(branch_parts, axis=0)
    ).astype(BF16)
    shard_out = scatter_blk(grad_mat_out.reshape(blocks, dim_rows, width)).astype(BF16)
    route = [(j, j % groups * blocks + j // groups) for j in range(devices)]
    shard_out = lax.ppermute(shard_out, ("heads", "blk"), route)
    grads = attend_back(spot, seg_row, seg_key, qkv, got, attn_t, lse)
    got = lax.all_to_all(grads, "blk", split_axis=0, concat_axis=0, tiled=True)
    got = after(got, shard_out)
    own_input, other_input, keep, send = input_grads(
        spot, got, mat_three, token_all, heads_here, groups, repeats
    )
    grad_input = grad_resid_one + own_input
    for k in range(1, groups):
        grad_input = grad_input + swapped(other_input[k - 1], "heads", k).astype(F32)
    grad_input = grad_input.reshape(tokens.shape)
    chip_sums = keep + swapped(send, "blk", 1).astype(F32)
    chip_low = chip_sums.astype(BF16)
    three_grads = chip_sums[0]
    for k in range(1, blocks // 2):
        three_grads = three_grads + swapped(chip_low[k], "blk", 2 * k).astype(F32)
    own_rows = three_grads[: groups * dim_rows].reshape(groups, dim_rows, 3 * width_here)
    own_sums = three_grads[groups * dim_rows, :256].reshape(2, 128)[:, : groups * dim_rows]
    own_sums = jnp.transpose(own_sums.reshape(2, groups, dim_rows), (1, 0, 2))
    row = lax.broadcasted_iota(jnp.int32, (1, 16, 1), 1)
    own_sums = jnp.concatenate(
        [
            own_sums.reshape(groups, 2 * dim_rows),
            jnp.zeros((groups, 3 * width_here - 2 * dim_rows), F32),
        ],
        axis=1,
    )
    own_sums = jnp.where(row == 0, own_sums[:, None, :], 0.0)
    own = jnp.concatenate([own_rows, own_sums], axis=1).astype(BF16)
    own = after(own, shard_up)
    own = lax.all_to_all(own, "heads", split_axis=0, concat_axis=0, tiled=True).astype(F32)
    shard_sums = jnp.sum(own[:, dim_rows, : 2 * dim_rows], axis=0)
    shards_three = [
        jnp.transpose(
            own[:, :dim_rows, which * width_here : (which + 1) * width_here], (1, 0, 2)
        ).reshape(dim_rows, width)
        for which in range(3)
    ]

    return (
        output,
        grad_input,
        shards_three[0],
        shards_three[1],
        shards_three[2],
        shard_out.astype(F32),
        shard_up,
        shard_down,
        shard_sums[:dim_rows],
        shard_sums[dim_rows:],
        vector_sums[0],
        shard_vec_up,
        vector_sums[3],
        vector_sums[1],
        vector_sums[2],
        vector_sums[4],
        vector_sums[5],
        rms,
    )


def solution(mesh):
    token_spec = P(None, ALL, None)
    matrix_spec = P(ALL, None)
    vector_spec = P(ALL)
    return jax.shard_map(
        per_device,
        mesh=mesh,
        in_specs=(token_spec,) * 2 + (P(),) * 2 + (matrix_spec,) * 6 + (vector_spec,) * 9,
        out_specs=(token_spec,) * 2 + (matrix_spec,) * 6 + (vector_spec,) * 9 + (P(),),
        check_vma=False,
    )
```

```python
import functools

import jax
import jax.numpy as jnp
from jax import lax
from jax.experimental import pallas as pl
from jax.experimental.pallas import tpu as pltpu
from jax.sharding import PartitionSpec as P

HEAD_DIM = 64
NORM_EPS = 1e-05
NEG_LARGE = -1e30
QUERY_ROWS = 256
BF16 = jnp.bfloat16
F32 = jnp.float32
ALL = ("blk", "heads")


def vmem_limit(length):
    return 8 * 1024 * 1024 + 6 * 1024 * length


def matmul(left, right):
    return jnp.dot(left, right, preferred_element_type=F32)


def matmul_tn(left, right):
    return lax.dot_general(left, right, (((0,), (0,)), ((), ())), preferred_element_type=F32)


def matmul_nt(left, right):
    return lax.dot_general(left, right, (((1,), (1,)), ((), ())), preferred_element_type=F32)


def after(block, other):
    spot = lax.slice(other, (0,) * other.ndim, (1,) * other.ndim).reshape(())
    return block + (spot * 0).astype(block.dtype)


def swapped(block, axis, mask):
    count = lax.axis_size(axis)
    return lax.ppermute(block, axis, [(i, i ^ mask) for i in range(count)])


def gather_parts(block, axis):
    return [block] + [swapped(block, axis, k) for k in range(1, lax.axis_size(axis))]


def scatter_parts(parts, axis):
    total = parts[0].astype(F32)
    for k in range(1, len(parts)):
        total = total + swapped(parts[k].astype(BF16), axis, k).astype(F32)
    return total


def xor_order(array, dim, index):
    pieces = [
        lax.dynamic_index_in_dim(array, index ^ k, dim, True) for k in range(array.shape[dim])
    ]
    return jnp.concatenate(pieces, axis=dim)


def gather_blk_parts(block, first_needs):
    count = lax.axis_size("blk")
    mine = jnp.stack([block] + [swapped(block, "blk", k) for k in range(2, count, 2)])
    mine = after(mine, first_needs)
    return mine, swapped(mine, "blk", 1)


def gather_blk(block, first_needs):
    mine, other = gather_blk_parts(block, first_needs)
    both = jnp.stack([mine, other], axis=1).reshape((-1,) + block.shape)
    return xor_order(both, 0, lax.axis_index("blk"))


def scatter_blk(blocks):
    index = lax.axis_index("blk")
    ordered = xor_order(blocks, 0, index)
    pairs = ordered.reshape((ordered.shape[0] // 2, 2) + ordered.shape[1:])
    total = pairs[:, 0].astype(F32) + swapped(pairs[:, 1], "blk", 1).astype(F32)
    low = total.astype(BF16)
    result = total[0]
    for k in range(1, low.shape[0]):
        result = result + swapped(low[k], "blk", 2 * k).astype(F32)
    return result


def layer_norm(resid, norm_gain, norm_bias):
    center = resid - jnp.mean(resid, axis=-1, keepdims=True)
    inv_std = lax.rsqrt(jnp.mean(center * center, axis=-1, keepdims=True) + NORM_EPS)
    normed = center * inv_std
    return (normed * norm_gain + norm_bias, normed, inv_std)


def norm_back(upstream, normed, inv_std, norm_gain):
    scaled = upstream * norm_gain
    return inv_std * (
        scaled
        - jnp.mean(scaled, axis=-1, keepdims=True)
        - normed * jnp.mean(scaled * normed, axis=-1, keepdims=True)
    )


def gelu_slope(hidden):
    cdf_part = 0.5 * (1.0 + lax.erf(hidden * 0.7071067811865476))
    pdf_part = jnp.exp(-0.5 * hidden * hidden) * 0.3989422804014327
    return cdf_part + hidden * pdf_part


def two_halves(values):
    high = lax.reduce_precision(values, 8, 7)
    return jnp.stack([high, values - high], axis=-1).astype(BF16)


def left_lanes(block):
    lane = lax.broadcasted_iota(jnp.int32, block.shape, 1)
    return jnp.where(lane < HEAD_DIM, block, 0.0)


def masked_scores(seg_key, seg_query, scores):
    width = scores.shape[1] // seg_key.shape[1]
    same = jnp.concatenate([seg_key] * width, axis=1) == seg_query
    return jnp.where(same, scores, NEG_LARGE)


def own_scores(seg_key, seg_query, scores):
    width = scores.shape[1] // seg_key.shape[1]
    same = jnp.concatenate([seg_key] * width, axis=1) == seg_query
    rows = lax.broadcasted_iota(jnp.int32, scores.shape, 0)
    columns = lax.broadcasted_iota(jnp.int32, scores.shape, 1)
    return jnp.where(same | (rows == columns), scores, NEG_LARGE)


def score_all(turn, seg_query, seg_key_ref, qkv_ref, query_t, scores):
    sources, rows = qkv_ref.shape[0], qkv_ref.shape[1] * 2 // 3
    per_source = rows // QUERY_ROWS
    query_now = query_t[turn]
    for b in range(sources):
        spot = slice(b * rows, (b + 1) * rows)
        scores[spot, :] = masked_scores(
            seg_key_ref[spot, :], seg_query, matmul(qkv_ref[b, 0:rows, :], query_now)
        )
    own = pl.ds(pl.multiple_of(turn * QUERY_ROWS, QUERY_ROWS), QUERY_ROWS)
    inner = pl.ds(pl.multiple_of(turn % per_source * QUERY_ROWS, QUERY_ROWS), QUERY_ROWS)
    own_pair = qkv_ref[turn // per_source, inner, :]
    scores[own, :] = own_scores(seg_key_ref[own, :], seg_query, matmul(own_pair, query_now))
    return own, own_pair


def turn_queries(b, turned, query_t):
    per_source = turned.shape[1] // QUERY_ROWS
    low = jnp.concatenate([jnp.zeros_like(turned[0:HEAD_DIM]), turned[0:HEAD_DIM]], axis=0)
    for t in range(per_source):
        spot = slice(t * QUERY_ROWS, (t + 1) * QUERY_ROWS)
        query_t[b * per_source + t] = low[:, spot].astype(BF16)


def attend_kernel(
    spot_ref, seg_row_ref, seg_key_ref, qkv_ref, low_ref, attn_ref, lse_ref,
    query_t, values_t, scores,
):
    step = pl.program_id(0)
    sources, rows = qkv_ref.shape[0], qkv_ref.shape[1] * 2 // 3
    half = rows // 2

    @pl.when(step == 0)
    def _():
        for b in range(sources):
            turn_queries(b, qkv_ref[b, 0:rows, :].astype(F32).T, query_t)
            turned = qkv_ref[b, rows : rows + half, :].astype(F32).T
            values_t[:, b * rows : b * rows + half] = turned[0:HEAD_DIM].astype(BF16)
            values_t[:, b * rows + half : (b + 1) * rows] = turned[
                HEAD_DIM : 2 * HEAD_DIM
            ].astype(BF16)

    turn = spot_ref[2] + step
    score_all(turn, seg_row_ref[0], seg_key_ref, qkv_ref, query_t, scores)
    top = jnp.max(scores[...], axis=0, keepdims=True)
    total = jnp.zeros_like(top)
    result = jnp.zeros((HEAD_DIM, QUERY_ROWS), F32)
    for b in range(sources):
        spot = slice(b * rows, (b + 1) * rows)
        probs = jnp.exp(scores[spot, :] - top)
        total = total + jnp.sum(probs, axis=0, keepdims=True)
        result = result + matmul(values_t[:, spot], probs.astype(BF16))
    result = result / total
    attn_ref[...] = result
    lse_ref[0] = top + jnp.log(total)
    turned = result.T
    wide = low_ref.shape[1]
    spans = QUERY_ROWS // (2 * wide)
    first = turn % (rows // QUERY_ROWS) * spans
    for t in range(spans):
        left = turned[2 * t * wide : (2 * t + 1) * wide]
        right = turned[(2 * t + 1) * wide : (2 * t + 2) * wide]
        low_ref[spot_ref[1] ^ (first + t)] = jnp.concatenate([left, right], axis=1).astype(BF16)


def attend(spot, seg_row, seg_key, qkv, wide, query_length):
    sources, rows = qkv.shape[0], qkv.shape[1] * 2 // 3
    length = sources * rows
    steps = query_length // QUERY_ROWS
    spans = rows // (2 * wide)
    per_source = rows // QUERY_ROWS
    return pl.pallas_call(
        attend_kernel,
        grid_spec=pltpu.PrefetchScalarGridSpec(
            num_scalar_prefetch=1,
            grid=(steps,),
            in_specs=[
                pl.BlockSpec((1, 1, QUERY_ROWS), lambda i, spot: (spot[2] + i, 0, 0)),
                pl.BlockSpec(seg_key.shape, lambda i, spot: (0, 0)),
                pl.BlockSpec(qkv.shape, lambda i, spot: (0, 0, 0)),
            ],
            out_specs=[
                pl.BlockSpec((spans, wide, 128), lambda i, spot: (i // per_source, 0, 0)),
                pl.BlockSpec((HEAD_DIM, QUERY_ROWS), lambda i, spot: (0, i)),
                pl.BlockSpec((1, 1, QUERY_ROWS), lambda i, spot: (i, 0, 0)),
            ],
            scratch_shapes=[
                pltpu.VMEM((length // QUERY_ROWS, 128, QUERY_ROWS), BF16),
                pltpu.VMEM((HEAD_DIM, length), BF16),
                pltpu.VMEM((length, QUERY_ROWS), F32),
            ],
        ),
        out_shape=[
            jax.ShapeDtypeStruct((steps // per_source * spans, wide, 128), BF16),
            jax.ShapeDtypeStruct((HEAD_DIM, query_length), F32),
            jax.ShapeDtypeStruct((steps, 1, QUERY_ROWS), F32),
        ],
        compiler_params=pltpu.CompilerParams(vmem_limit_bytes=vmem_limit(length)),
    )(spot, seg_row, seg_key, qkv)


def attend_back_kernel(
    spot_ref, seg_row_ref, seg_key_ref, qkv_ref, up_ref, attn_ref, lse_ref, grads_ref,
    query_t, keys_t, values, scores, grad_query, grad_key, grad_value,
):
    step = pl.program_id(0)
    sources, rows = qkv_ref.shape[0], qkv_ref.shape[1] * 2 // 3
    half = rows // 2
    lane = lax.broadcasted_iota(jnp.int32, (rows, 128), 1)

    @pl.when(step == 0)
    def _():
        for b in range(sources):
            turned = qkv_ref[b, 0:rows, :].astype(F32).T
            turn_queries(b, turned, query_t)
            keys_t[:, b * rows : (b + 1) * rows] = turned[HEAD_DIM : 2 * HEAD_DIM].astype(BF16)
            packed = qkv_ref[b, rows : rows + half, :].astype(F32)
            values[b * rows : b * rows + half, :] = left_lanes(packed).astype(BF16)
            values[b * rows + half : (b + 1) * rows, :] = left_lanes(
                pltpu.roll(packed, HEAD_DIM, 1)
            ).astype(BF16)
        grad_query[...] = jnp.zeros_like(grad_query)
        grad_key[...] = jnp.zeros_like(grad_key)
        grad_value[...] = jnp.zeros_like(grad_value)

    turn = spot_ref[2] + step
    lse = lse_ref[0]
    pieces = []
    spans = QUERY_ROWS // (rows // up_ref.shape[0])
    first = turn % (rows // QUERY_ROWS) * spans
    for t in range(spans):
        packed = up_ref[spot_ref[1] ^ (first + t), 0 : rows // up_ref.shape[0] // 2, :].astype(F32)
        pieces.append(left_lanes(packed))
        pieces.append(left_lanes(pltpu.roll(packed, HEAD_DIM, 1)))
    up_now = jnp.concatenate(pieces, axis=0)
    up_turned = up_now.T
    delta = jnp.sum(up_turned[0:HEAD_DIM] * attn_ref[...], axis=0, keepdims=True)
    up_now = up_now.astype(BF16)
    up_turned = up_turned.astype(BF16)
    own, own_pair = score_all(turn, seg_row_ref[0], seg_key_ref, qkv_ref, query_t, scores)
    query_now = pltpu.roll(own_pair.astype(F32), HEAD_DIM, 1).astype(BF16)
    result = jnp.zeros((HEAD_DIM, QUERY_ROWS), F32)
    for b in range(sources):
        spot = slice(b * rows, (b + 1) * rows)
        probs = jnp.exp(scores[spot, :] - lse)
        grad_probs = matmul(values[spot, :], up_turned)
        grad_scores = (probs * (grad_probs - delta)).astype(BF16)
        grad_value[spot, :] += matmul(probs.astype(BF16), up_now)
        grad_key[spot, :] += matmul(grad_scores, query_now)
        result = result + matmul(keys_t[:, spot], grad_scores)
    grad_query[own, :] = jnp.concatenate([result, jnp.zeros_like(result)], axis=0).T

    @pl.when(step == pl.num_programs(0) - 1)
    def _():
        for b in range(sources):
            spot = slice(b * rows, (b + 1) * rows)
            grads_ref[b, 0:rows, :] = jnp.where(
                lane < HEAD_DIM, grad_query[spot, :], grad_key[spot, :]
            ).astype(BF16)
            upper = grad_value[b * rows : b * rows + half, :]
            lower = grad_value[b * rows + half : (b + 1) * rows, :]
            grads_ref[b, rows : rows + half, :] = (
                upper + pltpu.roll(lower, HEAD_DIM, 1)
            ).astype(BF16)


def attend_back(spot, seg_row, seg_key, qkv, upstream, attn_t, lse):
    sources, rows = qkv.shape[0], qkv.shape[1] * 2 // 3
    length = sources * rows
    steps = lse.shape[0]
    groups = upstream.shape[0] // sources
    per_source = rows // QUERY_ROWS
    return pl.pallas_call(
        attend_back_kernel,
        grid_spec=pltpu.PrefetchScalarGridSpec(
            num_scalar_prefetch=1,
            grid=(steps,),
            in_specs=[
                pl.BlockSpec((1, 1, QUERY_ROWS), lambda i, spot: (spot[2] + i, 0, 0)),
                pl.BlockSpec(seg_key.shape, lambda i, spot: (0, 0)),
                pl.BlockSpec(qkv.shape, lambda i, spot: (0, 0, 0)),
                pl.BlockSpec(
                    (groups,) + upstream.shape[1:],
                    lambda i, spot: ((spot[2] + i) // per_source, 0, 0),
                ),
                pl.BlockSpec((HEAD_DIM, QUERY_ROWS), lambda i, spot: (0, i)),
                pl.BlockSpec((1, 1, QUERY_ROWS), lambda i, spot: (i, 0, 0)),
            ],
            out_specs=pl.BlockSpec(qkv.shape, lambda i, spot: (0, 0, 0)),
            scratch_shapes=[
                pltpu.VMEM((length // QUERY_ROWS, 128, QUERY_ROWS), BF16),
                pltpu.VMEM((HEAD_DIM, length), BF16),
                pltpu.VMEM((length, 128), BF16),
                pltpu.VMEM((length, QUERY_ROWS), F32),
                pltpu.VMEM((length, 128), F32),
                pltpu.VMEM((length, 128), F32),
                pltpu.VMEM((length, 128), F32),
            ],
        ),
        out_shape=jax.ShapeDtypeStruct(qkv.shape, BF16),
        compiler_params=pltpu.CompilerParams(vmem_limit_bytes=vmem_limit(length)),
    )(spot, seg_row, seg_key, qkv, upstream, attn_t, lse)


def left_pair(first, second):
    lane = lax.broadcasted_iota(jnp.int32, first.shape, 1)
    return jnp.where(lane < HEAD_DIM, first, pltpu.roll(second, HEAD_DIM, 1))


def right_pair(first, second):
    lane = lax.broadcasted_iota(jnp.int32, first.shape, 1)
    return jnp.where(lane < HEAD_DIM, pltpu.roll(first, HEAD_DIM, 1), second)


def join_kernel(
    seqs, heads_here, repeats, spot_ref, got_ref, tokens_ref, flags_ref, mat_ref, vectors_ref,
    *refs,
):
    sents, (normed_ref, unit_ref, inv_ref, squares_ref, attn) = refs[:-5], refs[-5:]
    my_group, part = spot_ref[1], spot_ref[3]
    groups = len(sents)
    wide = got_ref.shape[1]
    width = tokens_ref.shape[1]
    width_here = heads_here * HEAD_DIM
    for which in range(seqs):
        for group in range(groups):
            for head in range(0, heads_here, 2):
                first, second = [
                    got_ref[
                        ((which * heads_here + i) * repeats + part) * groups + group
                    ].astype(F32)
                    for i in (head, head + 1)
                ]
                start = group * width_here + head * HEAD_DIM
                top = 2 * which * wide
                attn[top : top + wide, start : start + 128] = left_pair(first, second).astype(BF16)
                attn[top + wide : top + 2 * wide, start : start + 128] = right_pair(
                    first, second
                ).astype(BF16)
    branch = matmul(attn[...], mat_ref[...]) + vectors_ref[0:1, :]
    resid_in = tokens_ref[...].astype(F32)
    normed, unit, inv_std = layer_norm(resid_in + branch, vectors_ref[2:3, :], vectors_ref[3:4, :])
    normed_ref[...] = normed
    unit_ref[...] = unit
    inv_ref[...] = jnp.broadcast_to(inv_std, inv_ref.shape)
    low = normed.astype(BF16)
    for k in range(groups):
        sents[k][:, 0:width] = low
        for group in range(groups):

            @pl.when((my_group ^ k) == group)
            def _():
                sents[k][:, width:] = attn[:, group * width_here : (group + 1) * width_here]

    lane = lax.broadcasted_iota(jnp.int32, squares_ref.shape, 1)
    total = jnp.zeros(squares_ref.shape, F32)
    for i, item in enumerate((resid_in, branch, normed)):
        size = flags_ref[...] * jnp.sum(item * item, axis=1, keepdims=True)
        total = total + jnp.where(lane == i, jnp.sum(size, axis=0, keepdims=True), 0.0)
    squares_ref[...] = total


def join(spot, got, tokens, flags, mat_out, vectors, seqs, heads_here, repeats):
    groups = tokens.shape[1] // (heads_here * HEAD_DIM)
    rows, width = tokens.shape
    vmem = pl.BlockSpec(memory_space=pltpu.VMEM)
    return pl.pallas_call(
        functools.partial(join_kernel, seqs, heads_here, repeats),
        in_specs=[pl.BlockSpec(memory_space=pltpu.SMEM)] + [vmem] * 5,
        out_specs=[vmem] * (groups + 4),
        out_shape=[jax.ShapeDtypeStruct((rows, width + heads_here * HEAD_DIM), BF16)] * groups
        + [
            jax.ShapeDtypeStruct((rows, width), F32),
            jax.ShapeDtypeStruct((rows, width), F32),
            jax.ShapeDtypeStruct((rows, 128), F32),
            jax.ShapeDtypeStruct((1, 128), F32),
        ],
        scratch_shapes=[pltpu.VMEM((rows, width), BF16)],
        compiler_params=pltpu.CompilerParams(vmem_limit_bytes=32 * 1024 * 1024),
    )(spot, got, tokens, flags, mat_out, vectors)


def middle_kernel(others, *refs):
    own_ref, normed_ref, vectors_ref, flags_ref, up_ref, squares_ref = refs[:6]
    parts = refs[6 : 6 + others]
    out_ref, resid_ref, low_ref, early_ref, total_ref = refs[6 + others :]
    ffn = own_ref[...]
    for part in parts:
        ffn = ffn + part[...].astype(F32)
    ffn = ffn + vectors_ref[1:2, :]
    gain = vectors_ref[4:5, :]
    normed, unit, inv_std = layer_norm(normed_ref[...] + ffn, gain, vectors_ref[5:6, :])
    out_ref[...] = normed.astype(BF16)
    upstream = up_ref[...].astype(F32)
    grad_resid = norm_back(upstream, unit, inv_std, gain)
    resid_ref[...] = grad_resid
    low = grad_resid.astype(BF16)
    low_ref[...] = low
    early_ref[0:1, :] = jnp.sum(low.astype(F32), axis=0, keepdims=True)
    early_ref[1:2, :] = jnp.sum(upstream * unit, axis=0, keepdims=True)
    early_ref[2:3, :] = jnp.sum(upstream, axis=0, keepdims=True)
    size = flags_ref[...] * jnp.sum(ffn * ffn, axis=1, keepdims=True)
    lane = lax.broadcasted_iota(jnp.int32, total_ref.shape, 1)
    total_ref[...] = squares_ref[...] + jnp.where(
        lane == 3, jnp.sum(size, axis=0, keepdims=True), 0.0
    )


def middle(own, others, normed, vectors, flags, upstream, squares):
    rows, width = own.shape
    return whole_call(
        functools.partial(middle_kernel, len(others)),
        [
            jax.ShapeDtypeStruct((rows, width), BF16),
            jax.ShapeDtypeStruct((rows, width), F32),
            jax.ShapeDtypeStruct((rows, width), BF16),
            jax.ShapeDtypeStruct((8, width), F32),
            jax.ShapeDtypeStruct((1, 128), F32),
        ],
        (own, normed, vectors, flags, upstream, squares, *others),
    )


def branch_back_kernel(
    seqs, heads_here, repeats, spot_ref, *refs,
):
    (own_ref, resid_ref, unit_ref, inv_ref, gain_ref, mat_ref, early_ref, up_sums_ref,
     squares_ref), others, (sent_ref, grad_ref, low_ref) = refs[:9], refs[9:-3], refs[-3:]
    my_group = spot_ref[1]
    groups = len(others) + 1
    rows, width = own_ref.shape
    span = rows // seqs
    wide = span // 2
    devices = sent_ref.shape[0]
    blocks = devices // groups
    grad_normed = own_ref[...]
    for other in others:
        grad_normed = grad_normed + other[...].astype(F32)
    grad_normed = grad_normed + resid_ref[...]
    unit = unit_ref[...]
    grad_resid = norm_back(grad_normed, unit, inv_ref[:, 0:1], gain_ref[...])
    grad_ref[...] = grad_resid
    low = grad_resid.astype(BF16)
    low_ref[...] = low
    grad_attn = matmul_nt(low, mat_ref[...])
    for which in range(seqs):
        top = which * span
        for group in range(groups):
            for head in range(0, heads_here, 2):
                start = (group * heads_here + head) * HEAD_DIM
                upper = grad_attn[top : top + wide, start : start + 128]
                lower = grad_attn[top + wide : top + span, start : start + 128]
                blocks_two = (left_pair(upper, lower), right_pair(upper, lower))
                for i in range(2):
                    for copy in range(repeats):
                        pair = which * heads_here + head + i
                        place = (pair * repeats + copy) * groups + group
                        sent_ref[place, 0:wide, :] = blocks_two[i].astype(BF16)
    sums = [
        jnp.sum(low.astype(F32), axis=0, keepdims=True),
        jnp.sum(grad_normed * unit, axis=0, keepdims=True),
        jnp.sum(grad_normed, axis=0, keepdims=True),
    ] + [early_ref[i : i + 1, :] for i in range(3)]
    row = lax.broadcasted_iota(jnp.int32, (8, 128), 0)
    dim_rows = width // devices
    unit_rows = up_sums_ref.shape[1] // blocks
    for tile in range(width // 128):
        base = jnp.where(row == 7, squares_ref[...], 0.0)
        for i in range(6):
            base = base + jnp.where(row == i, sums[i][:, tile * 128 : (tile + 1) * 128], 0.0)
        for place in range(tile * 128 // dim_rows, (tile + 1) * 128 // dim_rows):
            start = place // groups * unit_rows // 128 * 128
            mine = jnp.where(my_group == place % groups, up_sums_ref[:, start : start + 128], 0.0)
            block = base + jnp.where(row == 6, mine, 0.0)
            high = block.astype(BF16)
            rest = block - high.astype(F32)
            sent_ref[place, wide : wide + 16, :] = jnp.concatenate(
                [high.astype(F32), rest], axis=0
            ).astype(BF16)


def branch_back(spot, own, others, resid, unit, inv_std, gain, mat_out, early, up_sums, squares,
                seqs, heads_here, repeats, devices):
    rows, width = own.shape
    vmem = pl.BlockSpec(memory_space=pltpu.VMEM)
    return pl.pallas_call(
        functools.partial(branch_back_kernel, seqs, heads_here, repeats),
        in_specs=[pl.BlockSpec(memory_space=pltpu.SMEM)] + [vmem] * (9 + len(others)),
        out_specs=[vmem] * 3,
        out_shape=[
            jax.ShapeDtypeStruct((devices, rows // seqs // 2 + 16, 128), BF16),
            jax.ShapeDtypeStruct((rows, width), F32),
            jax.ShapeDtypeStruct((rows, width), BF16),
        ],
        compiler_params=pltpu.CompilerParams(vmem_limit_bytes=32 * 1024 * 1024),
    )(spot, own, resid, unit, inv_std, gain, mat_out, early, up_sums, squares, *others)


def pack_kernel(*refs):
    out_ref = refs[-1]
    rows = [jnp.zeros((1, 128), F32) for _ in range(out_ref.shape[0])]
    start = 0
    for ref in refs[:-1]:
        size = ref.shape[1]
        pieces = [ref[...].astype(F32)]
        if start % 128:
            pieces = [jnp.zeros((1, start % 128), F32)] + pieces
        if start % 128 + size < 128:
            pieces = pieces + [jnp.zeros((1, 128 - start % 128 - size), F32)]
        piece = jnp.concatenate(pieces, axis=1) if len(pieces) > 1 else pieces[0]
        rows[start // 128] = rows[start // 128] + piece
        start += size
    out_ref[...] = jnp.concatenate(rows, axis=0).astype(BF16)


def project_kernel(groups, heads_here, repeats, spot_ref, *refs):
    tokens, (mine_ref, other_ref, sent_ref, all_ref, mat_ref, short_ref, values) = (
        refs[:groups], refs[groups:]
    )
    my_block, my_group = spot_ref[0], spot_ref[1]
    halves, chip_rows, _ = mine_ref.shape
    blocks = 2 * halves
    dim_rows = chip_rows // groups
    rows, width = tokens[0].shape
    width_here = heads_here * HEAD_DIM
    seqs = sent_ref.shape[0] // (repeats * heads_here)
    span = rows // seqs
    block_rows = span * groups
    for k in range(groups):
        all_ref[k * rows : (k + 1) * rows, :] = tokens[k][...]
    for b in range(blocks):
        place = my_block ^ b
        spot = slice(b * chip_rows, (b + 1) * chip_rows)

        @pl.when(place % 2 == 0)
        def _():
            mat_ref[spot, :] = mine_ref[place // 2, :, 0 : 3 * width_here]

        @pl.when(place % 2 == 1)
        def _():
            mat_ref[spot, :] = other_ref[place // 2, :, 0 : 3 * width_here]

    for b in range(blocks):
        place = my_block ^ b
        vectors = jnp.where(
            place % 2 == 0,
            mine_ref[place // 2, :, 3 * width_here :].astype(F32),
            other_ref[place // 2, :, 3 * width_here :].astype(F32),
        )
        for group in range(groups):
            short_ref[b * groups + group] = vectors[group * dim_rows : group * dim_rows + 8]
    lane = lax.broadcasted_iota(jnp.int32, (1, 128), 1)
    tiles = width_here // 128
    biases = [[jnp.zeros((1, 128), F32) for _ in range(tiles)] for _ in range(2)]
    for t in range(blocks):
        place = my_block ^ (my_group * (blocks // groups) + t // groups)
        piece = jnp.where(
            place % 2 == 0,
            mine_ref[place // 2, :, 3 * width_here :].astype(F32),
            other_ref[place // 2, :, 3 * width_here :].astype(F32),
        )
        piece = piece[t % groups * dim_rows : t % groups * dim_rows + 1]
        tile, start = t * dim_rows // 128, t * dim_rows % 128
        inside = (lane >= start) & (lane < start + dim_rows)
        for which in range(2):
            shift = (start - which * dim_rows) % 128
            moved = pltpu.roll(piece, shift, 1) if shift else piece
            biases[which][tile] = biases[which][tile] + jnp.where(inside, moved, 0.0)
    query_bias, value_bias = [jnp.concatenate(item, axis=1) for item in biases]
    result = matmul(all_ref[...], mat_ref[...])
    query = (result[:, :width_here] + query_bias) * HEAD_DIM ** (-0.5)
    key = result[:, width_here : 2 * width_here]
    values[...] = result[:, 2 * width_here :] + value_bias
    half_parts = groups // 2
    for pair in range(seqs * heads_here):
        which, head = pair // heads_here, pair % heads_here
        columns = slice(head * HEAD_DIM, (head + 1) * HEAD_DIM)
        for k in range(groups):
            spot = slice(k * rows + which * span, k * rows + (which + 1) * span)
            block = jnp.concatenate([query[spot, columns], key[spot, columns]], axis=1)
            for copy in range(repeats):
                sent_ref[pair * repeats + copy, k * span : (k + 1) * span, :] = block.astype(BF16)
        for k in range(half_parts):
            upper = slice(k * rows + which * span, k * rows + (which + 1) * span)
            lower = slice(upper.start + half_parts * rows, upper.stop + half_parts * rows)
            block = jnp.concatenate([values[upper, columns], values[lower, columns]], axis=1)
            for copy in range(repeats):
                sent_ref[
                    pair * repeats + copy, block_rows + k * span : block_rows + (k + 1) * span, :
                ] = block.astype(BF16)


def project(spot, token_parts, mine, other, seqs, heads_here, repeats):
    groups = len(token_parts)
    rows, width = token_parts[0].shape
    blocks = seqs * heads_here * repeats
    block_rows = rows // seqs * groups
    vmem = pl.BlockSpec(memory_space=pltpu.VMEM)
    return pl.pallas_call(
        functools.partial(project_kernel, groups, heads_here, repeats),
        in_specs=[pl.BlockSpec(memory_space=pltpu.SMEM)] + [vmem] * (groups + 2),
        out_specs=[vmem] * 4,
        out_shape=[
            jax.ShapeDtypeStruct((blocks, block_rows * 3 // 2, 128), BF16),
            jax.ShapeDtypeStruct((groups * rows, width), BF16),
            jax.ShapeDtypeStruct((width, 3 * heads_here * HEAD_DIM), BF16),
            jax.ShapeDtypeStruct((blocks * groups, 8, 128), F32),
        ],
        scratch_shapes=[pltpu.VMEM((groups * rows, heads_here * HEAD_DIM), F32)],
        compiler_params=pltpu.CompilerParams(vmem_limit_bytes=40 * 1024 * 1024),
    )(spot, *token_parts, mine, other)


def input_kernel(
    groups, heads_here, repeats, spot_ref, got_ref, mat_ref, all_ref,
    own_ref, others_ref, keep_ref, send_ref, grads, mat_grads,
):
    my_block, my_group = spot_ref[0], spot_ref[1]
    blocks = got_ref.shape[0]
    seqs = blocks // (repeats * heads_here)
    rows = all_ref.shape[0] // groups
    span = rows // seqs
    block_rows = span * groups
    width_here = heads_here * HEAD_DIM
    chip_rows = keep_ref.shape[1] - 16
    half_parts = groups // 2

    def received(pair, start):
        spot = slice(start, start + span)
        total = got_ref[pair * repeats, spot, :].astype(F32)
        for copy in range(1, repeats):
            total = total + got_ref[pair * repeats + copy, spot, :].astype(F32)
        return total

    for which in range(seqs):
        for head in range(0, heads_here, 2):
            pair = which * heads_here + head
            start = head * HEAD_DIM
            for k in range(groups):
                spot = slice(k * rows + which * span, k * rows + (which + 1) * span)
                first, second = received(pair, k * span), received(pair + 1, k * span)
                grads[spot, start : start + 128] = (
                    left_pair(first, second) * HEAD_DIM ** (-0.5)
                ).astype(BF16)
                grads[spot, width_here + start : width_here + start + 128] = right_pair(
                    first, second
                ).astype(BF16)
                inner = block_rows + k % half_parts * span
                first, second = received(pair, inner), received(pair + 1, inner)
                grads[spot, 2 * width_here + start : 2 * width_here + start + 128] = (
                    left_pair(first, second) if k < half_parts else right_pair(first, second)
                ).astype(BF16)
    back = matmul_nt(grads[...], mat_ref[...])
    own_ref[...] = back[:rows]
    for k in range(1, groups):
        others_ref[k - 1] = back[k * rows : (k + 1) * rows].astype(BF16)
    mat_grads[...] = matmul_tn(all_ref[...], grads[...])
    query_sums = jnp.sum(grads[:, :width_here].astype(F32), axis=0, keepdims=True)
    value_sums = jnp.sum(grads[:, 2 * width_here :].astype(F32), axis=0, keepdims=True)
    chunks = blocks // groups
    chunk = width_here // chunks
    row = lax.broadcasted_iota(jnp.int32, (16, 128), 0)
    for k in range(blocks):
        owner = my_block ^ k
        spot = pl.ds(pl.multiple_of(owner * chip_rows, chip_rows), chip_rows)
        block = mat_grads[spot, :]
        sums = []
        for total in (query_sums, value_sums):
            chosen = jnp.zeros((1, chunk), F32)
            for i in range(chunks):
                piece = total[:, i * chunk : (i + 1) * chunk]
                chosen = chosen + jnp.where(owner == my_group * chunks + i, piece, 0.0)
            sums.append(jnp.concatenate([chosen, jnp.zeros((1, 128 - chunk), F32)], axis=1) if chunk < 128 else chosen)
        if k % 2 == 0:
            keep_ref[k // 2, 0:chip_rows, :] = block
        else:
            send_ref[k // 2, 0:chip_rows, :] = block.astype(BF16)
        for i in range(3 * width_here // 128):
            value = jnp.where(row == 0, sums[i], 0.0) if i < 2 else jnp.zeros((16, 128), F32)
            columns = slice(i * 128, (i + 1) * 128)
            if k % 2 == 0:
                keep_ref[k // 2, chip_rows : chip_rows + 16, columns] = value
            else:
                send_ref[k // 2, chip_rows : chip_rows + 16, columns] = value.astype(BF16)


def input_grads(spot, got, mat_three, token_all, heads_here, groups, repeats):
    blocks = got.shape[0]
    total_rows, width = token_all.shape
    rows = total_rows // groups
    chip_rows = width // blocks
    columns = mat_three.shape[1]
    vmem = pl.BlockSpec(memory_space=pltpu.VMEM)
    shape = (blocks // 2, chip_rows + 16, columns)
    return pl.pallas_call(
        functools.partial(input_kernel, groups, heads_here, repeats),
        in_specs=[pl.BlockSpec(memory_space=pltpu.SMEM)] + [vmem] * 3,
        out_specs=[vmem] * 4,
        out_shape=[
            jax.ShapeDtypeStruct((rows, width), F32),
            jax.ShapeDtypeStruct((groups - 1, rows, width), BF16),
            jax.ShapeDtypeStruct(shape, F32),
            jax.ShapeDtypeStruct(shape, BF16),
        ],
        scratch_shapes=[
            pltpu.VMEM((total_rows, columns), BF16),
            pltpu.VMEM((width, columns), F32),
        ],
        compiler_params=pltpu.CompilerParams(vmem_limit_bytes=40 * 1024 * 1024),
    )(spot, got, mat_three, token_all)


def whole_call(kernel, out_shape, arguments, scratch=(), megabytes=40):
    vmem = pl.BlockSpec(memory_space=pltpu.VMEM)
    return pl.pallas_call(
        kernel,
        in_specs=[vmem] * len(arguments),
        out_specs=[vmem] * len(out_shape),
        out_shape=out_shape,
        scratch_shapes=list(scratch),
        compiler_params=pltpu.CompilerParams(vmem_limit_bytes=megabytes * 1024 * 1024),
    )(*arguments)


def ffn_kernel(sent_ref, up_ref, down_ref, bias_ref, out_ref, act_ref, slope_ref):
    hidden = matmul(sent_ref[:, : up_ref.shape[0]], up_ref[...]) + bias_ref[...]
    cdf_part = 0.5 * (1.0 + lax.erf(hidden * 0.7071067811865476))
    act = (hidden * cdf_part).astype(BF16)
    act_ref[...] = act
    slope_ref[...] = cdf_part + hidden * (
        jnp.exp(-0.5 * hidden * hidden) * 0.3989422804014327
    )
    out_ref[...] = matmul(act, down_ref[...]).astype(out_ref.dtype)


def ffn_part(sent, mat_up, mat_down, vec_up, kind):
    rows = sent.shape[0]
    units, width = mat_down.shape
    return whole_call(
        ffn_kernel,
        [
            jax.ShapeDtypeStruct((rows, width), kind),
            jax.ShapeDtypeStruct((rows, units), BF16),
            jax.ShapeDtypeStruct((rows, units), F32),
        ],
        (sent, mat_up, mat_down, vec_up),
    )


def ffn_back_kernel(grad_ref, slope_ref, up_ref, down_ref, out_ref, hidden_ref):
    grad_hidden = (matmul_nt(grad_ref[...], down_ref[...]) * slope_ref[...]).astype(BF16)
    hidden_ref[...] = grad_hidden
    out_ref[...] = matmul_nt(grad_hidden, up_ref[...]).astype(out_ref.dtype)


def ffn_back_part(grad, slope, mat_up, mat_down, kind):
    rows, width = grad.shape
    return whole_call(
        ffn_back_kernel,
        [
            jax.ShapeDtypeStruct((rows, width), kind),
            jax.ShapeDtypeStruct(slope.shape, BF16),
        ],
        (grad, slope, mat_up, mat_down),
    )


def ffn_grads_kernel(groups, blocks, *refs):
    acts, grads, sents, hiddens = [refs[i * groups : (i + 1) * groups] for i in range(4)]
    *outs, sums_ref, left, right = refs[4 * groups :]
    rows, width = grads[0].shape
    units = acts[0].shape[1]
    for k in range(groups):
        spot = slice(k * rows, (k + 1) * rows)
        left[spot, 0:units] = acts[k][...]
        right[spot, 0:width] = grads[k][...]
    result = matmul_tn(left[:, 0:units], right[:, 0:width])
    chunk = units // blocks
    for b in range(blocks):
        outs[0][b, 0:chunk, :] = result[b * chunk : (b + 1) * chunk].astype(BF16)
    for k in range(groups):
        spot = slice(k * rows, (k + 1) * rows)
        left[spot, 0:width] = sents[k][:, 0:width]
        right[spot, 0:units] = hiddens[k][...]
    result = matmul_tn(left[:, 0:width], right[:, 0:units])
    chunk = width // blocks
    for b in range(blocks):
        block = result[b * chunk : (b + 1) * chunk].astype(BF16)
        if len(outs) == 1:
            outs[0][b, units // blocks :, :] = block
        else:
            outs[1][b] = block
    sums_ref[...] = jnp.sum(right[:, 0:units].astype(F32), axis=0, keepdims=True)


def ffn_grads_call(acts, grads, sents, hiddens, blocks):
    groups = len(acts)
    rows, width = grads[0].shape
    units = acts[0].shape[1]
    big = pltpu.VMEM((groups * rows, max(units, width)), BF16)
    if units == width:
        shapes = [jax.ShapeDtypeStruct((blocks, (units + width) // blocks, width), BF16)]
    else:
        shapes = [
            jax.ShapeDtypeStruct((blocks, units // blocks, width), BF16),
            jax.ShapeDtypeStruct((blocks, width // blocks, units), BF16),
        ]
    return whole_call(
        functools.partial(ffn_grads_kernel, groups, blocks),
        shapes + [jax.ShapeDtypeStruct((1, units), F32)],
        (*acts, *grads, *sents, *hiddens),
        (big, big),
    )


def split_kernel(own_ref, *outs):
    groups = own_ref.shape[0]
    dim_rows = outs[0].shape[0]
    columns = own_ref.shape[2] // 3
    total = jnp.zeros(outs[3].shape, F32)
    for group in range(groups):
        block = own_ref[group].astype(F32)
        for which in range(3):
            outs[which][:, group * columns : (group + 1) * columns] = block[
                :dim_rows, which * columns : (which + 1) * columns
            ]
        total = total + block[dim_rows : dim_rows + 8, 0:128]
    outs[3][...] = total


def split_columns(own, dim_rows):
    groups, _, columns = own.shape
    matrix = jax.ShapeDtypeStruct((dim_rows, groups * columns // 3), F32)
    return whole_call(split_kernel, [matrix] * 3 + [jax.ShapeDtypeStruct((8, 128), F32)], (own,))


def place_kernel(groups, blocks, spot_ref, *refs):
    parts, out_ref = refs[:groups], refs[groups]
    chunk = parts[0].shape[1] // blocks
    for k in range(groups):
        for group in range(groups):

            @pl.when((spot_ref[1] ^ k) == group)
            def _():
                for b in range(blocks):
                    start = (b * groups + group) * chunk
                    out_ref[:, start : start + chunk] = parts[k][
                        :, b * chunk : (b + 1) * chunk
                    ].astype(F32)


def place_columns(spot, parts, blocks):
    groups = len(parts)
    rows, columns = parts[0].shape
    chunk = columns // blocks
    if chunk % 128:
        whole = xor_order(jnp.stack(parts), 0, spot[1]).reshape(groups, rows, blocks, chunk)
        return jnp.transpose(whole, (1, 2, 0, 3)).reshape(rows, groups * columns).astype(F32)
    vmem = pl.BlockSpec(memory_space=pltpu.VMEM)
    return pl.pallas_call(
        functools.partial(place_kernel, groups, blocks),
        in_specs=[pl.BlockSpec(memory_space=pltpu.SMEM)] + [vmem] * groups,
        out_specs=vmem,
        out_shape=jax.ShapeDtypeStruct((rows, groups * columns), F32),
    )(spot, *parts)


def out_grads_kernel(groups, *refs):
    sents, grads, (out_ref, left, right) = refs[:groups], refs[groups : 2 * groups], refs[2 * groups :]
    rows, width = grads[0].shape
    for k in range(groups):
        spot = slice(k * rows, (k + 1) * rows)
        left[spot, :] = sents[k][:, width:]
        right[spot, :] = grads[k][...]
    out_ref[...] = matmul_tn(left[...], right[...]).astype(BF16)


def out_grads_call(sents, grads):
    groups = len(sents)
    rows, width = grads[0].shape
    columns = sents[0].shape[1] - width
    return whole_call(
        functools.partial(out_grads_kernel, groups),
        [jax.ShapeDtypeStruct((columns, width), BF16)],
        (*sents, *grads),
        (
            pltpu.VMEM((groups * rows, columns), BF16),
            pltpu.VMEM((groups * rows, width), BF16),
        ),
    )[0]


def per_device(
    tokens,
    cotangent,
    doc_offsets,
    valid_flags,
    w_query,
    w_key,
    w_value,
    w_out,
    w_fc1,
    w_fc2,
    b_query,
    b_value,
    b_out,
    b_fc1,
    b_fc2,
    gain_attn,
    bias_attn,
    gain_ffn,
    bias_ffn,
):
    seqs, span, width = tokens.shape
    groups = lax.axis_size("heads")
    blocks = lax.axis_size("blk")
    devices = groups * blocks
    my_group = lax.axis_index("heads")
    my_block = lax.axis_index("blk")
    rows = seqs * span
    block_rows = span * groups
    length = block_rows * blocks
    heads = width // HEAD_DIM
    heads_here = heads // groups
    pairs = seqs * heads_here
    repeats = blocks // pairs
    parts_length = length // repeats
    width_here = heads_here * HEAD_DIM
    dim_rows = w_query.shape[0]
    unit_rows = w_fc2.shape[0]
    hidden_size = w_fc1.shape[1]
    units_here = hidden_size // groups
    qk_scale = HEAD_DIM ** (-0.5)
    half = block_rows // 2
    wide = span // 2

    token_rows = tokens.reshape(rows, width)
    token_parts = gather_parts(token_rows, "heads")
    w_three = jnp.concatenate(
        [w.reshape(dim_rows, groups, width_here) for w in (w_query, w_key, w_value)], axis=-1
    )
    w_three = jnp.transpose(w_three, (1, 0, 2))
    short = [b_query, b_value, b_out, b_fc2, gain_attn, bias_attn, gain_ffn, bias_ffn, b_fc1]
    vectors = whole_call(
        pack_kernel,
        [jax.ShapeDtypeStruct((dim_rows, 128), BF16)],
        [item[None] for item in short],
    )[0]
    w_up = w_fc1.reshape(dim_rows, blocks, groups, unit_rows)
    w_up = jnp.transpose(w_up, (2, 0, 1, 3)).reshape(groups, dim_rows, units_here)
    first = jnp.concatenate(
        [w_three, jnp.broadcast_to(vectors[None], (groups,) + vectors.shape), w_up], axis=-1
    )
    first = lax.all_to_all(first, "heads", split_axis=0, concat_axis=0, tiled=True)
    first = first.reshape(groups * dim_rows, first.shape[-1])
    second = first[:, 3 * width_here + 128 :].reshape(-1, width)
    second = jnp.concatenate([second, w_fc2])
    mat_out = lax.all_gather(w_out, ALL, axis=0, tiled=True)

    first = first[:, : 3 * width_here + 128]
    for part in token_parts[1:]:
        second = after(second, part)
    mine, other = gather_blk_parts(first, second)
    part_blocks = blocks // repeats
    first_turn = my_block % repeats * (parts_length // QUERY_ROWS)
    spot = jnp.stack([my_block, my_group, first_turn, my_block // part_blocks]).astype(jnp.int32)
    sent, token_all, mat_three, short = project(
        spot, token_parts, mine, other, seqs, heads_here, repeats
    )
    qkv = lax.all_to_all(sent, "blk", split_axis=0, concat_axis=0, tiled=True)


    vectors = short.reshape(devices, 8 * 128)
    vec_up = vectors[:, 8 * dim_rows : 8 * dim_rows + unit_rows].reshape(blocks, groups, unit_rows)
    vec_up = lax.dynamic_index_in_dim(vec_up, my_group, 1, False).reshape(units_here)
    short = vectors[:, 2 * dim_rows : 8 * dim_rows].reshape(devices, 6, dim_rows)
    short = jnp.transpose(short, (1, 0, 2)).reshape(6, width)
    vec_out, vec_down, gain_one, bias_one, gain_two, bias_two = [short[i] for i in range(6)]

    second = lax.all_gather(after(second, qkv), "blk", axis=0, tiled=False)
    up_rows = groups * dim_rows * units_here // width
    mat_up = second[:, :up_rows].reshape(width, units_here)
    mat_down = second[:, up_rows:].reshape(units_here, width)

    my_pair = my_block // repeats
    my_part = my_block % repeats
    my_seq = my_pair // heads_here
    inner = jnp.arange(length, dtype=jnp.int32)
    place = (inner // block_rows) * block_rows + inner % span
    place = place + (((inner // span) % groups) ^ my_group) * span
    offsets = lax.dynamic_index_in_dim(doc_offsets, my_seq, 0, False)
    flags = lax.dynamic_index_in_dim(valid_flags, my_seq, 0, False)
    flags = xor_order(flags.reshape(blocks, groups, span), 1, my_group).reshape(length)
    segment = jnp.sum((offsets[None, :] <= place[:, None]).astype(jnp.int32), axis=1) - 1
    seg_row = segment.reshape(length // QUERY_ROWS, 1, QUERY_ROWS)
    seg_key = jnp.where(flags > 0, segment, -1)
    seg_key = jnp.broadcast_to(seg_key[:, None], (length, 128))
    attn_low, attn_t, lse = attend(spot, seg_row, seg_key, qkv, wide, parts_length)

    sent = jnp.concatenate([attn_low] * repeats, axis=0) if repeats > 1 else attn_low
    got = lax.all_to_all(sent, ALL, split_axis=0, concat_axis=0, tiled=True)
    my_span = my_block * groups + my_group
    local_flags = lax.dynamic_slice_in_dim(valid_flags, my_span * span, span, 1)
    local_flags = local_flags.reshape(rows, 1).astype(F32)
    *sent, normed_one, unit_one, inv_one, squares = join(
        spot, got, token_rows, local_flags, mat_out, short, seqs, heads_here, repeats
    )
    joint_parts = [sent[0]] + [swapped(sent[k], "heads", k) for k in range(1, groups)]
    ffn_results = [
        ffn_part(part, mat_up, mat_down, vec_up[None], F32 if k == 0 else BF16)
        for k, part in enumerate(joint_parts)
    ]
    ffn_others = [swapped(ffn_results[k][0], "heads", k) for k in range(1, groups)]
    output, grad_resid_two, grad_ffn, early, squares = middle(
        ffn_results[0][0], ffn_others, normed_one, short, local_flags,
        cotangent.reshape(rows, width), squares,
    )
    output = output.reshape(tokens.shape)
    grad_ffn_parts = gather_parts(grad_ffn, "heads")
    grad_results = [
        ffn_back_part(part, item[2], mat_up, mat_down, F32 if k == 0 else BF16)
        for k, (part, item) in enumerate(zip(grad_ffn_parts, ffn_results))
    ]
    grad_normed_parts = [item[0] for item in grad_results]
    grad_normed_others = [swapped(grad_normed_parts[k], "heads", k) for k in range(1, groups)]
    *ffn_grads, grad_vec_up = ffn_grads_call(
        [item[1] for item in ffn_results],
        grad_ffn_parts,
        joint_parts,
        [after(grad_results[0][1], grad_normed_others[-1])] + [item[1] for item in grad_results[1:]],
        blocks,
    )
    ffn_grads = [
        lax.psum_scatter(
            item.reshape(-1, item.shape[-1]), "blk", scatter_dimension=0, tiled=True
        )
        for item in ffn_grads
    ]
    if units_here == width:
        shard_down, shard_up = ffn_grads[0][:unit_rows], ffn_grads[0][unit_rows:]
    else:
        shard_down, shard_up = ffn_grads
    shard_down = shard_down.astype(F32)

    sent, grad_resid_one, grad_branch = branch_back(
        spot, grad_normed_parts[0], grad_normed_others, grad_resid_two, unit_one, inv_one,
        gain_one[None], mat_out, early,
        grad_vec_up, squares, seqs, heads_here, repeats, devices,
    )
    got = lax.all_to_all(sent, ALL, split_axis=0, concat_axis=0, tiled=True)
    small = jnp.sum(got[:, wide:].astype(F32), axis=0)
    small = small[:8] + small[8:]
    vector_sums = lax.dynamic_slice_in_dim(small[:6], my_span * dim_rows % 128, dim_rows, 1)
    shard_vec_up = lax.dynamic_slice_in_dim(small[6], my_block * unit_rows % 128, unit_rows, 0)
    real_count = jnp.maximum(jnp.sum(valid_flags.astype(F32)), 1.0)
    rms = jnp.sqrt(small[7, :4] / (real_count * width))

    grads = attend_back(spot, seg_row, seg_key, qkv, got, attn_t, lse)
    branch_parts = gather_parts(after(grad_branch, grads), "heads")
    grad_mat_out = out_grads_call(joint_parts, branch_parts)
    got = lax.all_to_all(grads, "blk", split_axis=0, concat_axis=0, tiled=True)
    shard_out = scatter_blk(after(grad_mat_out, got).reshape(blocks, dim_rows, width)).astype(BF16)
    route = [(j, j % groups * blocks + j // groups) for j in range(devices)]
    shard_out = lax.ppermute(shard_out, ("heads", "blk"), route)
    shard_up = after(shard_up, got).reshape(groups, dim_rows, units_here)
    shard_up = xor_order(shard_up, 0, my_group)
    up_parts = [shard_up[0]] + [swapped(shard_up[k], "heads", k) for k in range(1, groups)]
    shard_up = place_columns(spot, up_parts, blocks)
    own_input, other_input, keep, send = input_grads(
        spot, got, mat_three, token_all, heads_here, groups, repeats
    )
    grad_input = grad_resid_one + own_input
    for k in range(1, groups):
        grad_input = grad_input + swapped(other_input[k - 1], "heads", k).astype(F32)
    grad_input = grad_input.reshape(tokens.shape)
    chip_sums = keep + swapped(send, "blk", 1).astype(F32)
    chip_low = chip_sums.astype(BF16)
    three_grads = chip_sums[0]
    for k in range(1, blocks // 2):
        three_grads = three_grads + swapped(chip_low[k], "blk", 2 * k).astype(F32)
    own_rows = three_grads[: groups * dim_rows].reshape(groups, dim_rows, 3 * width_here)
    own_sums = three_grads[groups * dim_rows, :256].reshape(2, 128)[:, : groups * dim_rows]
    own_sums = jnp.transpose(own_sums.reshape(2, groups, dim_rows), (1, 0, 2))
    row = lax.broadcasted_iota(jnp.int32, (1, 16, 1), 1)
    own_sums = jnp.concatenate(
        [
            own_sums.reshape(groups, 2 * dim_rows),
            jnp.zeros((groups, 3 * width_here - 2 * dim_rows), F32),
        ],
        axis=1,
    )
    own_sums = jnp.where(row == 0, own_sums[:, None, :], 0.0)
    own = jnp.concatenate([own_rows, own_sums], axis=1).astype(BF16)
    for part in up_parts[1:]:
        own = after(own, part)
    own = lax.all_to_all(own, "heads", split_axis=0, concat_axis=0, tiled=True)
    shards_three = split_columns(own, dim_rows)
    shard_sums = shards_three[3][0]

    return (
        output,
        grad_input,
        shards_three[0],
        shards_three[1],
        shards_three[2],
        shard_out.astype(F32),
        shard_up,
        shard_down,
        shard_sums[:dim_rows],
        shard_sums[dim_rows : 2 * dim_rows],
        vector_sums[0],
        shard_vec_up,
        vector_sums[3],
        vector_sums[1],
        vector_sums[2],
        vector_sums[4],
        vector_sums[5],
        rms,
    )


def solution(mesh):
    token_spec = P(None, ALL, None)
    matrix_spec = P(ALL, None)
    vector_spec = P(ALL)
    return jax.shard_map(
        per_device,
        mesh=mesh,
        in_specs=(token_spec,) * 2 + (P(),) * 2 + (matrix_spec,) * 6 + (vector_spec,) * 9,
        out_specs=(token_spec,) * 2 + (matrix_spec,) * 6 + (vector_spec,) * 9 + (P(),),
        check_vma=False,
    )
```

```python
import functools

import jax
import jax.numpy as jnp
from jax import lax
from jax.experimental import pallas as pl
from jax.experimental.pallas import tpu as pltpu
from jax.sharding import PartitionSpec as P

HEAD_DIM = 64
NORM_EPS = 1e-05
NEG_LARGE = -1e30
QUERY_ROWS = 256
BF16 = jnp.bfloat16
F32 = jnp.float32
ALL = ("blk", "heads")


def vmem_limit(length):
    return 8 * 1024 * 1024 + 6 * 1024 * length


def matmul(left, right):
    return jnp.dot(left, right, preferred_element_type=F32)


def matmul_tn(left, right):
    return lax.dot_general(left, right, (((0,), (0,)), ((), ())), preferred_element_type=F32)


def matmul_nt(left, right):
    return lax.dot_general(left, right, (((1,), (1,)), ((), ())), preferred_element_type=F32)


def after(block, other):
    spot = lax.slice(other, (0,) * other.ndim, (1,) * other.ndim).reshape(())
    return block + (spot * 0).astype(block.dtype)


def swapped(block, axis, mask):
    count = lax.axis_size(axis)
    return lax.ppermute(block, axis, [(i, i ^ mask) for i in range(count)])


def gather_parts(block, axis):
    return [block] + [swapped(block, axis, k) for k in range(1, lax.axis_size(axis))]


def scatter_parts(parts, axis):
    total = parts[0].astype(F32)
    for k in range(1, len(parts)):
        total = total + swapped(parts[k].astype(BF16), axis, k).astype(F32)
    return total


def xor_order(array, dim, index):
    pieces = [
        lax.dynamic_index_in_dim(array, index ^ k, dim, True) for k in range(array.shape[dim])
    ]
    return jnp.concatenate(pieces, axis=dim)


def gather_blk_parts(block, first_needs):
    count = lax.axis_size("blk")
    mine = jnp.stack([block] + [swapped(block, "blk", k) for k in range(2, count, 2)])
    mine = after(mine, first_needs)
    return mine, swapped(mine, "blk", 1)


def gather_blk(block, first_needs):
    mine, other = gather_blk_parts(block, first_needs)
    both = jnp.stack([mine, other], axis=1).reshape((-1,) + block.shape)
    return xor_order(both, 0, lax.axis_index("blk"))


def scatter_blk(blocks):
    index = lax.axis_index("blk")
    ordered = xor_order(blocks, 0, index)
    pairs = ordered.reshape((ordered.shape[0] // 2, 2) + ordered.shape[1:])
    total = pairs[:, 0].astype(F32) + swapped(pairs[:, 1], "blk", 1).astype(F32)
    low = total.astype(BF16)
    result = total[0]
    for k in range(1, low.shape[0]):
        result = result + swapped(low[k], "blk", 2 * k).astype(F32)
    return result


def layer_norm(resid, norm_gain, norm_bias):
    center = resid - jnp.mean(resid, axis=-1, keepdims=True)
    inv_std = lax.rsqrt(jnp.mean(center * center, axis=-1, keepdims=True) + NORM_EPS)
    normed = center * inv_std
    return (normed * norm_gain + norm_bias, normed, inv_std)


def norm_back(upstream, normed, inv_std, norm_gain):
    scaled = upstream * norm_gain
    return inv_std * (
        scaled
        - jnp.mean(scaled, axis=-1, keepdims=True)
        - normed * jnp.mean(scaled * normed, axis=-1, keepdims=True)
    )


def gelu_slope(hidden):
    cdf_part = 0.5 * (1.0 + lax.erf(hidden * 0.7071067811865476))
    pdf_part = jnp.exp(-0.5 * hidden * hidden) * 0.3989422804014327
    return cdf_part + hidden * pdf_part


def two_halves(values):
    high = lax.reduce_precision(values, 8, 7)
    return jnp.stack([high, values - high], axis=-1).astype(BF16)


def left_lanes(block):
    lane = lax.broadcasted_iota(jnp.int32, block.shape, 1)
    return jnp.where(lane < HEAD_DIM, block, 0.0)


def masked_scores(seg_key, seg_query, scores):
    width = scores.shape[1] // seg_key.shape[1]
    same = jnp.concatenate([seg_key] * width, axis=1) == seg_query
    return jnp.where(same, scores, NEG_LARGE)


def own_scores(seg_key, seg_query, scores):
    width = scores.shape[1] // seg_key.shape[1]
    same = jnp.concatenate([seg_key] * width, axis=1) == seg_query
    rows = lax.broadcasted_iota(jnp.int32, scores.shape, 0)
    columns = lax.broadcasted_iota(jnp.int32, scores.shape, 1)
    return jnp.where(same | (rows == columns), scores, NEG_LARGE)


def score_all(turn, seg_query, seg_key_ref, qkv_ref, query_t, scores):
    sources, rows = qkv_ref.shape[0], qkv_ref.shape[1] * 2 // 3
    per_source = rows // QUERY_ROWS
    query_now = query_t[turn]
    for b in range(sources):
        spot = slice(b * rows, (b + 1) * rows)
        scores[spot, :] = masked_scores(
            seg_key_ref[spot, :], seg_query, matmul(qkv_ref[b, 0:rows, :], query_now)
        )
    own = pl.ds(pl.multiple_of(turn * QUERY_ROWS, QUERY_ROWS), QUERY_ROWS)
    inner = pl.ds(pl.multiple_of(turn % per_source * QUERY_ROWS, QUERY_ROWS), QUERY_ROWS)
    own_pair = qkv_ref[turn // per_source, inner, :]
    scores[own, :] = own_scores(seg_key_ref[own, :], seg_query, matmul(own_pair, query_now))
    return own, own_pair


def turn_queries(b, turned, query_t):
    per_source = turned.shape[1] // QUERY_ROWS
    low = jnp.concatenate([jnp.zeros_like(turned[0:HEAD_DIM]), turned[0:HEAD_DIM]], axis=0)
    for t in range(per_source):
        spot = slice(t * QUERY_ROWS, (t + 1) * QUERY_ROWS)
        query_t[b * per_source + t] = low[:, spot].astype(BF16)


def attend_kernel(
    spot_ref, seg_row_ref, seg_key_ref, qkv_ref, low_ref, attn_ref, lse_ref,
    query_t, values_t, scores,
):
    step = pl.program_id(0)
    sources, rows = qkv_ref.shape[0], qkv_ref.shape[1] * 2 // 3
    half = rows // 2

    @pl.when(step == 0)
    def _():
        for b in range(sources):
            turn_queries(b, qkv_ref[b, 0:rows, :].astype(F32).T, query_t)
            turned = qkv_ref[b, rows : rows + half, :].astype(F32).T
            values_t[:, b * rows : b * rows + half] = turned[0:HEAD_DIM].astype(BF16)
            values_t[:, b * rows + half : (b + 1) * rows] = turned[
                HEAD_DIM : 2 * HEAD_DIM
            ].astype(BF16)

    turn = spot_ref[2] + step
    score_all(turn, seg_row_ref[0], seg_key_ref, qkv_ref, query_t, scores)
    top = jnp.max(scores[...], axis=0, keepdims=True)
    total = jnp.zeros_like(top)
    result = jnp.zeros((HEAD_DIM, QUERY_ROWS), F32)
    for b in range(sources):
        spot = slice(b * rows, (b + 1) * rows)
        probs = jnp.exp(scores[spot, :] - top)
        total = total + jnp.sum(probs, axis=0, keepdims=True)
        result = result + matmul(values_t[:, spot], probs.astype(BF16))
    result = result / total
    attn_ref[...] = result
    lse_ref[0] = top + jnp.log(total)
    turned = result.T
    wide = low_ref.shape[1]
    spans = QUERY_ROWS // (2 * wide)
    first = turn % (rows // QUERY_ROWS) * spans
    for t in range(spans):
        left = turned[2 * t * wide : (2 * t + 1) * wide]
        right = turned[(2 * t + 1) * wide : (2 * t + 2) * wide]
        low_ref[spot_ref[1] ^ (first + t)] = jnp.concatenate([left, right], axis=1).astype(BF16)


def attend(spot, seg_row, seg_key, qkv, wide, query_length):
    sources, rows = qkv.shape[0], qkv.shape[1] * 2 // 3
    length = sources * rows
    steps = query_length // QUERY_ROWS
    spans = rows // (2 * wide)
    per_source = rows // QUERY_ROWS
    return pl.pallas_call(
        attend_kernel,
        grid_spec=pltpu.PrefetchScalarGridSpec(
            num_scalar_prefetch=1,
            grid=(steps,),
            in_specs=[
                pl.BlockSpec((1, 1, QUERY_ROWS), lambda i, spot: (spot[2] + i, 0, 0)),
                pl.BlockSpec(seg_key.shape, lambda i, spot: (0, 0)),
                pl.BlockSpec(qkv.shape, lambda i, spot: (0, 0, 0)),
            ],
            out_specs=[
                pl.BlockSpec((spans, wide, 128), lambda i, spot: (i // per_source, 0, 0)),
                pl.BlockSpec((HEAD_DIM, QUERY_ROWS), lambda i, spot: (0, i)),
                pl.BlockSpec((1, 1, QUERY_ROWS), lambda i, spot: (i, 0, 0)),
            ],
            scratch_shapes=[
                pltpu.VMEM((length // QUERY_ROWS, 128, QUERY_ROWS), BF16),
                pltpu.VMEM((HEAD_DIM, length), BF16),
                pltpu.VMEM((length, QUERY_ROWS), F32),
            ],
        ),
        out_shape=[
            jax.ShapeDtypeStruct((steps // per_source * spans, wide, 128), BF16),
            jax.ShapeDtypeStruct((HEAD_DIM, query_length), F32),
            jax.ShapeDtypeStruct((steps, 1, QUERY_ROWS), F32),
        ],
        compiler_params=pltpu.CompilerParams(vmem_limit_bytes=vmem_limit(length)),
    )(spot, seg_row, seg_key, qkv)


def attend_back_kernel(
    spot_ref, seg_row_ref, seg_key_ref, qkv_ref, up_ref, attn_ref, lse_ref, grads_ref,
    query_t, keys_t, values, scores, grad_query, grad_key, grad_value,
):
    step = pl.program_id(0)
    sources, rows = qkv_ref.shape[0], qkv_ref.shape[1] * 2 // 3
    half = rows // 2
    lane = lax.broadcasted_iota(jnp.int32, (rows, 128), 1)

    @pl.when(step == 0)
    def _():
        for b in range(sources):
            turned = qkv_ref[b, 0:rows, :].astype(F32).T
            turn_queries(b, turned, query_t)
            keys_t[:, b * rows : (b + 1) * rows] = turned[HEAD_DIM : 2 * HEAD_DIM].astype(BF16)
            packed = qkv_ref[b, rows : rows + half, :].astype(F32)
            values[b * rows : b * rows + half, :] = left_lanes(packed).astype(BF16)
            values[b * rows + half : (b + 1) * rows, :] = left_lanes(
                pltpu.roll(packed, HEAD_DIM, 1)
            ).astype(BF16)
        grad_query[...] = jnp.zeros_like(grad_query)
        grad_key[...] = jnp.zeros_like(grad_key)
        grad_value[...] = jnp.zeros_like(grad_value)

    turn = spot_ref[2] + step
    lse = lse_ref[0]
    pieces = []
    spans = QUERY_ROWS // (rows // up_ref.shape[0])
    first = turn % (rows // QUERY_ROWS) * spans
    for t in range(spans):
        packed = up_ref[spot_ref[1] ^ (first + t), 0 : rows // up_ref.shape[0] // 2, :].astype(F32)
        pieces.append(left_lanes(packed))
        pieces.append(left_lanes(pltpu.roll(packed, HEAD_DIM, 1)))
    up_now = jnp.concatenate(pieces, axis=0)
    up_turned = up_now.T
    delta = jnp.sum(up_turned[0:HEAD_DIM] * attn_ref[...], axis=0, keepdims=True)
    up_now = up_now.astype(BF16)
    up_turned = up_turned.astype(BF16)
    own, own_pair = score_all(turn, seg_row_ref[0], seg_key_ref, qkv_ref, query_t, scores)
    query_now = pltpu.roll(own_pair.astype(F32), HEAD_DIM, 1).astype(BF16)
    result = jnp.zeros((HEAD_DIM, QUERY_ROWS), F32)
    for b in range(sources):
        spot = slice(b * rows, (b + 1) * rows)
        probs = jnp.exp(scores[spot, :] - lse)
        grad_probs = matmul(values[spot, :], up_turned)
        grad_scores = (probs * (grad_probs - delta)).astype(BF16)
        grad_value[spot, :] += matmul(probs.astype(BF16), up_now)
        grad_key[spot, :] += matmul(grad_scores, query_now)
        result = result + matmul(keys_t[:, spot], grad_scores)
    grad_query[own, :] = jnp.concatenate([result, jnp.zeros_like(result)], axis=0).T

    @pl.when(step == pl.num_programs(0) - 1)
    def _():
        for b in range(sources):
            spot = slice(b * rows, (b + 1) * rows)
            grads_ref[b, 0:rows, :] = jnp.where(
                lane < HEAD_DIM, grad_query[spot, :], grad_key[spot, :]
            ).astype(BF16)
            upper = grad_value[b * rows : b * rows + half, :]
            lower = grad_value[b * rows + half : (b + 1) * rows, :]
            grads_ref[b, rows : rows + half, :] = (
                upper + pltpu.roll(lower, HEAD_DIM, 1)
            ).astype(BF16)


def attend_back(spot, seg_row, seg_key, qkv, upstream, attn_t, lse):
    sources, rows = qkv.shape[0], qkv.shape[1] * 2 // 3
    length = sources * rows
    steps = lse.shape[0]
    groups = upstream.shape[0] // sources
    per_source = rows // QUERY_ROWS
    return pl.pallas_call(
        attend_back_kernel,
        grid_spec=pltpu.PrefetchScalarGridSpec(
            num_scalar_prefetch=1,
            grid=(steps,),
            in_specs=[
                pl.BlockSpec((1, 1, QUERY_ROWS), lambda i, spot: (spot[2] + i, 0, 0)),
                pl.BlockSpec(seg_key.shape, lambda i, spot: (0, 0)),
                pl.BlockSpec(qkv.shape, lambda i, spot: (0, 0, 0)),
                pl.BlockSpec(
                    (groups,) + upstream.shape[1:],
                    lambda i, spot: ((spot[2] + i) // per_source, 0, 0),
                ),
                pl.BlockSpec((HEAD_DIM, QUERY_ROWS), lambda i, spot: (0, i)),
                pl.BlockSpec((1, 1, QUERY_ROWS), lambda i, spot: (i, 0, 0)),
            ],
            out_specs=pl.BlockSpec(qkv.shape, lambda i, spot: (0, 0, 0)),
            scratch_shapes=[
                pltpu.VMEM((length // QUERY_ROWS, 128, QUERY_ROWS), BF16),
                pltpu.VMEM((HEAD_DIM, length), BF16),
                pltpu.VMEM((length, 128), BF16),
                pltpu.VMEM((length, QUERY_ROWS), F32),
                pltpu.VMEM((length, 128), F32),
                pltpu.VMEM((length, 128), F32),
                pltpu.VMEM((length, 128), F32),
            ],
        ),
        out_shape=jax.ShapeDtypeStruct(qkv.shape, BF16),
        compiler_params=pltpu.CompilerParams(vmem_limit_bytes=vmem_limit(length)),
    )(spot, seg_row, seg_key, qkv, upstream, attn_t, lse)


def left_pair(first, second):
    lane = lax.broadcasted_iota(jnp.int32, first.shape, 1)
    return jnp.where(lane < HEAD_DIM, first, pltpu.roll(second, HEAD_DIM, 1))


def right_pair(first, second):
    lane = lax.broadcasted_iota(jnp.int32, first.shape, 1)
    return jnp.where(lane < HEAD_DIM, pltpu.roll(first, HEAD_DIM, 1), second)


def join_kernel(
    seqs, heads_here, repeats, spot_ref, got_ref, tokens_ref, flags_ref, mat_ref, vectors_ref,
    *refs,
):
    sents, (normed_ref, unit_ref, inv_ref, squares_ref, attn) = refs[:-5], refs[-5:]
    my_group, part = spot_ref[1], spot_ref[3]
    groups = len(sents)
    wide = got_ref.shape[1]
    width = tokens_ref.shape[1]
    width_here = heads_here * HEAD_DIM
    for which in range(seqs):
        for group in range(groups):
            for head in range(0, heads_here, 2):
                first, second = [
                    got_ref[
                        ((which * heads_here + i) * repeats + part) * groups + group
                    ].astype(F32)
                    for i in (head, head + 1)
                ]
                start = group * width_here + head * HEAD_DIM
                top = 2 * which * wide
                attn[top : top + wide, start : start + 128] = left_pair(first, second).astype(BF16)
                attn[top + wide : top + 2 * wide, start : start + 128] = right_pair(
                    first, second
                ).astype(BF16)
    branch = matmul(attn[...], mat_ref[...]) + vectors_ref[0:1, :]
    resid_in = tokens_ref[...].astype(F32)
    normed, unit, inv_std = layer_norm(resid_in + branch, vectors_ref[2:3, :], vectors_ref[3:4, :])
    normed_ref[...] = normed
    unit_ref[...] = unit
    inv_ref[...] = jnp.broadcast_to(inv_std, inv_ref.shape)
    low = normed.astype(BF16)
    for k in range(groups):
        sents[k][:, 0:width] = low
        for group in range(groups):

            @pl.when((my_group ^ k) == group)
            def _():
                sents[k][:, width:] = attn[:, group * width_here : (group + 1) * width_here]

    lane = lax.broadcasted_iota(jnp.int32, squares_ref.shape, 1)
    total = jnp.zeros(squares_ref.shape, F32)
    for i, item in enumerate((resid_in, branch, normed)):
        size = flags_ref[...] * jnp.sum(item * item, axis=1, keepdims=True)
        total = total + jnp.where(lane == i, jnp.sum(size, axis=0, keepdims=True), 0.0)
    squares_ref[...] = total


def join(spot, got, tokens, flags, mat_out, vectors, seqs, heads_here, repeats):
    groups = tokens.shape[1] // (heads_here * HEAD_DIM)
    rows, width = tokens.shape
    vmem = pl.BlockSpec(memory_space=pltpu.VMEM)
    return pl.pallas_call(
        functools.partial(join_kernel, seqs, heads_here, repeats),
        in_specs=[pl.BlockSpec(memory_space=pltpu.SMEM)] + [vmem] * 5,
        out_specs=[vmem] * (groups + 4),
        out_shape=[jax.ShapeDtypeStruct((rows, width + heads_here * HEAD_DIM), BF16)] * groups
        + [
            jax.ShapeDtypeStruct((rows, width), F32),
            jax.ShapeDtypeStruct((rows, width), F32),
            jax.ShapeDtypeStruct((rows, 128), F32),
            jax.ShapeDtypeStruct((1, 128), F32),
        ],
        scratch_shapes=[pltpu.VMEM((rows, width), BF16)],
        compiler_params=pltpu.CompilerParams(vmem_limit_bytes=32 * 1024 * 1024),
    )(spot, got, tokens, flags, mat_out, vectors)


def middle_kernel(others, *refs):
    own_ref, normed_ref, vectors_ref, flags_ref, up_ref, squares_ref = refs[:6]
    parts = refs[6 : 6 + others]
    out_ref, resid_ref, low_ref, early_ref, total_ref = refs[6 + others :]
    ffn = own_ref[...]
    for part in parts:
        ffn = ffn + part[...].astype(F32)
    ffn = ffn + vectors_ref[1:2, :]
    gain = vectors_ref[4:5, :]
    normed, unit, inv_std = layer_norm(normed_ref[...] + ffn, gain, vectors_ref[5:6, :])
    out_ref[...] = normed.astype(BF16)
    upstream = up_ref[...].astype(F32)
    grad_resid = norm_back(upstream, unit, inv_std, gain)
    resid_ref[...] = grad_resid
    low = grad_resid.astype(BF16)
    low_ref[...] = low
    early_ref[0:1, :] = jnp.sum(low.astype(F32), axis=0, keepdims=True)
    early_ref[1:2, :] = jnp.sum(upstream * unit, axis=0, keepdims=True)
    early_ref[2:3, :] = jnp.sum(upstream, axis=0, keepdims=True)
    size = flags_ref[...] * jnp.sum(ffn * ffn, axis=1, keepdims=True)
    lane = lax.broadcasted_iota(jnp.int32, total_ref.shape, 1)
    total_ref[...] = squares_ref[...] + jnp.where(
        lane == 3, jnp.sum(size, axis=0, keepdims=True), 0.0
    )


def middle(own, others, normed, vectors, flags, upstream, squares):
    rows, width = own.shape
    return whole_call(
        functools.partial(middle_kernel, len(others)),
        [
            jax.ShapeDtypeStruct((rows, width), BF16),
            jax.ShapeDtypeStruct((rows, width), F32),
            jax.ShapeDtypeStruct((rows, width), BF16),
            jax.ShapeDtypeStruct((8, width), F32),
            jax.ShapeDtypeStruct((1, 128), F32),
        ],
        (own, normed, vectors, flags, upstream, squares, *others),
    )


def branch_back_kernel(
    seqs, heads_here, repeats, spot_ref, *refs,
):
    (own_ref, resid_ref, unit_ref, inv_ref, gain_ref, mat_ref, early_ref, up_sums_ref,
     squares_ref), others, (sent_ref, grad_ref, low_ref) = refs[:9], refs[9:-3], refs[-3:]
    my_group = spot_ref[1]
    groups = len(others) + 1
    rows, width = own_ref.shape
    span = rows // seqs
    wide = span // 2
    devices = sent_ref.shape[0]
    blocks = devices // groups
    grad_normed = own_ref[...]
    for other in others:
        grad_normed = grad_normed + other[...].astype(F32)
    grad_normed = grad_normed + resid_ref[...]
    unit = unit_ref[...]
    grad_resid = norm_back(grad_normed, unit, inv_ref[:, 0:1], gain_ref[...])
    grad_ref[...] = grad_resid
    low = grad_resid.astype(BF16)
    low_ref[...] = low
    grad_attn = matmul_nt(low, mat_ref[...])
    for which in range(seqs):
        top = which * span
        for group in range(groups):
            for head in range(0, heads_here, 2):
                start = (group * heads_here + head) * HEAD_DIM
                upper = grad_attn[top : top + wide, start : start + 128]
                lower = grad_attn[top + wide : top + span, start : start + 128]
                blocks_two = (left_pair(upper, lower), right_pair(upper, lower))
                for i in range(2):
                    for copy in range(repeats):
                        pair = which * heads_here + head + i
                        place = (pair * repeats + copy) * groups + group
                        sent_ref[place, 0:wide, :] = blocks_two[i].astype(BF16)
    sums = [
        jnp.sum(low.astype(F32), axis=0, keepdims=True),
        jnp.sum(grad_normed * unit, axis=0, keepdims=True),
        jnp.sum(grad_normed, axis=0, keepdims=True),
    ] + [early_ref[i : i + 1, :] for i in range(3)]
    row = lax.broadcasted_iota(jnp.int32, (8, 128), 0)
    dim_rows = width // devices
    unit_rows = up_sums_ref.shape[1] // blocks
    for tile in range(width // 128):
        base = jnp.where(row == 7, squares_ref[...], 0.0)
        for i in range(6):
            base = base + jnp.where(row == i, sums[i][:, tile * 128 : (tile + 1) * 128], 0.0)
        for place in range(tile * 128 // dim_rows, (tile + 1) * 128 // dim_rows):
            start = place // groups * unit_rows // 128 * 128
            mine = jnp.where(my_group == place % groups, up_sums_ref[:, start : start + 128], 0.0)
            block = base + jnp.where(row == 6, mine, 0.0)
            high = block.astype(BF16)
            rest = block - high.astype(F32)
            sent_ref[place, wide : wide + 16, :] = jnp.concatenate(
                [high.astype(F32), rest], axis=0
            ).astype(BF16)


def branch_back(spot, own, others, resid, unit, inv_std, gain, mat_out, early, up_sums, squares,
                seqs, heads_here, repeats, devices):
    rows, width = own.shape
    vmem = pl.BlockSpec(memory_space=pltpu.VMEM)
    return pl.pallas_call(
        functools.partial(branch_back_kernel, seqs, heads_here, repeats),
        in_specs=[pl.BlockSpec(memory_space=pltpu.SMEM)] + [vmem] * (9 + len(others)),
        out_specs=[vmem] * 3,
        out_shape=[
            jax.ShapeDtypeStruct((devices, rows // seqs // 2 + 16, 128), BF16),
            jax.ShapeDtypeStruct((rows, width), F32),
            jax.ShapeDtypeStruct((rows, width), BF16),
        ],
        compiler_params=pltpu.CompilerParams(vmem_limit_bytes=32 * 1024 * 1024),
    )(spot, own, resid, unit, inv_std, gain, mat_out, early, up_sums, squares, *others)


def pack_kernel(*refs):
    out_ref = refs[-1]
    rows = [jnp.zeros((1, 128), F32) for _ in range(out_ref.shape[0])]
    start = 0
    for ref in refs[:-1]:
        size = ref.shape[1]
        pieces = [ref[...].astype(F32)]
        if start % 128:
            pieces = [jnp.zeros((1, start % 128), F32)] + pieces
        if start % 128 + size < 128:
            pieces = pieces + [jnp.zeros((1, 128 - start % 128 - size), F32)]
        piece = jnp.concatenate(pieces, axis=1) if len(pieces) > 1 else pieces[0]
        rows[start // 128] = rows[start // 128] + piece
        start += size
    out_ref[...] = jnp.concatenate(rows, axis=0).astype(BF16)


def project_kernel(groups, heads_here, repeats, spot_ref, *refs):
    tokens, (mine_ref, other_ref, sent_ref, all_ref, mat_ref, short_ref, values) = (
        refs[:groups], refs[groups:]
    )
    my_block, my_group = spot_ref[0], spot_ref[1]
    halves, chip_rows, _ = mine_ref.shape
    blocks = 2 * halves
    dim_rows = chip_rows // groups
    rows, width = tokens[0].shape
    width_here = heads_here * HEAD_DIM
    seqs = sent_ref.shape[0] // (repeats * heads_here)
    span = rows // seqs
    block_rows = span * groups
    for k in range(groups):
        all_ref[k * rows : (k + 1) * rows, :] = tokens[k][...]
    for b in range(blocks):
        place = my_block ^ b
        spot = slice(b * chip_rows, (b + 1) * chip_rows)

        @pl.when(place % 2 == 0)
        def _():
            mat_ref[spot, :] = mine_ref[place // 2, :, 0 : 3 * width_here]

        @pl.when(place % 2 == 1)
        def _():
            mat_ref[spot, :] = other_ref[place // 2, :, 0 : 3 * width_here]

    for b in range(blocks):
        place = my_block ^ b
        vectors = jnp.where(
            place % 2 == 0,
            mine_ref[place // 2, :, 3 * width_here :].astype(F32),
            other_ref[place // 2, :, 3 * width_here :].astype(F32),
        )
        for group in range(groups):
            short_ref[b * groups + group] = vectors[group * dim_rows : group * dim_rows + 8]
    lane = lax.broadcasted_iota(jnp.int32, (1, 128), 1)
    tiles = width_here // 128
    biases = [[jnp.zeros((1, 128), F32) for _ in range(tiles)] for _ in range(2)]
    for t in range(blocks):
        place = my_block ^ (my_group * (blocks // groups) + t // groups)
        piece = jnp.where(
            place % 2 == 0,
            mine_ref[place // 2, :, 3 * width_here :].astype(F32),
            other_ref[place // 2, :, 3 * width_here :].astype(F32),
        )
        piece = piece[t % groups * dim_rows : t % groups * dim_rows + 1]
        tile, start = t * dim_rows // 128, t * dim_rows % 128
        inside = (lane >= start) & (lane < start + dim_rows)
        for which in range(2):
            shift = (start - which * dim_rows) % 128
            moved = pltpu.roll(piece, shift, 1) if shift else piece
            biases[which][tile] = biases[which][tile] + jnp.where(inside, moved, 0.0)
    query_bias, value_bias = [jnp.concatenate(item, axis=1) for item in biases]
    result = matmul(all_ref[...], mat_ref[...])
    query = (result[:, :width_here] + query_bias) * HEAD_DIM ** (-0.5)
    key = result[:, width_here : 2 * width_here]
    values[...] = result[:, 2 * width_here :] + value_bias
    half_parts = groups // 2
    for pair in range(seqs * heads_here):
        which, head = pair // heads_here, pair % heads_here
        columns = slice(head * HEAD_DIM, (head + 1) * HEAD_DIM)
        for k in range(groups):
            spot = slice(k * rows + which * span, k * rows + (which + 1) * span)
            block = jnp.concatenate([query[spot, columns], key[spot, columns]], axis=1)
            for copy in range(repeats):
                sent_ref[pair * repeats + copy, k * span : (k + 1) * span, :] = block.astype(BF16)
        for k in range(half_parts):
            upper = slice(k * rows + which * span, k * rows + (which + 1) * span)
            lower = slice(upper.start + half_parts * rows, upper.stop + half_parts * rows)
            block = jnp.concatenate([values[upper, columns], values[lower, columns]], axis=1)
            for copy in range(repeats):
                sent_ref[
                    pair * repeats + copy, block_rows + k * span : block_rows + (k + 1) * span, :
                ] = block.astype(BF16)


def project(spot, token_parts, mine, other, seqs, heads_here, repeats):
    groups = len(token_parts)
    rows, width = token_parts[0].shape
    blocks = seqs * heads_here * repeats
    block_rows = rows // seqs * groups
    vmem = pl.BlockSpec(memory_space=pltpu.VMEM)
    return pl.pallas_call(
        functools.partial(project_kernel, groups, heads_here, repeats),
        in_specs=[pl.BlockSpec(memory_space=pltpu.SMEM)] + [vmem] * (groups + 2),
        out_specs=[vmem] * 4,
        out_shape=[
            jax.ShapeDtypeStruct((blocks, block_rows * 3 // 2, 128), BF16),
            jax.ShapeDtypeStruct((groups * rows, width), BF16),
            jax.ShapeDtypeStruct((width, 3 * heads_here * HEAD_DIM), BF16),
            jax.ShapeDtypeStruct((blocks * groups, 8, 128), F32),
        ],
        scratch_shapes=[pltpu.VMEM((groups * rows, heads_here * HEAD_DIM), F32)],
        compiler_params=pltpu.CompilerParams(vmem_limit_bytes=40 * 1024 * 1024),
    )(spot, *token_parts, mine, other)


def input_kernel(
    groups, heads_here, repeats, spot_ref, got_ref, mat_ref, all_ref,
    own_ref, others_ref, keep_ref, send_ref, grads, mat_grads,
):
    my_block, my_group = spot_ref[0], spot_ref[1]
    blocks = got_ref.shape[0]
    seqs = blocks // (repeats * heads_here)
    rows = all_ref.shape[0] // groups
    span = rows // seqs
    block_rows = span * groups
    width_here = heads_here * HEAD_DIM
    chip_rows = keep_ref.shape[1] - 16
    half_parts = groups // 2

    def received(pair, start):
        spot = slice(start, start + span)
        total = got_ref[pair * repeats, spot, :].astype(F32)
        for copy in range(1, repeats):
            total = total + got_ref[pair * repeats + copy, spot, :].astype(F32)
        return total

    for which in range(seqs):
        for head in range(0, heads_here, 2):
            pair = which * heads_here + head
            start = head * HEAD_DIM
            for k in range(groups):
                spot = slice(k * rows + which * span, k * rows + (which + 1) * span)
                first, second = received(pair, k * span), received(pair + 1, k * span)
                grads[spot, start : start + 128] = (
                    left_pair(first, second) * HEAD_DIM ** (-0.5)
                ).astype(BF16)
                grads[spot, width_here + start : width_here + start + 128] = right_pair(
                    first, second
                ).astype(BF16)
                inner = block_rows + k % half_parts * span
                first, second = received(pair, inner), received(pair + 1, inner)
                grads[spot, 2 * width_here + start : 2 * width_here + start + 128] = (
                    left_pair(first, second) if k < half_parts else right_pair(first, second)
                ).astype(BF16)
    back = matmul_nt(grads[...], mat_ref[...])
    own_ref[...] = back[:rows]
    for k in range(1, groups):
        others_ref[k - 1] = back[k * rows : (k + 1) * rows].astype(BF16)
    mat_grads[...] = matmul_tn(all_ref[...], grads[...])
    query_sums = jnp.sum(grads[:, :width_here].astype(F32), axis=0, keepdims=True)
    value_sums = jnp.sum(grads[:, 2 * width_here :].astype(F32), axis=0, keepdims=True)
    chunks = blocks // groups
    chunk = width_here // chunks
    row = lax.broadcasted_iota(jnp.int32, (16, 128), 0)
    for k in range(blocks):
        owner = my_block ^ k
        spot = pl.ds(pl.multiple_of(owner * chip_rows, chip_rows), chip_rows)
        block = mat_grads[spot, :]
        sums = []
        for total in (query_sums, value_sums):
            chosen = jnp.zeros((1, chunk), F32)
            for i in range(chunks):
                piece = total[:, i * chunk : (i + 1) * chunk]
                chosen = chosen + jnp.where(owner == my_group * chunks + i, piece, 0.0)
            sums.append(jnp.concatenate([chosen, jnp.zeros((1, 128 - chunk), F32)], axis=1) if chunk < 128 else chosen)
        if k % 2 == 0:
            keep_ref[k // 2, 0:chip_rows, :] = block
        else:
            send_ref[k // 2, 0:chip_rows, :] = block.astype(BF16)
        for i in range(3 * width_here // 128):
            value = jnp.where(row == 0, sums[i], 0.0) if i < 2 else jnp.zeros((16, 128), F32)
            columns = slice(i * 128, (i + 1) * 128)
            if k % 2 == 0:
                keep_ref[k // 2, chip_rows : chip_rows + 16, columns] = value
            else:
                send_ref[k // 2, chip_rows : chip_rows + 16, columns] = value.astype(BF16)


def input_grads(spot, got, mat_three, token_all, heads_here, groups, repeats):
    blocks = got.shape[0]
    total_rows, width = token_all.shape
    rows = total_rows // groups
    chip_rows = width // blocks
    columns = mat_three.shape[1]
    vmem = pl.BlockSpec(memory_space=pltpu.VMEM)
    shape = (blocks // 2, chip_rows + 16, columns)
    return pl.pallas_call(
        functools.partial(input_kernel, groups, heads_here, repeats),
        in_specs=[pl.BlockSpec(memory_space=pltpu.SMEM)] + [vmem] * 3,
        out_specs=[vmem] * 4,
        out_shape=[
            jax.ShapeDtypeStruct((rows, width), F32),
            jax.ShapeDtypeStruct((groups - 1, rows, width), BF16),
            jax.ShapeDtypeStruct(shape, F32),
            jax.ShapeDtypeStruct(shape, BF16),
        ],
        scratch_shapes=[
            pltpu.VMEM((total_rows, columns), BF16),
            pltpu.VMEM((width, columns), F32),
        ],
        compiler_params=pltpu.CompilerParams(vmem_limit_bytes=40 * 1024 * 1024),
    )(spot, got, mat_three, token_all)


def whole_call(kernel, out_shape, arguments, scratch=(), megabytes=40):
    vmem = pl.BlockSpec(memory_space=pltpu.VMEM)
    return pl.pallas_call(
        kernel,
        in_specs=[vmem] * len(arguments),
        out_specs=[vmem] * len(out_shape),
        out_shape=out_shape,
        scratch_shapes=list(scratch),
        compiler_params=pltpu.CompilerParams(vmem_limit_bytes=megabytes * 1024 * 1024),
    )(*arguments)


def ffn_kernel(sent_ref, up_ref, down_ref, bias_ref, out_ref, act_ref, slope_ref):
    hidden = matmul(sent_ref[:, : up_ref.shape[0]], up_ref[...]) + bias_ref[...]
    cdf_part = 0.5 * (1.0 + lax.erf(hidden * 0.7071067811865476))
    act = (hidden * cdf_part).astype(BF16)
    act_ref[...] = act
    slope_ref[...] = cdf_part + hidden * (
        jnp.exp(-0.5 * hidden * hidden) * 0.3989422804014327
    )
    out_ref[...] = matmul(act, down_ref[...]).astype(out_ref.dtype)


def ffn_part(sent, mat_up, mat_down, vec_up, kind):
    rows = sent.shape[0]
    units, width = mat_down.shape
    return whole_call(
        ffn_kernel,
        [
            jax.ShapeDtypeStruct((rows, width), kind),
            jax.ShapeDtypeStruct((rows, units), BF16),
            jax.ShapeDtypeStruct((rows, units), F32),
        ],
        (sent, mat_up, mat_down, vec_up),
    )


def ffn_back_kernel(grad_ref, slope_ref, up_ref, down_ref, out_ref, hidden_ref):
    grad_hidden = (matmul_nt(grad_ref[...], down_ref[...]) * slope_ref[...]).astype(BF16)
    hidden_ref[...] = grad_hidden
    out_ref[...] = matmul_nt(grad_hidden, up_ref[...]).astype(out_ref.dtype)


def ffn_back_part(grad, slope, mat_up, mat_down, kind):
    rows, width = grad.shape
    return whole_call(
        ffn_back_kernel,
        [
            jax.ShapeDtypeStruct((rows, width), kind),
            jax.ShapeDtypeStruct(slope.shape, BF16),
        ],
        (grad, slope, mat_up, mat_down),
    )


def ffn_grads_kernel(groups, blocks, *refs):
    acts, grads, sents, hiddens = [refs[i * groups : (i + 1) * groups] for i in range(4)]
    *outs, sums_ref, left, right = refs[4 * groups :]
    rows, width = grads[0].shape
    units = acts[0].shape[1]
    for k in range(groups):
        spot = slice(k * rows, (k + 1) * rows)
        left[spot, 0:units] = acts[k][...]
        right[spot, 0:width] = grads[k][...]
    result = matmul_tn(left[:, 0:units], right[:, 0:width])
    chunk = units // blocks
    for b in range(blocks):
        outs[0][b, 0:chunk, :] = result[b * chunk : (b + 1) * chunk].astype(BF16)
    for k in range(groups):
        spot = slice(k * rows, (k + 1) * rows)
        left[spot, 0:width] = sents[k][:, 0:width]
        right[spot, 0:units] = hiddens[k][...]
    result = matmul_tn(left[:, 0:width], right[:, 0:units])
    chunk = width // blocks
    for b in range(blocks):
        block = result[b * chunk : (b + 1) * chunk].astype(BF16)
        if len(outs) == 1:
            outs[0][b, units // blocks :, :] = block
        else:
            outs[1][b] = block
    sums_ref[...] = jnp.sum(right[:, 0:units].astype(F32), axis=0, keepdims=True)


def ffn_grads_call(acts, grads, sents, hiddens, blocks):
    groups = len(acts)
    rows, width = grads[0].shape
    units = acts[0].shape[1]
    big = pltpu.VMEM((groups * rows, max(units, width)), BF16)
    if units == width:
        shapes = [jax.ShapeDtypeStruct((blocks, (units + width) // blocks, width), BF16)]
    else:
        shapes = [
            jax.ShapeDtypeStruct((blocks, units // blocks, width), BF16),
            jax.ShapeDtypeStruct((blocks, width // blocks, units), BF16),
        ]
    return whole_call(
        functools.partial(ffn_grads_kernel, groups, blocks),
        shapes + [jax.ShapeDtypeStruct((1, units), F32)],
        (*acts, *grads, *sents, *hiddens),
        (big, big),
    )


def split_kernel(own_ref, *outs):
    groups = own_ref.shape[0]
    dim_rows = outs[0].shape[0]
    columns = own_ref.shape[2] // 3
    total = jnp.zeros(outs[3].shape, F32)
    for group in range(groups):
        block = own_ref[group].astype(F32)
        for which in range(3):
            outs[which][:, group * columns : (group + 1) * columns] = block[
                :dim_rows, which * columns : (which + 1) * columns
            ]
        total = total + block[dim_rows : dim_rows + 8, 0:128]
    outs[3][...] = total


def split_columns(own, dim_rows):
    groups, _, columns = own.shape
    matrix = jax.ShapeDtypeStruct((dim_rows, groups * columns // 3), F32)
    return whole_call(split_kernel, [matrix] * 3 + [jax.ShapeDtypeStruct((8, 128), F32)], (own,))


def place_kernel(groups, blocks, spot_ref, *refs):
    parts, out_ref = refs[:groups], refs[groups]
    chunk = parts[0].shape[1] // blocks
    for k in range(groups):
        for group in range(groups):

            @pl.when((spot_ref[1] ^ k) == group)
            def _():
                for b in range(blocks):
                    start = (b * groups + group) * chunk
                    out_ref[:, start : start + chunk] = parts[k][
                        :, b * chunk : (b + 1) * chunk
                    ].astype(F32)


def place_columns(spot, parts, blocks):
    groups = len(parts)
    rows, columns = parts[0].shape
    chunk = columns // blocks
    if chunk % 128:
        whole = xor_order(jnp.stack(parts), 0, spot[1]).reshape(groups, rows, blocks, chunk)
        return jnp.transpose(whole, (1, 2, 0, 3)).reshape(rows, groups * columns).astype(F32)
    vmem = pl.BlockSpec(memory_space=pltpu.VMEM)
    return pl.pallas_call(
        functools.partial(place_kernel, groups, blocks),
        in_specs=[pl.BlockSpec(memory_space=pltpu.SMEM)] + [vmem] * groups,
        out_specs=vmem,
        out_shape=jax.ShapeDtypeStruct((rows, groups * columns), F32),
    )(spot, *parts)


def out_grads_kernel(groups, *refs):
    sents, grads, (out_ref, left, right) = refs[:groups], refs[groups : 2 * groups], refs[2 * groups :]
    rows, width = grads[0].shape
    for k in range(groups):
        spot = slice(k * rows, (k + 1) * rows)
        left[spot, :] = sents[k][:, width:]
        right[spot, :] = grads[k][...]
    out_ref[...] = matmul_tn(left[...], right[...]).astype(BF16)


def out_grads_call(sents, grads):
    groups = len(sents)
    rows, width = grads[0].shape
    columns = sents[0].shape[1] - width
    return whole_call(
        functools.partial(out_grads_kernel, groups),
        [jax.ShapeDtypeStruct((columns, width), BF16)],
        (*sents, *grads),
        (
            pltpu.VMEM((groups * rows, columns), BF16),
            pltpu.VMEM((groups * rows, width), BF16),
        ),
    )[0]


def per_device(
    tokens,
    cotangent,
    doc_offsets,
    valid_flags,
    w_query,
    w_key,
    w_value,
    w_out,
    w_fc1,
    w_fc2,
    b_query,
    b_value,
    b_out,
    b_fc1,
    b_fc2,
    gain_attn,
    bias_attn,
    gain_ffn,
    bias_ffn,
):
    seqs, span, width = tokens.shape
    groups = lax.axis_size("heads")
    blocks = lax.axis_size("blk")
    devices = groups * blocks
    my_group = lax.axis_index("heads")
    my_block = lax.axis_index("blk")
    rows = seqs * span
    block_rows = span * groups
    length = block_rows * blocks
    heads = width // HEAD_DIM
    heads_here = heads // groups
    pairs = seqs * heads_here
    repeats = blocks // pairs
    parts_length = length // repeats
    width_here = heads_here * HEAD_DIM
    dim_rows = w_query.shape[0]
    unit_rows = w_fc2.shape[0]
    hidden_size = w_fc1.shape[1]
    units_here = hidden_size // groups
    qk_scale = HEAD_DIM ** (-0.5)
    half = block_rows // 2
    wide = span // 2

    token_rows = tokens.reshape(rows, width)
    token_parts = gather_parts(token_rows, "heads")
    w_three = jnp.concatenate(
        [w.reshape(dim_rows, groups, width_here) for w in (w_query, w_key, w_value)], axis=-1
    )
    w_three = jnp.transpose(w_three, (1, 0, 2))
    short = [b_query, b_value, b_out, b_fc2, gain_attn, bias_attn, gain_ffn, bias_ffn, b_fc1]
    vectors = whole_call(
        pack_kernel,
        [jax.ShapeDtypeStruct((dim_rows, 128), BF16)],
        [item[None] for item in short],
    )[0]
    w_up = w_fc1.reshape(dim_rows, blocks, groups, unit_rows)
    w_up = jnp.transpose(w_up, (2, 0, 1, 3)).reshape(groups, dim_rows, units_here)
    first = jnp.concatenate(
        [w_three, jnp.broadcast_to(vectors[None], (groups,) + vectors.shape), w_up], axis=-1
    )
    first = lax.all_to_all(first, "heads", split_axis=0, concat_axis=0, tiled=True)
    first = first.reshape(groups * dim_rows, first.shape[-1])
    second = first[:, 3 * width_here + 128 :].reshape(-1, width)
    second = jnp.concatenate([second, w_fc2])
    mat_out = lax.all_gather(w_out, ALL, axis=0, tiled=True)

    first = first[:, : 3 * width_here + 128]
    for part in token_parts[1:]:
        second = after(second, part)
    mine, other = gather_blk_parts(first, second)
    part_blocks = blocks // repeats
    first_turn = my_block % repeats * (parts_length // QUERY_ROWS)
    spot = jnp.stack([my_block, my_group, first_turn, my_block // part_blocks]).astype(jnp.int32)
    sent, token_all, mat_three, short = project(
        spot, token_parts, mine, other, seqs, heads_here, repeats
    )
    qkv = lax.all_to_all(sent, "blk", split_axis=0, concat_axis=0, tiled=True)


    vectors = short.reshape(devices, 8 * 128)
    vec_up = vectors[:, 8 * dim_rows : 8 * dim_rows + unit_rows].reshape(blocks, groups, unit_rows)
    vec_up = lax.dynamic_index_in_dim(vec_up, my_group, 1, False).reshape(units_here)
    short = vectors[:, 2 * dim_rows : 8 * dim_rows].reshape(devices, 6, dim_rows)
    short = jnp.transpose(short, (1, 0, 2)).reshape(6, width)
    vec_out, vec_down, gain_one, bias_one, gain_two, bias_two = [short[i] for i in range(6)]

    second = lax.all_gather(after(second, qkv), "blk", axis=0, tiled=False)
    up_rows = groups * dim_rows * units_here // width
    mat_up = second[:, :up_rows].reshape(width, units_here)
    mat_down = second[:, up_rows:].reshape(units_here, width)

    my_pair = my_block // repeats
    my_part = my_block % repeats
    my_seq = my_pair // heads_here
    inner = jnp.arange(length, dtype=jnp.int32)
    place = (inner // block_rows) * block_rows + inner % span
    place = place + (((inner // span) % groups) ^ my_group) * span
    offsets = lax.dynamic_index_in_dim(doc_offsets, my_seq, 0, False)
    flags = lax.dynamic_index_in_dim(valid_flags, my_seq, 0, False)
    flags = xor_order(flags.reshape(blocks, groups, span), 1, my_group).reshape(length)
    segment = jnp.sum((offsets[None, :] <= place[:, None]).astype(jnp.int32), axis=1) - 1
    seg_row = segment.reshape(length // QUERY_ROWS, 1, QUERY_ROWS)
    seg_key = jnp.where(flags > 0, segment, -1)
    seg_key = jnp.broadcast_to(seg_key[:, None], (length, 128))
    attn_low, attn_t, lse = attend(spot, seg_row, seg_key, qkv, wide, parts_length)

    sent = jnp.concatenate([attn_low] * repeats, axis=0) if repeats > 1 else attn_low
    got = lax.all_to_all(sent, ALL, split_axis=0, concat_axis=0, tiled=True)
    my_span = my_block * groups + my_group
    local_flags = lax.dynamic_slice_in_dim(valid_flags, my_span * span, span, 1)
    local_flags = local_flags.reshape(rows, 1).astype(F32)
    *sent, normed_one, unit_one, inv_one, squares = join(
        spot, got, token_rows, local_flags, mat_out, short, seqs, heads_here, repeats
    )
    joint_parts = [sent[0]] + [swapped(sent[k], "heads", k) for k in range(1, groups)]
    ffn_results = [
        ffn_part(part, mat_up, mat_down, vec_up[None], F32 if k == 0 else BF16)
        for k, part in enumerate(joint_parts)
    ]
    ffn_others = [swapped(ffn_results[k][0], "heads", k) for k in range(1, groups)]
    output, grad_resid_two, grad_ffn, early, squares = middle(
        ffn_results[0][0], ffn_others, normed_one, short, local_flags,
        cotangent.reshape(rows, width), squares,
    )
    output = output.reshape(tokens.shape)
    grad_ffn_parts = gather_parts(grad_ffn, "heads")
    grad_results = [
        ffn_back_part(part, item[2], mat_up, mat_down, F32 if k == 0 else BF16)
        for k, (part, item) in enumerate(zip(grad_ffn_parts, ffn_results))
    ]
    grad_normed_parts = [item[0] for item in grad_results]
    grad_normed_others = [swapped(grad_normed_parts[k], "heads", k) for k in range(1, groups)]
    *ffn_grads, grad_vec_up = ffn_grads_call(
        [item[1] for item in ffn_results],
        grad_ffn_parts,
        joint_parts,
        [after(grad_results[0][1], grad_normed_others[-1])] + [item[1] for item in grad_results[1:]],
        blocks,
    )
    ffn_grads = [
        lax.psum_scatter(
            item.reshape(-1, item.shape[-1]), "blk", scatter_dimension=0, tiled=True
        )
        for item in ffn_grads
    ]
    if units_here == width:
        shard_down, shard_up = ffn_grads[0][:unit_rows], ffn_grads[0][unit_rows:]
    else:
        shard_down, shard_up = ffn_grads
    shard_down = shard_down.astype(F32)

    sent, grad_resid_one, grad_branch = branch_back(
        spot, grad_normed_parts[0], grad_normed_others, grad_resid_two, unit_one, inv_one,
        gain_one[None], mat_out, early,
        grad_vec_up, squares, seqs, heads_here, repeats, devices,
    )
    got = lax.all_to_all(sent, ALL, split_axis=0, concat_axis=0, tiled=True)
    small = jnp.sum(got[:, wide:].astype(F32), axis=0)
    small = small[:8] + small[8:]
    vector_sums = lax.dynamic_slice_in_dim(small[:6], my_span * dim_rows % 128, dim_rows, 1)
    shard_vec_up = lax.dynamic_slice_in_dim(small[6], my_block * unit_rows % 128, unit_rows, 0)
    real_count = jnp.maximum(jnp.sum(valid_flags.astype(F32)), 1.0)
    rms = jnp.sqrt(small[7, :4] / (real_count * width))

    grads = attend_back(spot, seg_row, seg_key, qkv, got, attn_t, lse)
    branch_parts = gather_parts(after(grad_branch, grads), "heads")
    grad_mat_out = out_grads_call(joint_parts, branch_parts)
    got = lax.all_to_all(grads, "blk", split_axis=0, concat_axis=0, tiled=True)
    shard_up = after(shard_up, grads).reshape(groups, dim_rows, units_here)
    shard_up = xor_order(shard_up, 0, my_group)
    up_parts = [shard_up[0]] + [swapped(shard_up[k], "heads", k) for k in range(1, groups)]
    for part in up_parts[1:]:
        got = after(got, part)
    shard_out = scatter_blk(after(grad_mat_out, got).reshape(blocks, dim_rows, width)).astype(BF16)
    route = [(j, j % groups * blocks + j // groups) for j in range(devices)]
    shard_out = lax.ppermute(shard_out, ("heads", "blk"), route)
    own_input, other_input, keep, send = input_grads(
        spot, got, mat_three, token_all, heads_here, groups, repeats
    )
    grad_input = grad_resid_one + own_input
    for k in range(1, groups):
        grad_input = grad_input + swapped(other_input[k - 1], "heads", k).astype(F32)
    grad_input = grad_input.reshape(tokens.shape)
    chip_sums = keep + swapped(send, "blk", 1).astype(F32)
    chip_low = chip_sums.astype(BF16)
    three_grads = chip_sums[0]
    for k in range(1, blocks // 2):
        three_grads = three_grads + swapped(chip_low[k], "blk", 2 * k).astype(F32)
    own_rows = three_grads[: groups * dim_rows].reshape(groups, dim_rows, 3 * width_here)
    own_sums = three_grads[groups * dim_rows, :256].reshape(2, 128)[:, : groups * dim_rows]
    own_sums = jnp.transpose(own_sums.reshape(2, groups, dim_rows), (1, 0, 2))
    row = lax.broadcasted_iota(jnp.int32, (1, 16, 1), 1)
    own_sums = jnp.concatenate(
        [
            own_sums.reshape(groups, 2 * dim_rows),
            jnp.zeros((groups, 3 * width_here - 2 * dim_rows), F32),
        ],
        axis=1,
    )
    own_sums = jnp.where(row == 0, own_sums[:, None, :], 0.0)
    own = jnp.concatenate([own_rows, own_sums], axis=1).astype(BF16)
    shard_up = place_columns(after(spot, own), up_parts, blocks)
    own = lax.all_to_all(own, "heads", split_axis=0, concat_axis=0, tiled=True)
    shards_three = split_columns(own, dim_rows)
    shard_sums = shards_three[3][0]

    return (
        output,
        grad_input,
        shards_three[0],
        shards_three[1],
        shards_three[2],
        shard_out.astype(F32),
        shard_up,
        shard_down,
        shard_sums[:dim_rows],
        shard_sums[dim_rows : 2 * dim_rows],
        vector_sums[0],
        shard_vec_up,
        vector_sums[3],
        vector_sums[1],
        vector_sums[2],
        vector_sums[4],
        vector_sums[5],
        rms,
    )


def solution(mesh):
    token_spec = P(None, ALL, None)
    matrix_spec = P(ALL, None)
    vector_spec = P(ALL)
    return jax.shard_map(
        per_device,
        mesh=mesh,
        in_specs=(token_spec,) * 2 + (P(),) * 2 + (matrix_spec,) * 6 + (vector_spec,) * 9,
        out_specs=(token_spec,) * 2 + (matrix_spec,) * 6 + (vector_spec,) * 9 + (P(),),
        check_vma=False,
    )
```

```python
import functools

import jax
import jax.numpy as jnp
from jax import lax
from jax.experimental import pallas as pl
from jax.experimental.pallas import tpu as pltpu
from jax.sharding import PartitionSpec as P

HEAD_DIM = 64
NORM_EPS = 1e-05
NEG_LARGE = -1e30
QUERY_ROWS = 256
BF16 = jnp.bfloat16
F32 = jnp.float32
ALL = ("blk", "heads")


def vmem_limit(length):
    return 8 * 1024 * 1024 + 6 * 1024 * length


def matmul(left, right):
    return jnp.dot(left, right, preferred_element_type=F32)


def matmul_tn(left, right):
    return lax.dot_general(left, right, (((0,), (0,)), ((), ())), preferred_element_type=F32)


def matmul_nt(left, right):
    return lax.dot_general(left, right, (((1,), (1,)), ((), ())), preferred_element_type=F32)


def after(block, other):
    spot = lax.slice(other, (0,) * other.ndim, (1,) * other.ndim).reshape(())
    return block + (spot * 0).astype(block.dtype)


def swapped(block, axis, mask):
    count = lax.axis_size(axis)
    return lax.ppermute(block, axis, [(i, i ^ mask) for i in range(count)])


def gather_parts(block, axis):
    return [block] + [swapped(block, axis, k) for k in range(1, lax.axis_size(axis))]


def scatter_parts(parts, axis):
    total = parts[0].astype(F32)
    for k in range(1, len(parts)):
        total = total + swapped(parts[k].astype(BF16), axis, k).astype(F32)
    return total


def xor_order(array, dim, index):
    pieces = [
        lax.dynamic_index_in_dim(array, index ^ k, dim, True) for k in range(array.shape[dim])
    ]
    return jnp.concatenate(pieces, axis=dim)


def gather_blk_parts(block, first_needs):
    count = lax.axis_size("blk")
    mine = jnp.stack([block] + [swapped(block, "blk", k) for k in range(2, count, 2)])
    mine = after(mine, first_needs)
    return mine, swapped(mine, "blk", 1)


def gather_blk(block, first_needs):
    mine, other = gather_blk_parts(block, first_needs)
    both = jnp.stack([mine, other], axis=1).reshape((-1,) + block.shape)
    return xor_order(both, 0, lax.axis_index("blk"))


def scatter_blk(blocks):
    index = lax.axis_index("blk")
    ordered = xor_order(blocks, 0, index)
    pairs = ordered.reshape((ordered.shape[0] // 2, 2) + ordered.shape[1:])
    total = pairs[:, 0].astype(F32) + swapped(pairs[:, 1], "blk", 1).astype(F32)
    low = total.astype(BF16)
    result = total[0]
    for k in range(1, low.shape[0]):
        result = result + swapped(low[k], "blk", 2 * k).astype(F32)
    return result


def layer_norm(resid, norm_gain, norm_bias):
    center = resid - jnp.mean(resid, axis=-1, keepdims=True)
    inv_std = lax.rsqrt(jnp.mean(center * center, axis=-1, keepdims=True) + NORM_EPS)
    normed = center * inv_std
    return (normed * norm_gain + norm_bias, normed, inv_std)


def norm_back(upstream, normed, inv_std, norm_gain):
    scaled = upstream * norm_gain
    return inv_std * (
        scaled
        - jnp.mean(scaled, axis=-1, keepdims=True)
        - normed * jnp.mean(scaled * normed, axis=-1, keepdims=True)
    )


def gelu_slope(hidden):
    cdf_part = 0.5 * (1.0 + lax.erf(hidden * 0.7071067811865476))
    pdf_part = jnp.exp(-0.5 * hidden * hidden) * 0.3989422804014327
    return cdf_part + hidden * pdf_part


def two_halves(values):
    high = lax.reduce_precision(values, 8, 7)
    return jnp.stack([high, values - high], axis=-1).astype(BF16)


def left_lanes(block):
    lane = lax.broadcasted_iota(jnp.int32, block.shape, 1)
    return jnp.where(lane < HEAD_DIM, block, 0.0)


def masked_scores(seg_key, seg_query, scores):
    width = scores.shape[1] // seg_key.shape[1]
    same = jnp.concatenate([seg_key] * width, axis=1) == seg_query
    return jnp.where(same, scores, NEG_LARGE)


def own_scores(seg_key, seg_query, scores):
    width = scores.shape[1] // seg_key.shape[1]
    same = jnp.concatenate([seg_key] * width, axis=1) == seg_query
    rows = lax.broadcasted_iota(jnp.int32, scores.shape, 0)
    columns = lax.broadcasted_iota(jnp.int32, scores.shape, 1)
    return jnp.where(same | (rows == columns), scores, NEG_LARGE)


def score_all(turn, seg_query, seg_key_ref, qkv_ref, query_t, scores):
    sources, rows = qkv_ref.shape[0], (qkv_ref.shape[1] - 16) * 2 // 3
    per_source = rows // QUERY_ROWS
    query_now = query_t[turn]
    for b in range(sources):
        spot = slice(b * rows, (b + 1) * rows)
        scores[spot, :] = masked_scores(
            seg_key_ref[spot, :], seg_query, matmul(qkv_ref[b, 0:rows, :], query_now)
        )
    own = pl.ds(pl.multiple_of(turn * QUERY_ROWS, QUERY_ROWS), QUERY_ROWS)
    inner = pl.ds(pl.multiple_of(turn % per_source * QUERY_ROWS, QUERY_ROWS), QUERY_ROWS)
    own_pair = qkv_ref[turn // per_source, inner, :]
    scores[own, :] = own_scores(seg_key_ref[own, :], seg_query, matmul(own_pair, query_now))
    return own, own_pair


def turn_queries(b, turned, query_t):
    per_source = turned.shape[1] // QUERY_ROWS
    low = jnp.concatenate([jnp.zeros_like(turned[0:HEAD_DIM]), turned[0:HEAD_DIM]], axis=0)
    for t in range(per_source):
        spot = slice(t * QUERY_ROWS, (t + 1) * QUERY_ROWS)
        query_t[b * per_source + t] = low[:, spot].astype(BF16)


def attend_kernel(
    spot_ref, seg_row_ref, seg_key_ref, qkv_ref, low_ref, attn_ref, lse_ref,
    query_t, values_t, scores,
):
    step = pl.program_id(0)
    sources, rows = qkv_ref.shape[0], (qkv_ref.shape[1] - 16) * 2 // 3
    half = rows // 2

    @pl.when(step == 0)
    def _():
        for b in range(sources):
            turn_queries(b, qkv_ref[b, 0:rows, :].astype(F32).T, query_t)
            turned = qkv_ref[b, rows : rows + half, :].astype(F32).T
            values_t[:, b * rows : b * rows + half] = turned[0:HEAD_DIM].astype(BF16)
            values_t[:, b * rows + half : (b + 1) * rows] = turned[
                HEAD_DIM : 2 * HEAD_DIM
            ].astype(BF16)

    turn = spot_ref[2] + step
    score_all(turn, seg_row_ref[0], seg_key_ref, qkv_ref, query_t, scores)
    top = jnp.max(scores[...], axis=0, keepdims=True)
    total = jnp.zeros_like(top)
    result = jnp.zeros((HEAD_DIM, QUERY_ROWS), F32)
    for b in range(sources):
        spot = slice(b * rows, (b + 1) * rows)
        probs = jnp.exp(scores[spot, :] - top)
        total = total + jnp.sum(probs, axis=0, keepdims=True)
        result = result + matmul(values_t[:, spot], probs.astype(BF16))
    result = result / total
    attn_ref[...] = result
    lse_ref[0] = top + jnp.log(total)
    turned = result.T
    wide = low_ref.shape[1]
    spans = QUERY_ROWS // (2 * wide)
    first = turn % (rows // QUERY_ROWS) * spans
    for t in range(spans):
        left = turned[2 * t * wide : (2 * t + 1) * wide]
        right = turned[(2 * t + 1) * wide : (2 * t + 2) * wide]
        low_ref[spot_ref[1] ^ (first + t)] = jnp.concatenate([left, right], axis=1).astype(BF16)


def attend(spot, seg_row, seg_key, qkv, wide, query_length):
    sources, rows = qkv.shape[0], (qkv.shape[1] - 16) * 2 // 3
    length = sources * rows
    steps = query_length // QUERY_ROWS
    spans = rows // (2 * wide)
    per_source = rows // QUERY_ROWS
    return pl.pallas_call(
        attend_kernel,
        grid_spec=pltpu.PrefetchScalarGridSpec(
            num_scalar_prefetch=1,
            grid=(steps,),
            in_specs=[
                pl.BlockSpec((1, 1, QUERY_ROWS), lambda i, spot: (spot[2] + i, 0, 0)),
                pl.BlockSpec(seg_key.shape, lambda i, spot: (0, 0)),
                pl.BlockSpec(qkv.shape, lambda i, spot: (0, 0, 0)),
            ],
            out_specs=[
                pl.BlockSpec((spans, wide, 128), lambda i, spot: (i // per_source, 0, 0)),
                pl.BlockSpec((HEAD_DIM, QUERY_ROWS), lambda i, spot: (0, i)),
                pl.BlockSpec((1, 1, QUERY_ROWS), lambda i, spot: (i, 0, 0)),
            ],
            scratch_shapes=[
                pltpu.VMEM((length // QUERY_ROWS, 128, QUERY_ROWS), BF16),
                pltpu.VMEM((HEAD_DIM, length), BF16),
                pltpu.VMEM((length, QUERY_ROWS), F32),
            ],
        ),
        out_shape=[
            jax.ShapeDtypeStruct((steps // per_source * spans, wide, 128), BF16),
            jax.ShapeDtypeStruct((HEAD_DIM, query_length), F32),
            jax.ShapeDtypeStruct((steps, 1, QUERY_ROWS), F32),
        ],
        compiler_params=pltpu.CompilerParams(vmem_limit_bytes=vmem_limit(length)),
    )(spot, seg_row, seg_key, qkv)


def attend_back_kernel(
    spot_ref, seg_row_ref, seg_key_ref, qkv_ref, up_ref, attn_ref, lse_ref, grads_ref,
    query_t, keys_t, values, scores, grad_query, grad_key, grad_value,
):
    step = pl.program_id(0)
    sources, rows = qkv_ref.shape[0], (qkv_ref.shape[1] - 16) * 2 // 3
    half = rows // 2
    lane = lax.broadcasted_iota(jnp.int32, (rows, 128), 1)

    @pl.when(step == 0)
    def _():
        for b in range(sources):
            turned = qkv_ref[b, 0:rows, :].astype(F32).T
            turn_queries(b, turned, query_t)
            keys_t[:, b * rows : (b + 1) * rows] = turned[HEAD_DIM : 2 * HEAD_DIM].astype(BF16)
            packed = qkv_ref[b, rows : rows + half, :].astype(F32)
            values[b * rows : b * rows + half, :] = left_lanes(packed).astype(BF16)
            values[b * rows + half : (b + 1) * rows, :] = left_lanes(
                pltpu.roll(packed, HEAD_DIM, 1)
            ).astype(BF16)
        grad_query[...] = jnp.zeros_like(grad_query)
        grad_key[...] = jnp.zeros_like(grad_key)
        grad_value[...] = jnp.zeros_like(grad_value)

    turn = spot_ref[2] + step
    lse = lse_ref[0]
    pieces = []
    spans = QUERY_ROWS // (rows // up_ref.shape[0])
    first = turn % (rows // QUERY_ROWS) * spans
    for t in range(spans):
        packed = up_ref[spot_ref[1] ^ (first + t), 0 : rows // up_ref.shape[0] // 2, :].astype(F32)
        pieces.append(left_lanes(packed))
        pieces.append(left_lanes(pltpu.roll(packed, HEAD_DIM, 1)))
    up_now = jnp.concatenate(pieces, axis=0)
    up_turned = up_now.T
    delta = jnp.sum(up_turned[0:HEAD_DIM] * attn_ref[...], axis=0, keepdims=True)
    up_now = up_now.astype(BF16)
    up_turned = up_turned.astype(BF16)
    own, own_pair = score_all(turn, seg_row_ref[0], seg_key_ref, qkv_ref, query_t, scores)
    query_now = pltpu.roll(own_pair.astype(F32), HEAD_DIM, 1).astype(BF16)
    result = jnp.zeros((HEAD_DIM, QUERY_ROWS), F32)
    for b in range(sources):
        spot = slice(b * rows, (b + 1) * rows)
        probs = jnp.exp(scores[spot, :] - lse)
        grad_probs = matmul(values[spot, :], up_turned)
        grad_scores = (probs * (grad_probs - delta)).astype(BF16)
        grad_value[spot, :] += matmul(probs.astype(BF16), up_now)
        grad_key[spot, :] += matmul(grad_scores, query_now)
        result = result + matmul(keys_t[:, spot], grad_scores)
    grad_query[own, :] = jnp.concatenate([result, jnp.zeros_like(result)], axis=0).T

    @pl.when(step == pl.num_programs(0) - 1)
    def _():
        for b in range(sources):
            spot = slice(b * rows, (b + 1) * rows)
            grads_ref[b, 0:rows, :] = jnp.where(
                lane < HEAD_DIM, grad_query[spot, :], grad_key[spot, :]
            ).astype(BF16)
            upper = grad_value[b * rows : b * rows + half, :]
            lower = grad_value[b * rows + half : (b + 1) * rows, :]
            grads_ref[b, rows : rows + half, :] = (
                upper + pltpu.roll(lower, HEAD_DIM, 1)
            ).astype(BF16)


def attend_back(spot, seg_row, seg_key, qkv, upstream, attn_t, lse):
    sources, rows = qkv.shape[0], (qkv.shape[1] - 16) * 2 // 3
    length = sources * rows
    steps = lse.shape[0]
    groups = upstream.shape[0] // sources
    per_source = rows // QUERY_ROWS
    return pl.pallas_call(
        attend_back_kernel,
        grid_spec=pltpu.PrefetchScalarGridSpec(
            num_scalar_prefetch=1,
            grid=(steps,),
            in_specs=[
                pl.BlockSpec((1, 1, QUERY_ROWS), lambda i, spot: (spot[2] + i, 0, 0)),
                pl.BlockSpec(seg_key.shape, lambda i, spot: (0, 0)),
                pl.BlockSpec(qkv.shape, lambda i, spot: (0, 0, 0)),
                pl.BlockSpec(
                    (groups,) + upstream.shape[1:],
                    lambda i, spot: ((spot[2] + i) // per_source, 0, 0),
                ),
                pl.BlockSpec((HEAD_DIM, QUERY_ROWS), lambda i, spot: (0, i)),
                pl.BlockSpec((1, 1, QUERY_ROWS), lambda i, spot: (i, 0, 0)),
            ],
            out_specs=pl.BlockSpec(
                (sources, rows * 3 // 2, 128), lambda i, spot: (0, 0, 0)
            ),
            scratch_shapes=[
                pltpu.VMEM((length // QUERY_ROWS, 128, QUERY_ROWS), BF16),
                pltpu.VMEM((HEAD_DIM, length), BF16),
                pltpu.VMEM((length, 128), BF16),
                pltpu.VMEM((length, QUERY_ROWS), F32),
                pltpu.VMEM((length, 128), F32),
                pltpu.VMEM((length, 128), F32),
                pltpu.VMEM((length, 128), F32),
            ],
        ),
        out_shape=jax.ShapeDtypeStruct((sources, rows * 3 // 2, 128), BF16),
        compiler_params=pltpu.CompilerParams(vmem_limit_bytes=vmem_limit(length)),
    )(spot, seg_row, seg_key, qkv, upstream, attn_t, lse)


def left_pair(first, second):
    lane = lax.broadcasted_iota(jnp.int32, first.shape, 1)
    return jnp.where(lane < HEAD_DIM, first, pltpu.roll(second, HEAD_DIM, 1))


def right_pair(first, second):
    lane = lax.broadcasted_iota(jnp.int32, first.shape, 1)
    return jnp.where(lane < HEAD_DIM, pltpu.roll(first, HEAD_DIM, 1), second)


def join_kernel(
    seqs, heads_here, repeats, spot_ref, got_ref, tokens_ref, flags_ref, mat_ref, vectors_ref,
    *refs,
):
    sents, (normed_ref, unit_ref, inv_ref, squares_ref, attn) = refs[:-5], refs[-5:]
    my_group, part = spot_ref[1], spot_ref[3]
    groups = len(sents)
    wide = got_ref.shape[1]
    width = tokens_ref.shape[1]
    width_here = heads_here * HEAD_DIM
    for which in range(seqs):
        for group in range(groups):
            for head in range(0, heads_here, 2):
                first, second = [
                    got_ref[
                        ((which * heads_here + i) * repeats + part) * groups + group
                    ].astype(F32)
                    for i in (head, head + 1)
                ]
                start = group * width_here + head * HEAD_DIM
                top = 2 * which * wide
                attn[top : top + wide, start : start + 128] = left_pair(first, second).astype(BF16)
                attn[top + wide : top + 2 * wide, start : start + 128] = right_pair(
                    first, second
                ).astype(BF16)
    branch = matmul(attn[...], mat_ref[...]) + vectors_ref[0:1, :]
    resid_in = tokens_ref[...].astype(F32)
    normed, unit, inv_std = layer_norm(resid_in + branch, vectors_ref[2:3, :], vectors_ref[3:4, :])
    normed_ref[...] = normed
    unit_ref[...] = unit
    inv_ref[...] = jnp.broadcast_to(inv_std, inv_ref.shape)
    low = normed.astype(BF16)
    for k in range(groups):
        sents[k][:, 0:width] = low
        for group in range(groups):

            @pl.when((my_group ^ k) == group)
            def _():
                sents[k][:, width:] = attn[:, group * width_here : (group + 1) * width_here]

    lane = lax.broadcasted_iota(jnp.int32, squares_ref.shape, 1)
    total = jnp.zeros(squares_ref.shape, F32)
    for i, item in enumerate((resid_in, branch, normed)):
        size = flags_ref[...] * jnp.sum(item * item, axis=1, keepdims=True)
        total = total + jnp.where(lane == i, jnp.sum(size, axis=0, keepdims=True), 0.0)
    squares_ref[...] = total


def join(spot, got, tokens, flags, mat_out, vectors, seqs, heads_here, repeats):
    groups = tokens.shape[1] // (heads_here * HEAD_DIM)
    rows, width = tokens.shape
    vmem = pl.BlockSpec(memory_space=pltpu.VMEM)
    return pl.pallas_call(
        functools.partial(join_kernel, seqs, heads_here, repeats),
        in_specs=[pl.BlockSpec(memory_space=pltpu.SMEM)] + [vmem] * 5,
        out_specs=[vmem] * (groups + 4),
        out_shape=[jax.ShapeDtypeStruct((rows, width + heads_here * HEAD_DIM), BF16)] * groups
        + [
            jax.ShapeDtypeStruct((rows, width), F32),
            jax.ShapeDtypeStruct((rows, width), F32),
            jax.ShapeDtypeStruct((rows, 128), F32),
            jax.ShapeDtypeStruct((1, 128), F32),
        ],
        scratch_shapes=[pltpu.VMEM((rows, width), BF16)],
        compiler_params=pltpu.CompilerParams(vmem_limit_bytes=32 * 1024 * 1024),
    )(spot, got, tokens, flags, mat_out, vectors)


def middle_kernel(others, *refs):
    own_ref, normed_ref, vectors_ref, flags_ref, up_ref, squares_ref = refs[:6]
    parts = refs[6 : 6 + others]
    out_ref, resid_ref, low_ref, early_ref, total_ref = refs[6 + others :]
    ffn = own_ref[...]
    for part in parts:
        ffn = ffn + part[...].astype(F32)
    ffn = ffn + vectors_ref[1:2, :]
    gain = vectors_ref[4:5, :]
    normed, unit, inv_std = layer_norm(normed_ref[...] + ffn, gain, vectors_ref[5:6, :])
    out_ref[...] = normed.astype(BF16)
    upstream = up_ref[...].astype(F32)
    grad_resid = norm_back(upstream, unit, inv_std, gain)
    resid_ref[...] = grad_resid
    low = grad_resid.astype(BF16)
    low_ref[...] = low
    early_ref[0:1, :] = jnp.sum(low.astype(F32), axis=0, keepdims=True)
    early_ref[1:2, :] = jnp.sum(upstream * unit, axis=0, keepdims=True)
    early_ref[2:3, :] = jnp.sum(upstream, axis=0, keepdims=True)
    size = flags_ref[...] * jnp.sum(ffn * ffn, axis=1, keepdims=True)
    lane = lax.broadcasted_iota(jnp.int32, total_ref.shape, 1)
    total_ref[...] = squares_ref[...] + jnp.where(
        lane == 3, jnp.sum(size, axis=0, keepdims=True), 0.0
    )


def middle(own, others, normed, vectors, flags, upstream, squares):
    rows, width = own.shape
    return whole_call(
        functools.partial(middle_kernel, len(others)),
        [
            jax.ShapeDtypeStruct((rows, width), BF16),
            jax.ShapeDtypeStruct((rows, width), F32),
            jax.ShapeDtypeStruct((rows, width), BF16),
            jax.ShapeDtypeStruct((8, width), F32),
            jax.ShapeDtypeStruct((1, 128), F32),
        ],
        (own, normed, vectors, flags, upstream, squares, *others),
    )


def branch_back_kernel(
    seqs, heads_here, repeats, spot_ref, *refs,
):
    (own_ref, resid_ref, unit_ref, inv_ref, gain_ref, mat_ref, early_ref, up_sums_ref,
     squares_ref), others, (sent_ref, grad_ref, low_ref) = refs[:9], refs[9:-3], refs[-3:]
    my_group = spot_ref[1]
    groups = len(others) + 1
    rows, width = own_ref.shape
    span = rows // seqs
    wide = span // 2
    devices = sent_ref.shape[0]
    blocks = devices // groups
    grad_normed = own_ref[...]
    for other in others:
        grad_normed = grad_normed + other[...].astype(F32)
    grad_normed = grad_normed + resid_ref[...]
    unit = unit_ref[...]
    grad_resid = norm_back(grad_normed, unit, inv_ref[:, 0:1], gain_ref[...])
    grad_ref[...] = grad_resid
    low = grad_resid.astype(BF16)
    low_ref[...] = low
    grad_attn = matmul_nt(low, mat_ref[...])
    for which in range(seqs):
        top = which * span
        for group in range(groups):
            for head in range(0, heads_here, 2):
                start = (group * heads_here + head) * HEAD_DIM
                upper = grad_attn[top : top + wide, start : start + 128]
                lower = grad_attn[top + wide : top + span, start : start + 128]
                blocks_two = (left_pair(upper, lower), right_pair(upper, lower))
                for i in range(2):
                    for copy in range(repeats):
                        pair = which * heads_here + head + i
                        place = (pair * repeats + copy) * groups + group
                        sent_ref[place, 0:wide, :] = blocks_two[i].astype(BF16)
    sums = [
        jnp.sum(low.astype(F32), axis=0, keepdims=True),
        jnp.sum(grad_normed * unit, axis=0, keepdims=True),
        jnp.sum(grad_normed, axis=0, keepdims=True),
    ] + [early_ref[i : i + 1, :] for i in range(3)]
    row = lax.broadcasted_iota(jnp.int32, (8, 128), 0)
    dim_rows = width // devices
    unit_rows = up_sums_ref.shape[1] // blocks
    for tile in range(width // 128):
        base = jnp.where(row == 7, squares_ref[...], 0.0)
        for i in range(6):
            base = base + jnp.where(row == i, sums[i][:, tile * 128 : (tile + 1) * 128], 0.0)
        for place in range(tile * 128 // dim_rows, (tile + 1) * 128 // dim_rows):
            start = place // groups * unit_rows // 128 * 128
            mine = jnp.where(my_group == place % groups, up_sums_ref[:, start : start + 128], 0.0)
            block = base + jnp.where(row == 6, mine, 0.0)
            high = block.astype(BF16)
            rest = block - high.astype(F32)
            sent_ref[place, wide : wide + 16, :] = jnp.concatenate(
                [high.astype(F32), rest], axis=0
            ).astype(BF16)


def branch_back(spot, own, others, resid, unit, inv_std, gain, mat_out, early, up_sums, squares,
                seqs, heads_here, repeats, devices):
    rows, width = own.shape
    vmem = pl.BlockSpec(memory_space=pltpu.VMEM)
    return pl.pallas_call(
        functools.partial(branch_back_kernel, seqs, heads_here, repeats),
        in_specs=[pl.BlockSpec(memory_space=pltpu.SMEM)] + [vmem] * (9 + len(others)),
        out_specs=[vmem] * 3,
        out_shape=[
            jax.ShapeDtypeStruct((devices, rows // seqs // 2 + 16, 128), BF16),
            jax.ShapeDtypeStruct((rows, width), F32),
            jax.ShapeDtypeStruct((rows, width), BF16),
        ],
        compiler_params=pltpu.CompilerParams(vmem_limit_bytes=32 * 1024 * 1024),
    )(spot, own, resid, unit, inv_std, gain, mat_out, early, up_sums, squares, *others)


def project_kernel(groups, heads_here, repeats, spot_ref, *refs):
    tokens, (mine_ref, other_ref, sent_ref, all_ref, mat_ref, values) = refs[:groups], refs[groups:]
    my_block, my_group = spot_ref[0], spot_ref[1]
    halves, chip_rows, _ = mine_ref.shape
    blocks = 2 * halves
    dim_rows = chip_rows // groups
    rows, width = all_ref.shape[0] // groups, all_ref.shape[1]
    width_here = heads_here * HEAD_DIM
    seqs = sent_ref.shape[0] // (repeats * heads_here)
    span = rows // seqs
    block_rows = span * groups
    each = 16 // groups
    row = lax.broadcasted_iota(jnp.int32, (16, 128), 0)
    short = jnp.zeros((16, 128), F32)
    for k in range(groups):
        all_ref[k * rows : (k + 1) * rows, :] = tokens[k][0:rows, :]
        vectors = tokens[k][rows : rows + 16, :].astype(F32)
        for i in range(each):
            piece = vectors[0:1, i * 128 : (i + 1) * 128]
            short = short + jnp.where(row == (my_group ^ k) * each + i, piece, 0.0)
    for place in range(sent_ref.shape[0]):
        sent_ref[place, block_rows * 3 // 2 :, :] = short.astype(BF16)
    for b in range(blocks):
        place = my_block ^ b
        spot = slice(b * chip_rows, (b + 1) * chip_rows)

        @pl.when(place % 2 == 0)
        def _():
            mat_ref[spot, :] = mine_ref[place // 2, :, 0 : 3 * width_here]

        @pl.when(place % 2 == 1)
        def _():
            mat_ref[spot, :] = other_ref[place // 2, :, 0 : 3 * width_here]

    lane = lax.broadcasted_iota(jnp.int32, (1, 128), 1)
    tiles = width_here // 128
    biases = [[jnp.zeros((1, 128), F32) for _ in range(tiles)] for _ in range(2)]
    for t in range(blocks):
        place = my_block ^ (my_group * (blocks // groups) + t // groups)
        piece = jnp.where(
            place % 2 == 0,
            mine_ref[place // 2, :, 3 * width_here :].astype(F32),
            other_ref[place // 2, :, 3 * width_here :].astype(F32),
        )
        piece = piece[t % groups * dim_rows : t % groups * dim_rows + 1]
        tile, start = t * dim_rows // 128, t * dim_rows % 128
        inside = (lane >= start) & (lane < start + dim_rows)
        for which in range(2):
            shift = (start - which * dim_rows) % 128
            moved = pltpu.roll(piece, shift, 1) if shift else piece
            biases[which][tile] = biases[which][tile] + jnp.where(inside, moved, 0.0)
    query_bias, value_bias = [jnp.concatenate(item, axis=1) for item in biases]
    result = matmul(all_ref[...], mat_ref[...])
    query = (result[:, :width_here] + query_bias) * HEAD_DIM ** (-0.5)
    key = result[:, width_here : 2 * width_here]
    values[...] = result[:, 2 * width_here :] + value_bias
    half_parts = groups // 2
    for pair in range(seqs * heads_here):
        which, head = pair // heads_here, pair % heads_here
        columns = slice(head * HEAD_DIM, (head + 1) * HEAD_DIM)
        for k in range(groups):
            spot = slice(k * rows + which * span, k * rows + (which + 1) * span)
            block = jnp.concatenate([query[spot, columns], key[spot, columns]], axis=1)
            for copy in range(repeats):
                sent_ref[pair * repeats + copy, k * span : (k + 1) * span, :] = block.astype(BF16)
        for k in range(half_parts):
            upper = slice(k * rows + which * span, k * rows + (which + 1) * span)
            lower = slice(upper.start + half_parts * rows, upper.stop + half_parts * rows)
            block = jnp.concatenate([values[upper, columns], values[lower, columns]], axis=1)
            for copy in range(repeats):
                sent_ref[
                    pair * repeats + copy, block_rows + k * span : block_rows + (k + 1) * span, :
                ] = block.astype(BF16)


def project(spot, token_parts, mine, other, seqs, heads_here, repeats):
    groups = len(token_parts)
    rows, width = token_parts[0].shape
    rows -= 16
    blocks = seqs * heads_here * repeats
    block_rows = rows // seqs * groups
    vmem = pl.BlockSpec(memory_space=pltpu.VMEM)
    return pl.pallas_call(
        functools.partial(project_kernel, groups, heads_here, repeats),
        in_specs=[pl.BlockSpec(memory_space=pltpu.SMEM)] + [vmem] * (groups + 2),
        out_specs=[vmem] * 3,
        out_shape=[
            jax.ShapeDtypeStruct((blocks, block_rows * 3 // 2 + 16, 128), BF16),
            jax.ShapeDtypeStruct((groups * rows, width), BF16),
            jax.ShapeDtypeStruct((width, 3 * heads_here * HEAD_DIM), BF16),
        ],
        scratch_shapes=[pltpu.VMEM((groups * rows, heads_here * HEAD_DIM), F32)],
        compiler_params=pltpu.CompilerParams(vmem_limit_bytes=40 * 1024 * 1024),
    )(spot, *token_parts, mine, other)


def input_kernel(
    groups, heads_here, repeats, spot_ref, got_ref, mat_ref, all_ref,
    own_ref, others_ref, keep_ref, send_ref, grads, mat_grads,
):
    my_block, my_group = spot_ref[0], spot_ref[1]
    blocks = got_ref.shape[0]
    seqs = blocks // (repeats * heads_here)
    rows = all_ref.shape[0] // groups
    span = rows // seqs
    block_rows = span * groups
    width_here = heads_here * HEAD_DIM
    chip_rows = keep_ref.shape[1] - 16
    half_parts = groups // 2

    def received(pair, start):
        spot = slice(start, start + span)
        total = got_ref[pair * repeats, spot, :].astype(F32)
        for copy in range(1, repeats):
            total = total + got_ref[pair * repeats + copy, spot, :].astype(F32)
        return total

    for which in range(seqs):
        for head in range(0, heads_here, 2):
            pair = which * heads_here + head
            start = head * HEAD_DIM
            for k in range(groups):
                spot = slice(k * rows + which * span, k * rows + (which + 1) * span)
                first, second = received(pair, k * span), received(pair + 1, k * span)
                grads[spot, start : start + 128] = (
                    left_pair(first, second) * HEAD_DIM ** (-0.5)
                ).astype(BF16)
                grads[spot, width_here + start : width_here + start + 128] = right_pair(
                    first, second
                ).astype(BF16)
                inner = block_rows + k % half_parts * span
                first, second = received(pair, inner), received(pair + 1, inner)
                grads[spot, 2 * width_here + start : 2 * width_here + start + 128] = (
                    left_pair(first, second) if k < half_parts else right_pair(first, second)
                ).astype(BF16)
    back = matmul_nt(grads[...], mat_ref[...])
    own_ref[...] = back[:rows]
    for k in range(1, groups):
        others_ref[k - 1] = back[k * rows : (k + 1) * rows].astype(BF16)
    mat_grads[...] = matmul_tn(all_ref[...], grads[...])
    query_sums = jnp.sum(grads[:, :width_here].astype(F32), axis=0, keepdims=True)
    value_sums = jnp.sum(grads[:, 2 * width_here :].astype(F32), axis=0, keepdims=True)
    chunks = blocks // groups
    chunk = width_here // chunks
    row = lax.broadcasted_iota(jnp.int32, (16, 128), 0)
    for k in range(blocks):
        owner = my_block ^ k
        spot = pl.ds(pl.multiple_of(owner * chip_rows, chip_rows), chip_rows)
        block = mat_grads[spot, :]
        sums = []
        for total in (query_sums, value_sums):
            chosen = jnp.zeros((1, chunk), F32)
            for i in range(chunks):
                piece = total[:, i * chunk : (i + 1) * chunk]
                chosen = chosen + jnp.where(owner == my_group * chunks + i, piece, 0.0)
            sums.append(jnp.concatenate([chosen, jnp.zeros((1, 128 - chunk), F32)], axis=1) if chunk < 128 else chosen)
        if k % 2 == 0:
            keep_ref[k // 2, 0:chip_rows, :] = block
        else:
            send_ref[k // 2, 0:chip_rows, :] = block.astype(BF16)
        for i in range(3 * width_here // 128):
            value = jnp.where(row == 0, sums[i], 0.0) if i < 2 else jnp.zeros((16, 128), F32)
            columns = slice(i * 128, (i + 1) * 128)
            if k % 2 == 0:
                keep_ref[k // 2, chip_rows : chip_rows + 16, columns] = value
            else:
                send_ref[k // 2, chip_rows : chip_rows + 16, columns] = value.astype(BF16)


def input_grads(spot, got, mat_three, token_all, heads_here, groups, repeats):
    blocks = got.shape[0]
    total_rows, width = token_all.shape
    rows = total_rows // groups
    chip_rows = width // blocks
    columns = mat_three.shape[1]
    vmem = pl.BlockSpec(memory_space=pltpu.VMEM)
    shape = (blocks // 2, chip_rows + 16, columns)
    return pl.pallas_call(
        functools.partial(input_kernel, groups, heads_here, repeats),
        in_specs=[pl.BlockSpec(memory_space=pltpu.SMEM)] + [vmem] * 3,
        out_specs=[vmem] * 4,
        out_shape=[
            jax.ShapeDtypeStruct((rows, width), F32),
            jax.ShapeDtypeStruct((groups - 1, rows, width), BF16),
            jax.ShapeDtypeStruct(shape, F32),
            jax.ShapeDtypeStruct(shape, BF16),
        ],
        scratch_shapes=[
            pltpu.VMEM((total_rows, columns), BF16),
            pltpu.VMEM((width, columns), F32),
        ],
        compiler_params=pltpu.CompilerParams(vmem_limit_bytes=40 * 1024 * 1024),
    )(spot, got, mat_three, token_all)


def whole_call(kernel, out_shape, arguments, scratch=(), megabytes=40):
    vmem = pl.BlockSpec(memory_space=pltpu.VMEM)
    return pl.pallas_call(
        kernel,
        in_specs=[vmem] * len(arguments),
        out_specs=[vmem] * len(out_shape),
        out_shape=out_shape,
        scratch_shapes=list(scratch),
        compiler_params=pltpu.CompilerParams(vmem_limit_bytes=megabytes * 1024 * 1024),
    )(*arguments)


def ffn_kernel(sent_ref, up_ref, down_ref, bias_ref, out_ref, act_ref, slope_ref):
    hidden = matmul(sent_ref[:, : up_ref.shape[0]], up_ref[...]) + bias_ref[...]
    cdf_part = 0.5 * (1.0 + lax.erf(hidden * 0.7071067811865476))
    act = (hidden * cdf_part).astype(BF16)
    act_ref[...] = act
    slope_ref[...] = cdf_part + hidden * (
        jnp.exp(-0.5 * hidden * hidden) * 0.3989422804014327
    )
    out_ref[...] = matmul(act, down_ref[...]).astype(out_ref.dtype)


def ffn_part(sent, mat_up, mat_down, vec_up, kind):
    rows = sent.shape[0]
    units, width = mat_down.shape
    return whole_call(
        ffn_kernel,
        [
            jax.ShapeDtypeStruct((rows, width), kind),
            jax.ShapeDtypeStruct((rows, units), BF16),
            jax.ShapeDtypeStruct((rows, units), F32),
        ],
        (sent, mat_up, mat_down, vec_up),
    )


def ffn_back_kernel(grad_ref, slope_ref, up_ref, down_ref, out_ref, hidden_ref):
    grad_hidden = (matmul_nt(grad_ref[...], down_ref[...]) * slope_ref[...]).astype(BF16)
    hidden_ref[...] = grad_hidden
    out_ref[...] = matmul_nt(grad_hidden, up_ref[...]).astype(out_ref.dtype)


def ffn_back_part(grad, slope, mat_up, mat_down, kind):
    rows, width = grad.shape
    return whole_call(
        ffn_back_kernel,
        [
            jax.ShapeDtypeStruct((rows, width), kind),
            jax.ShapeDtypeStruct(slope.shape, BF16),
        ],
        (grad, slope, mat_up, mat_down),
    )


def ffn_grads_kernel(groups, blocks, *refs):
    acts, grads, sents, hiddens = [refs[i * groups : (i + 1) * groups] for i in range(4)]
    *outs, sums_ref, left, right = refs[4 * groups :]
    rows, width = grads[0].shape
    units = acts[0].shape[1]
    for k in range(groups):
        spot = slice(k * rows, (k + 1) * rows)
        left[spot, 0:units] = acts[k][...]
        right[spot, 0:width] = grads[k][...]
    result = matmul_tn(left[:, 0:units], right[:, 0:width])
    chunk = units // blocks
    for b in range(blocks):
        outs[0][b, 0:chunk, :] = result[b * chunk : (b + 1) * chunk].astype(BF16)
    for k in range(groups):
        spot = slice(k * rows, (k + 1) * rows)
        left[spot, 0:width] = sents[k][:, 0:width]
        right[spot, 0:units] = hiddens[k][...]
    result = matmul_tn(left[:, 0:width], right[:, 0:units])
    chunk = width // blocks
    for b in range(blocks):
        block = result[b * chunk : (b + 1) * chunk].astype(BF16)
        if len(outs) == 1:
            outs[0][b, units // blocks :, :] = block
        else:
            outs[1][b] = block
    sums_ref[...] = jnp.sum(right[:, 0:units].astype(F32), axis=0, keepdims=True)


def ffn_grads_call(acts, grads, sents, hiddens, blocks):
    groups = len(acts)
    rows, width = grads[0].shape
    units = acts[0].shape[1]
    big = pltpu.VMEM((groups * rows, max(units, width)), BF16)
    if units == width:
        shapes = [jax.ShapeDtypeStruct((blocks, (units + width) // blocks, width), BF16)]
    else:
        shapes = [
            jax.ShapeDtypeStruct((blocks, units // blocks, width), BF16),
            jax.ShapeDtypeStruct((blocks, width // blocks, units), BF16),
        ]
    return whole_call(
        functools.partial(ffn_grads_kernel, groups, blocks),
        shapes + [jax.ShapeDtypeStruct((1, units), F32)],
        (*acts, *grads, *sents, *hiddens),
        (big, big),
    )


def split_kernel(own_ref, *outs):
    groups = own_ref.shape[0]
    dim_rows = outs[0].shape[0]
    columns = own_ref.shape[2] // 3
    total = jnp.zeros(outs[3].shape, F32)
    for group in range(groups):
        block = own_ref[group].astype(F32)
        for which in range(3):
            outs[which][:, group * columns : (group + 1) * columns] = block[
                :dim_rows, which * columns : (which + 1) * columns
            ]
        total = total + block[dim_rows : dim_rows + 8, 0:128]
    outs[3][...] = total


def split_columns(own, dim_rows):
    groups, _, columns = own.shape
    matrix = jax.ShapeDtypeStruct((dim_rows, groups * columns // 3), F32)
    return whole_call(split_kernel, [matrix] * 3 + [jax.ShapeDtypeStruct((8, 128), F32)], (own,))


def place_kernel(groups, blocks, spot_ref, *refs):
    parts, out_ref = refs[:groups], refs[groups]
    chunk = parts[0].shape[1] // blocks
    for k in range(groups):
        for group in range(groups):

            @pl.when((spot_ref[1] ^ k) == group)
            def _():
                for b in range(blocks):
                    start = (b * groups + group) * chunk
                    out_ref[:, start : start + chunk] = parts[k][
                        :, b * chunk : (b + 1) * chunk
                    ].astype(F32)


def place_columns(spot, parts, blocks):
    groups = len(parts)
    rows, columns = parts[0].shape
    chunk = columns // blocks
    if chunk % 128:
        whole = xor_order(jnp.stack(parts), 0, spot[1]).reshape(groups, rows, blocks, chunk)
        return jnp.transpose(whole, (1, 2, 0, 3)).reshape(rows, groups * columns).astype(F32)
    vmem = pl.BlockSpec(memory_space=pltpu.VMEM)
    return pl.pallas_call(
        functools.partial(place_kernel, groups, blocks),
        in_specs=[pl.BlockSpec(memory_space=pltpu.SMEM)] + [vmem] * groups,
        out_specs=vmem,
        out_shape=jax.ShapeDtypeStruct((rows, groups * columns), F32),
    )(spot, *parts)


def out_grads_kernel(groups, *refs):
    sents, grads, (out_ref, left, right) = refs[:groups], refs[groups : 2 * groups], refs[2 * groups :]
    rows, width = grads[0].shape
    for k in range(groups):
        spot = slice(k * rows, (k + 1) * rows)
        left[spot, :] = sents[k][:, width:]
        right[spot, :] = grads[k][...]
    out_ref[...] = matmul_tn(left[...], right[...]).astype(BF16)


def out_grads_call(sents, grads):
    groups = len(sents)
    rows, width = grads[0].shape
    columns = sents[0].shape[1] - width
    return whole_call(
        functools.partial(out_grads_kernel, groups),
        [jax.ShapeDtypeStruct((columns, width), BF16)],
        (*sents, *grads),
        (
            pltpu.VMEM((groups * rows, columns), BF16),
            pltpu.VMEM((groups * rows, width), BF16),
        ),
    )[0]


def per_device(
    tokens,
    cotangent,
    doc_offsets,
    valid_flags,
    w_query,
    w_key,
    w_value,
    w_out,
    w_fc1,
    w_fc2,
    b_query,
    b_value,
    b_out,
    b_fc1,
    b_fc2,
    gain_attn,
    bias_attn,
    gain_ffn,
    bias_ffn,
):
    seqs, span, width = tokens.shape
    groups = lax.axis_size("heads")
    blocks = lax.axis_size("blk")
    devices = groups * blocks
    my_group = lax.axis_index("heads")
    my_block = lax.axis_index("blk")
    rows = seqs * span
    block_rows = span * groups
    length = block_rows * blocks
    heads = width // HEAD_DIM
    heads_here = heads // groups
    pairs = seqs * heads_here
    repeats = blocks // pairs
    parts_length = length // repeats
    width_here = heads_here * HEAD_DIM
    dim_rows = w_query.shape[0]
    unit_rows = w_fc2.shape[0]
    hidden_size = w_fc1.shape[1]
    units_here = hidden_size // groups
    qk_scale = HEAD_DIM ** (-0.5)
    half = block_rows // 2
    wide = span // 2

    token_rows = tokens.reshape(rows, width)
    short = jnp.concatenate(
        [b_out, b_fc2, gain_attn, bias_attn, gain_ffn, bias_ffn, b_fc1]
    )
    short_size = short.shape[0]
    short = jnp.pad(short, (0, 16 * width - short_size)).reshape(16, width)
    token_parts = gather_parts(jnp.concatenate([token_rows, short]), "heads")
    w_three = jnp.concatenate(
        [w.reshape(dim_rows, groups, width_here) for w in (w_query, w_key, w_value)], axis=-1
    )
    w_three = jnp.transpose(w_three, (1, 0, 2))
    def lanes_of(pieces):
        flat = jnp.concatenate(pieces)
        return jnp.pad(flat, (0, dim_rows * 128 - flat.shape[0])).reshape(dim_rows, 128)

    vectors = lanes_of([b_query, b_value])
    w_up = w_fc1.reshape(dim_rows, blocks, groups, unit_rows)
    w_up = jnp.transpose(w_up, (2, 0, 1, 3)).reshape(groups, dim_rows, units_here)
    first = jnp.concatenate(
        [w_three, jnp.broadcast_to(vectors[None], (groups,) + vectors.shape), w_up], axis=-1
    )
    first = lax.all_to_all(first, "heads", split_axis=0, concat_axis=0, tiled=True)
    first = first.reshape(groups * dim_rows, first.shape[-1])
    second = first[:, 3 * width_here + 128 :].reshape(-1, width)
    second = jnp.concatenate([second, w_fc2])
    mat_out = lax.all_gather(w_out, ALL, axis=0, tiled=True)

    first = first[:, : 3 * width_here + 128]
    for part in token_parts[1:]:
        second = after(second, part)
    mine, other = gather_blk_parts(first, second)
    part_blocks = blocks // repeats
    first_turn = my_block % repeats * (parts_length // QUERY_ROWS)
    spot = jnp.stack([my_block, my_group, first_turn, my_block // part_blocks]).astype(jnp.int32)
    sent, token_all, mat_three = project(
        spot, token_parts, mine, other, seqs, heads_here, repeats
    )
    qkv = lax.all_to_all(sent, "blk", split_axis=0, concat_axis=0, tiled=True)


    vectors = qkv[:, block_rows * 3 // 2 :, :].reshape(devices, 16 // groups * 128)[:, :short_size]
    vec_up = vectors[:, 6 * dim_rows : 6 * dim_rows + unit_rows]
    vec_up = vec_up.reshape(blocks, groups, unit_rows)
    vec_up = lax.dynamic_index_in_dim(vec_up, my_group, 1, False).reshape(units_here).astype(F32)
    short = jnp.transpose(vectors[:, : 6 * dim_rows].reshape(devices, 6, dim_rows), (1, 0, 2))
    short = short.reshape(6, width).astype(F32)
    vec_out, vec_down, gain_one, bias_one, gain_two, bias_two = [short[i] for i in range(6)]

    second = after(second, sent)
    if units_here == width:
        second = lax.all_gather(second.reshape(2, unit_rows, width), "blk", axis=1, tiled=True)
        mat_up, mat_down = second[0], second[1]
    else:
        second = lax.all_gather(second, "blk", axis=0, tiled=False)
        up_rows = groups * dim_rows * units_here // width
        mat_up = second[:, :up_rows].reshape(width, units_here)
        mat_down = second[:, up_rows:].reshape(units_here, width)

    my_pair = my_block // repeats
    my_part = my_block % repeats
    my_seq = my_pair // heads_here
    inner = jnp.arange(length, dtype=jnp.int32)
    place = (inner // block_rows) * block_rows + inner % span
    place = place + (((inner // span) % groups) ^ my_group) * span
    offsets = lax.dynamic_index_in_dim(doc_offsets, my_seq, 0, False)
    flags = lax.dynamic_index_in_dim(valid_flags, my_seq, 0, False)
    flags = xor_order(flags.reshape(blocks, groups, span), 1, my_group).reshape(length)
    segment = jnp.sum((offsets[None, :] <= place[:, None]).astype(jnp.int32), axis=1) - 1
    seg_row = segment.reshape(length // QUERY_ROWS, 1, QUERY_ROWS)
    seg_key = jnp.where(flags > 0, segment, -1)
    seg_key = jnp.broadcast_to(seg_key[:, None], (length, 128))
    attn_low, attn_t, lse = attend(spot, seg_row, seg_key, qkv, wide, parts_length)

    sent = jnp.concatenate([attn_low] * repeats, axis=0) if repeats > 1 else attn_low
    got = lax.all_to_all(sent, ALL, split_axis=0, concat_axis=0, tiled=True)
    my_span = my_block * groups + my_group
    local_flags = lax.dynamic_slice_in_dim(valid_flags, my_span * span, span, 1)
    local_flags = local_flags.reshape(rows, 1).astype(F32)
    *sent, normed_one, unit_one, inv_one, squares = join(
        spot, got, token_rows, local_flags, mat_out, short, seqs, heads_here, repeats
    )
    joint_parts = [sent[0]] + [swapped(sent[k], "heads", k) for k in range(1, groups)]
    ffn_results = [
        ffn_part(part, mat_up, mat_down, vec_up[None], F32 if k == 0 else BF16)
        for k, part in enumerate(joint_parts)
    ]
    ffn_others = [swapped(ffn_results[k][0], "heads", k) for k in range(1, groups)]
    output, grad_resid_two, grad_ffn, early, squares = middle(
        ffn_results[0][0], ffn_others, normed_one, short, local_flags,
        cotangent.reshape(rows, width), squares,
    )
    output = output.reshape(tokens.shape)
    grad_ffn_parts = gather_parts(grad_ffn, "heads")
    grad_results = [
        ffn_back_part(part, item[2], mat_up, mat_down, F32 if k == 0 else BF16)
        for k, (part, item) in enumerate(zip(grad_ffn_parts, ffn_results))
    ]
    grad_normed_parts = [item[0] for item in grad_results]
    grad_normed_others = [swapped(grad_normed_parts[k], "heads", k) for k in range(1, groups)]
    *ffn_grads, grad_vec_up = ffn_grads_call(
        [item[1] for item in ffn_results],
        grad_ffn_parts,
        joint_parts,
        [after(grad_results[0][1], grad_normed_others[-1])] + [item[1] for item in grad_results[1:]],
        blocks,
    )
    ffn_grads = [
        lax.psum_scatter(
            item.reshape(-1, item.shape[-1]), "blk", scatter_dimension=0, tiled=True
        )
        for item in ffn_grads
    ]
    if units_here == width:
        shard_down, shard_up = ffn_grads[0][:unit_rows], ffn_grads[0][unit_rows:]
    else:
        shard_down, shard_up = ffn_grads
    shard_down = shard_down.astype(F32)

    sent, grad_resid_one, grad_branch = branch_back(
        spot, grad_normed_parts[0], grad_normed_others, grad_resid_two, unit_one, inv_one,
        gain_one[None], mat_out, early,
        grad_vec_up, squares, seqs, heads_here, repeats, devices,
    )
    got = lax.all_to_all(sent, ALL, split_axis=0, concat_axis=0, tiled=True)
    small = jnp.sum(got[:, wide:].astype(F32), axis=0)
    small = small[:8] + small[8:]
    vector_sums = lax.dynamic_slice_in_dim(small[:6], my_span * dim_rows % 128, dim_rows, 1)
    shard_vec_up = lax.dynamic_slice_in_dim(small[6], my_block * unit_rows % 128, unit_rows, 0)
    real_count = jnp.maximum(jnp.sum(valid_flags.astype(F32)), 1.0)
    rms = jnp.sqrt(small[7, :4] / (real_count * width))

    grads = attend_back(spot, seg_row, seg_key, qkv, got, attn_t, lse)
    branch_parts = gather_parts(after(grad_branch, grads), "heads")
    grad_mat_out = out_grads_call(joint_parts, branch_parts)
    got = lax.all_to_all(grads, "blk", split_axis=0, concat_axis=0, tiled=True)
    shard_up = after(shard_up, grads).reshape(groups, dim_rows, units_here)
    shard_up = xor_order(shard_up, 0, my_group)
    up_parts = [shard_up[0]] + [swapped(shard_up[k], "heads", k) for k in range(1, groups)]
    got = after(got, up_parts[-1])
    shard_out = scatter_blk(after(grad_mat_out, got).reshape(blocks, dim_rows, width)).astype(BF16)
    route = [(j, j % groups * blocks + j // groups) for j in range(devices)]
    shard_out = lax.ppermute(shard_out, ("heads", "blk"), route)
    own_input, other_input, keep, send = input_grads(
        spot, got, mat_three, token_all, heads_here, groups, repeats
    )
    grad_input = grad_resid_one + own_input
    for k in range(1, groups):
        grad_input = grad_input + swapped(other_input[k - 1], "heads", k).astype(F32)
    grad_input = grad_input.reshape(tokens.shape)
    chip_sums = keep + swapped(send, "blk", 1).astype(F32)
    chip_low = chip_sums.astype(BF16)
    three_grads = chip_sums[0]
    for k in range(1, blocks // 2):
        three_grads = three_grads + swapped(chip_low[k], "blk", 2 * k).astype(F32)
    own_rows = three_grads[: groups * dim_rows].reshape(groups, dim_rows, 3 * width_here)
    own_sums = three_grads[groups * dim_rows, :256].reshape(2, 128)[:, : groups * dim_rows]
    own_sums = jnp.transpose(own_sums.reshape(2, groups, dim_rows), (1, 0, 2))
    row = lax.broadcasted_iota(jnp.int32, (1, 16, 1), 1)
    own_sums = jnp.concatenate(
        [
            own_sums.reshape(groups, 2 * dim_rows),
            jnp.zeros((groups, 3 * width_here - 2 * dim_rows), F32),
        ],
        axis=1,
    )
    own_sums = jnp.where(row == 0, own_sums[:, None, :], 0.0)
    own = jnp.concatenate([own_rows, own_sums], axis=1).astype(BF16)
    shard_up = place_columns(after(spot, own), up_parts, blocks)
    own = lax.all_to_all(own, "heads", split_axis=0, concat_axis=0, tiled=True)
    shards_three = split_columns(own, dim_rows)
    shard_sums = shards_three[3][0]

    return (
        output,
        grad_input,
        shards_three[0],
        shards_three[1],
        shards_three[2],
        shard_out.astype(F32),
        shard_up,
        shard_down,
        shard_sums[:dim_rows],
        shard_sums[dim_rows : 2 * dim_rows],
        vector_sums[0],
        shard_vec_up,
        vector_sums[3],
        vector_sums[1],
        vector_sums[2],
        vector_sums[4],
        vector_sums[5],
        rms,
    )


def solution(mesh):
    token_spec = P(None, ALL, None)
    matrix_spec = P(ALL, None)
    vector_spec = P(ALL)
    return jax.shard_map(
        per_device,
        mesh=mesh,
        in_specs=(token_spec,) * 2 + (P(),) * 2 + (matrix_spec,) * 6 + (vector_spec,) * 9,
        out_specs=(token_spec,) * 2 + (matrix_spec,) * 6 + (vector_spec,) * 9 + (P(),),
        check_vma=False,
    )
```

```python
import functools

import jax
import jax.numpy as jnp
from jax import lax
from jax.experimental import pallas as pl
from jax.experimental.pallas import tpu as pltpu
from jax.sharding import PartitionSpec as P

HEAD_DIM = 64
NORM_EPS = 1e-05
NEG_LARGE = -1e30
QUERY_ROWS = 256
BF16 = jnp.bfloat16
F32 = jnp.float32
ALL = ("blk", "heads")


def vmem_limit(length):
    return 8 * 1024 * 1024 + 6 * 1024 * length


def matmul(left, right):
    return jnp.dot(left, right, preferred_element_type=F32)


def matmul_tn(left, right):
    return lax.dot_general(left, right, (((0,), (0,)), ((), ())), preferred_element_type=F32)


def matmul_nt(left, right):
    return lax.dot_general(left, right, (((1,), (1,)), ((), ())), preferred_element_type=F32)


def after(block, other):
    spot = lax.slice(other, (0,) * other.ndim, (1,) * other.ndim).reshape(())
    return block + (spot * 0).astype(block.dtype)


def swapped(block, axis, mask):
    count = lax.axis_size(axis)
    return lax.ppermute(block, axis, [(i, i ^ mask) for i in range(count)])


def gather_parts(block, axis):
    return [block] + [swapped(block, axis, k) for k in range(1, lax.axis_size(axis))]


def scatter_parts(parts, axis):
    total = parts[0].astype(F32)
    for k in range(1, len(parts)):
        total = total + swapped(parts[k].astype(BF16), axis, k).astype(F32)
    return total


def xor_order(array, dim, index):
    pieces = [
        lax.dynamic_index_in_dim(array, index ^ k, dim, True) for k in range(array.shape[dim])
    ]
    return jnp.concatenate(pieces, axis=dim)


def gather_blk_parts(block, first_needs):
    count = lax.axis_size("blk")
    mine = jnp.stack([block] + [swapped(block, "blk", k) for k in range(2, count, 2)])
    mine = after(mine, first_needs)
    return mine, swapped(mine, "blk", 1)


def gather_blk(block, first_needs):
    mine, other = gather_blk_parts(block, first_needs)
    both = jnp.stack([mine, other], axis=1).reshape((-1,) + block.shape)
    return xor_order(both, 0, lax.axis_index("blk"))


def scatter_blk(blocks):
    index = lax.axis_index("blk")
    ordered = xor_order(blocks, 0, index)
    pairs = ordered.reshape((ordered.shape[0] // 2, 2) + ordered.shape[1:])
    total = pairs[:, 0].astype(F32) + swapped(pairs[:, 1], "blk", 1).astype(F32)
    low = total.astype(BF16)
    result = total[0]
    for k in range(1, low.shape[0]):
        result = result + swapped(low[k], "blk", 2 * k).astype(F32)
    return result


def layer_norm(resid, norm_gain, norm_bias):
    center = resid - jnp.mean(resid, axis=-1, keepdims=True)
    inv_std = lax.rsqrt(jnp.mean(center * center, axis=-1, keepdims=True) + NORM_EPS)
    normed = center * inv_std
    return (normed * norm_gain + norm_bias, normed, inv_std)


def norm_back(upstream, normed, inv_std, norm_gain):
    scaled = upstream * norm_gain
    return inv_std * (
        scaled
        - jnp.mean(scaled, axis=-1, keepdims=True)
        - normed * jnp.mean(scaled * normed, axis=-1, keepdims=True)
    )


def gelu_slope(hidden):
    cdf_part = 0.5 * (1.0 + lax.erf(hidden * 0.7071067811865476))
    pdf_part = jnp.exp(-0.5 * hidden * hidden) * 0.3989422804014327
    return cdf_part + hidden * pdf_part


def two_halves(values):
    high = lax.reduce_precision(values, 8, 7)
    return jnp.stack([high, values - high], axis=-1).astype(BF16)


def left_lanes(block):
    lane = lax.broadcasted_iota(jnp.int32, block.shape, 1)
    return jnp.where(lane < HEAD_DIM, block, 0.0)


def masked_scores(seg_key, seg_query, scores):
    width = scores.shape[1] // seg_key.shape[1]
    same = jnp.concatenate([seg_key] * width, axis=1) == seg_query
    return jnp.where(same, scores, NEG_LARGE)


def own_scores(seg_key, seg_query, scores):
    width = scores.shape[1] // seg_key.shape[1]
    same = jnp.concatenate([seg_key] * width, axis=1) == seg_query
    rows = lax.broadcasted_iota(jnp.int32, scores.shape, 0)
    columns = lax.broadcasted_iota(jnp.int32, scores.shape, 1)
    return jnp.where(same | (rows == columns), scores, NEG_LARGE)


def score_all(turn, seg_query, seg_key_ref, qkv_ref, query_t, scores):
    sources, rows = qkv_ref.shape[0], (qkv_ref.shape[1] - 16) * 2 // 3
    per_source = rows // QUERY_ROWS
    query_now = query_t[turn]
    for b in range(sources):
        spot = slice(b * rows, (b + 1) * rows)
        scores[spot, :] = masked_scores(
            seg_key_ref[spot, :], seg_query, matmul(qkv_ref[b, 0:rows, :], query_now)
        )
    own = pl.ds(pl.multiple_of(turn * QUERY_ROWS, QUERY_ROWS), QUERY_ROWS)
    inner = pl.ds(pl.multiple_of(turn % per_source * QUERY_ROWS, QUERY_ROWS), QUERY_ROWS)
    own_pair = qkv_ref[turn // per_source, inner, :]
    scores[own, :] = own_scores(seg_key_ref[own, :], seg_query, matmul(own_pair, query_now))
    return own, own_pair


def turn_queries(b, turned, query_t):
    per_source = turned.shape[1] // QUERY_ROWS
    low = jnp.concatenate([jnp.zeros_like(turned[0:HEAD_DIM]), turned[0:HEAD_DIM]], axis=0)
    for t in range(per_source):
        spot = slice(t * QUERY_ROWS, (t + 1) * QUERY_ROWS)
        query_t[b * per_source + t] = low[:, spot].astype(BF16)


def attend_kernel(
    spot_ref, seg_row_ref, seg_key_ref, qkv_ref, low_ref, attn_ref, lse_ref,
    query_t, values_t, scores,
):
    step = pl.program_id(0)
    sources, rows = qkv_ref.shape[0], (qkv_ref.shape[1] - 16) * 2 // 3
    half = rows // 2

    @pl.when(step == 0)
    def _():
        for b in range(sources):
            turn_queries(b, qkv_ref[b, 0:rows, :].astype(F32).T, query_t)
            turned = qkv_ref[b, rows : rows + half, :].astype(F32).T
            values_t[:, b * rows : b * rows + half] = turned[0:HEAD_DIM].astype(BF16)
            values_t[:, b * rows + half : (b + 1) * rows] = turned[
                HEAD_DIM : 2 * HEAD_DIM
            ].astype(BF16)

    turn = spot_ref[2] + step
    score_all(turn, seg_row_ref[0], seg_key_ref, qkv_ref, query_t, scores)
    top = jnp.max(scores[...], axis=0, keepdims=True)
    total = jnp.zeros_like(top)
    result = jnp.zeros((HEAD_DIM, QUERY_ROWS), F32)
    for b in range(sources):
        spot = slice(b * rows, (b + 1) * rows)
        probs = jnp.exp(scores[spot, :] - top)
        total = total + jnp.sum(probs, axis=0, keepdims=True)
        result = result + matmul(values_t[:, spot], probs.astype(BF16))
    result = result / total
    attn_ref[...] = result
    lse_ref[0] = top + jnp.log(total)
    turned = result.T
    wide = low_ref.shape[1]
    spans = QUERY_ROWS // (2 * wide)
    first = turn % (rows // QUERY_ROWS) * spans
    for t in range(spans):
        left = turned[2 * t * wide : (2 * t + 1) * wide]
        right = turned[(2 * t + 1) * wide : (2 * t + 2) * wide]
        low_ref[spot_ref[1] ^ (first + t)] = jnp.concatenate([left, right], axis=1).astype(BF16)


def attend(spot, seg_row, seg_key, qkv, wide, query_length):
    sources, rows = qkv.shape[0], (qkv.shape[1] - 16) * 2 // 3
    length = sources * rows
    steps = query_length // QUERY_ROWS
    spans = rows // (2 * wide)
    per_source = rows // QUERY_ROWS
    return pl.pallas_call(
        attend_kernel,
        grid_spec=pltpu.PrefetchScalarGridSpec(
            num_scalar_prefetch=1,
            grid=(steps,),
            in_specs=[
                pl.BlockSpec((1, 1, QUERY_ROWS), lambda i, spot: (spot[2] + i, 0, 0)),
                pl.BlockSpec(seg_key.shape, lambda i, spot: (0, 0)),
                pl.BlockSpec(qkv.shape, lambda i, spot: (0, 0, 0)),
            ],
            out_specs=[
                pl.BlockSpec((spans, wide, 128), lambda i, spot: (i // per_source, 0, 0)),
                pl.BlockSpec((HEAD_DIM, QUERY_ROWS), lambda i, spot: (0, i)),
                pl.BlockSpec((1, 1, QUERY_ROWS), lambda i, spot: (i, 0, 0)),
            ],
            scratch_shapes=[
                pltpu.VMEM((length // QUERY_ROWS, 128, QUERY_ROWS), BF16),
                pltpu.VMEM((HEAD_DIM, length), BF16),
                pltpu.VMEM((length, QUERY_ROWS), F32),
            ],
        ),
        out_shape=[
            jax.ShapeDtypeStruct((steps // per_source * spans, wide, 128), BF16),
            jax.ShapeDtypeStruct((HEAD_DIM, query_length), F32),
            jax.ShapeDtypeStruct((steps, 1, QUERY_ROWS), F32),
        ],
        compiler_params=pltpu.CompilerParams(vmem_limit_bytes=vmem_limit(length)),
    )(spot, seg_row, seg_key, qkv)


def attend_back_kernel(
    spot_ref, seg_row_ref, seg_key_ref, qkv_ref, up_ref, attn_ref, lse_ref, grads_ref,
    query_t, keys_t, values, scores, grad_query, grad_key, grad_value,
):
    step = pl.program_id(0)
    sources, rows = qkv_ref.shape[0], (qkv_ref.shape[1] - 16) * 2 // 3
    half = rows // 2
    lane = lax.broadcasted_iota(jnp.int32, (rows, 128), 1)

    @pl.when(step == 0)
    def _():
        for b in range(sources):
            turned = qkv_ref[b, 0:rows, :].astype(F32).T
            turn_queries(b, turned, query_t)
            keys_t[:, b * rows : (b + 1) * rows] = turned[HEAD_DIM : 2 * HEAD_DIM].astype(BF16)
            packed = qkv_ref[b, rows : rows + half, :].astype(F32)
            values[b * rows : b * rows + half, :] = left_lanes(packed).astype(BF16)
            values[b * rows + half : (b + 1) * rows, :] = left_lanes(
                pltpu.roll(packed, HEAD_DIM, 1)
            ).astype(BF16)
        grad_query[...] = jnp.zeros_like(grad_query)
        grad_key[...] = jnp.zeros_like(grad_key)
        grad_value[...] = jnp.zeros_like(grad_value)

    turn = spot_ref[2] + step
    lse = lse_ref[0]
    pieces = []
    spans = QUERY_ROWS // (rows // up_ref.shape[0])
    first = turn % (rows // QUERY_ROWS) * spans
    for t in range(spans):
        packed = up_ref[spot_ref[1] ^ (first + t), 0 : rows // up_ref.shape[0] // 2, :].astype(F32)
        pieces.append(left_lanes(packed))
        pieces.append(left_lanes(pltpu.roll(packed, HEAD_DIM, 1)))
    up_now = jnp.concatenate(pieces, axis=0)
    up_turned = up_now.T
    delta = jnp.sum(up_turned[0:HEAD_DIM] * attn_ref[...], axis=0, keepdims=True)
    up_now = up_now.astype(BF16)
    up_turned = up_turned.astype(BF16)
    own, own_pair = score_all(turn, seg_row_ref[0], seg_key_ref, qkv_ref, query_t, scores)
    query_now = pltpu.roll(own_pair.astype(F32), HEAD_DIM, 1).astype(BF16)
    result = jnp.zeros((HEAD_DIM, QUERY_ROWS), F32)
    for b in range(sources):
        spot = slice(b * rows, (b + 1) * rows)
        probs = jnp.exp(scores[spot, :] - lse)
        grad_probs = matmul(values[spot, :], up_turned)
        grad_scores = (probs * (grad_probs - delta)).astype(BF16)
        grad_value[spot, :] += matmul(probs.astype(BF16), up_now)
        grad_key[spot, :] += matmul(grad_scores, query_now)
        result = result + matmul(keys_t[:, spot], grad_scores)
    grad_query[own, :] = jnp.concatenate([result, jnp.zeros_like(result)], axis=0).T

    @pl.when(step == pl.num_programs(0) - 1)
    def _():
        for b in range(sources):
            spot = slice(b * rows, (b + 1) * rows)
            grads_ref[b, 0:rows, :] = jnp.where(
                lane < HEAD_DIM, grad_query[spot, :], grad_key[spot, :]
            ).astype(BF16)
            upper = grad_value[b * rows : b * rows + half, :]
            lower = grad_value[b * rows + half : (b + 1) * rows, :]
            grads_ref[b, rows : rows + half, :] = (
                upper + pltpu.roll(lower, HEAD_DIM, 1)
            ).astype(BF16)


def attend_back(spot, seg_row, seg_key, qkv, upstream, attn_t, lse):
    sources, rows = qkv.shape[0], (qkv.shape[1] - 16) * 2 // 3
    length = sources * rows
    steps = lse.shape[0]
    groups = upstream.shape[0] // sources
    per_source = rows // QUERY_ROWS
    return pl.pallas_call(
        attend_back_kernel,
        grid_spec=pltpu.PrefetchScalarGridSpec(
            num_scalar_prefetch=1,
            grid=(steps,),
            in_specs=[
                pl.BlockSpec((1, 1, QUERY_ROWS), lambda i, spot: (spot[2] + i, 0, 0)),
                pl.BlockSpec(seg_key.shape, lambda i, spot: (0, 0)),
                pl.BlockSpec(qkv.shape, lambda i, spot: (0, 0, 0)),
                pl.BlockSpec(
                    (groups,) + upstream.shape[1:],
                    lambda i, spot: ((spot[2] + i) // per_source, 0, 0),
                ),
                pl.BlockSpec((HEAD_DIM, QUERY_ROWS), lambda i, spot: (0, i)),
                pl.BlockSpec((1, 1, QUERY_ROWS), lambda i, spot: (i, 0, 0)),
            ],
            out_specs=pl.BlockSpec(
                (sources, rows * 3 // 2, 128), lambda i, spot: (0, 0, 0)
            ),
            scratch_shapes=[
                pltpu.VMEM((length // QUERY_ROWS, 128, QUERY_ROWS), BF16),
                pltpu.VMEM((HEAD_DIM, length), BF16),
                pltpu.VMEM((length, 128), BF16),
                pltpu.VMEM((length, QUERY_ROWS), F32),
                pltpu.VMEM((length, 128), F32),
                pltpu.VMEM((length, 128), F32),
                pltpu.VMEM((length, 128), F32),
            ],
        ),
        out_shape=jax.ShapeDtypeStruct((sources, rows * 3 // 2, 128), BF16),
        compiler_params=pltpu.CompilerParams(vmem_limit_bytes=vmem_limit(length)),
    )(spot, seg_row, seg_key, qkv, upstream, attn_t, lse)


def left_pair(first, second):
    lane = lax.broadcasted_iota(jnp.int32, first.shape, 1)
    return jnp.where(lane < HEAD_DIM, first, pltpu.roll(second, HEAD_DIM, 1))


def right_pair(first, second):
    lane = lax.broadcasted_iota(jnp.int32, first.shape, 1)
    return jnp.where(lane < HEAD_DIM, pltpu.roll(first, HEAD_DIM, 1), second)


def join_kernel(
    seqs, heads_here, repeats, spot_ref, got_ref, tokens_ref, flags_ref, mat_ref, vectors_ref,
    *refs,
):
    sents, (low_ref, normed_ref, unit_ref, inv_ref, squares_ref, attn) = refs[:-6], refs[-6:]
    my_group, part = spot_ref[1], spot_ref[3]
    groups = len(sents)
    wide = got_ref.shape[1]
    width = tokens_ref.shape[1]
    width_here = heads_here * HEAD_DIM
    for which in range(seqs):
        for group in range(groups):
            for head in range(0, heads_here, 2):
                first, second = [
                    got_ref[
                        ((which * heads_here + i) * repeats + part) * groups + group
                    ].astype(F32)
                    for i in (head, head + 1)
                ]
                start = group * width_here + head * HEAD_DIM
                top = 2 * which * wide
                attn[top : top + wide, start : start + 128] = left_pair(first, second).astype(BF16)
                attn[top + wide : top + 2 * wide, start : start + 128] = right_pair(
                    first, second
                ).astype(BF16)
    branch = matmul(attn[...], mat_ref[...]) + vectors_ref[0:1, :]
    resid_in = tokens_ref[...].astype(F32)
    normed, unit, inv_std = layer_norm(resid_in + branch, vectors_ref[2:3, :], vectors_ref[3:4, :])
    normed_ref[...] = normed
    unit_ref[...] = unit
    inv_ref[...] = jnp.broadcast_to(inv_std, inv_ref.shape)
    low_ref[...] = normed.astype(BF16)
    for k in range(groups):
        for group in range(groups):

            @pl.when((my_group ^ k) == group)
            def _():
                sents[k][...] = attn[:, group * width_here : (group + 1) * width_here]

    lane = lax.broadcasted_iota(jnp.int32, squares_ref.shape, 1)
    total = jnp.zeros(squares_ref.shape, F32)
    for i, item in enumerate((resid_in, branch, normed)):
        size = flags_ref[...] * jnp.sum(item * item, axis=1, keepdims=True)
        total = total + jnp.where(lane == i, jnp.sum(size, axis=0, keepdims=True), 0.0)
    squares_ref[...] = total


def join(spot, got, tokens, flags, mat_out, vectors, seqs, heads_here, repeats):
    groups = tokens.shape[1] // (heads_here * HEAD_DIM)
    rows, width = tokens.shape
    vmem = pl.BlockSpec(memory_space=pltpu.VMEM)
    return pl.pallas_call(
        functools.partial(join_kernel, seqs, heads_here, repeats),
        in_specs=[pl.BlockSpec(memory_space=pltpu.SMEM)] + [vmem] * 5,
        out_specs=[vmem] * (groups + 5),
        out_shape=[jax.ShapeDtypeStruct((rows, heads_here * HEAD_DIM), BF16)] * groups
        + [
            jax.ShapeDtypeStruct((rows, width), BF16),
            jax.ShapeDtypeStruct((rows, width), F32),
            jax.ShapeDtypeStruct((rows, width), F32),
            jax.ShapeDtypeStruct((rows, 128), F32),
            jax.ShapeDtypeStruct((1, 128), F32),
        ],
        scratch_shapes=[pltpu.VMEM((rows, width), BF16)],
        compiler_params=pltpu.CompilerParams(vmem_limit_bytes=32 * 1024 * 1024),
    )(spot, got, tokens, flags, mat_out, vectors)


def middle_kernel(others, *refs):
    own_ref, normed_ref, vectors_ref, flags_ref, up_ref, squares_ref = refs[:6]
    parts = refs[6 : 6 + others]
    out_ref, resid_ref, low_ref, early_ref, total_ref = refs[6 + others :]
    ffn = own_ref[...]
    for part in parts:
        ffn = ffn + part[...].astype(F32)
    ffn = ffn + vectors_ref[1:2, :]
    gain = vectors_ref[4:5, :]
    normed, unit, inv_std = layer_norm(normed_ref[...] + ffn, gain, vectors_ref[5:6, :])
    out_ref[...] = normed.astype(BF16)
    upstream = up_ref[...].astype(F32)
    grad_resid = norm_back(upstream, unit, inv_std, gain)
    resid_ref[...] = grad_resid
    low = grad_resid.astype(BF16)
    low_ref[...] = low
    early_ref[0:1, :] = jnp.sum(low.astype(F32), axis=0, keepdims=True)
    early_ref[1:2, :] = jnp.sum(upstream * unit, axis=0, keepdims=True)
    early_ref[2:3, :] = jnp.sum(upstream, axis=0, keepdims=True)
    size = flags_ref[...] * jnp.sum(ffn * ffn, axis=1, keepdims=True)
    lane = lax.broadcasted_iota(jnp.int32, total_ref.shape, 1)
    total_ref[...] = squares_ref[...] + jnp.where(
        lane == 3, jnp.sum(size, axis=0, keepdims=True), 0.0
    )


def middle(own, others, normed, vectors, flags, upstream, squares):
    rows, width = own.shape
    return whole_call(
        functools.partial(middle_kernel, len(others)),
        [
            jax.ShapeDtypeStruct((rows, width), BF16),
            jax.ShapeDtypeStruct((rows, width), F32),
            jax.ShapeDtypeStruct((rows, width), BF16),
            jax.ShapeDtypeStruct((8, width), F32),
            jax.ShapeDtypeStruct((1, 128), F32),
        ],
        (own, normed, vectors, flags, upstream, squares, *others),
    )


def branch_back_kernel(
    seqs, heads_here, repeats, spot_ref, *refs,
):
    (own_ref, resid_ref, unit_ref, inv_ref, gain_ref, mat_ref, early_ref, up_sums_ref,
     squares_ref), others, (sent_ref, grad_ref, low_ref) = refs[:9], refs[9:-3], refs[-3:]
    my_group = spot_ref[1]
    groups = len(others) + 1
    rows, width = own_ref.shape
    span = rows // seqs
    wide = span // 2
    devices = sent_ref.shape[0]
    blocks = devices // groups
    grad_normed = own_ref[...]
    for other in others:
        grad_normed = grad_normed + other[...].astype(F32)
    grad_normed = grad_normed + resid_ref[...]
    unit = unit_ref[...]
    grad_resid = norm_back(grad_normed, unit, inv_ref[:, 0:1], gain_ref[...])
    grad_ref[...] = grad_resid
    low = grad_resid.astype(BF16)
    low_ref[...] = low
    grad_attn = matmul_nt(low, mat_ref[...])
    for which in range(seqs):
        top = which * span
        for group in range(groups):
            for head in range(0, heads_here, 2):
                start = (group * heads_here + head) * HEAD_DIM
                upper = grad_attn[top : top + wide, start : start + 128]
                lower = grad_attn[top + wide : top + span, start : start + 128]
                blocks_two = (left_pair(upper, lower), right_pair(upper, lower))
                for i in range(2):
                    for copy in range(repeats):
                        pair = which * heads_here + head + i
                        place = (pair * repeats + copy) * groups + group
                        sent_ref[place, 0:wide, :] = blocks_two[i].astype(BF16)
    sums = [
        jnp.sum(low.astype(F32), axis=0, keepdims=True),
        jnp.sum(grad_normed * unit, axis=0, keepdims=True),
        jnp.sum(grad_normed, axis=0, keepdims=True),
    ] + [early_ref[i : i + 1, :] for i in range(3)]
    row = lax.broadcasted_iota(jnp.int32, (8, 128), 0)
    dim_rows = width // devices
    unit_rows = up_sums_ref.shape[1] // blocks
    for tile in range(width // 128):
        base = jnp.where(row == 7, squares_ref[...], 0.0)
        for i in range(6):
            base = base + jnp.where(row == i, sums[i][:, tile * 128 : (tile + 1) * 128], 0.0)
        for place in range(tile * 128 // dim_rows, (tile + 1) * 128 // dim_rows):
            start = place // groups * unit_rows // 128 * 128
            mine = jnp.where(my_group == place % groups, up_sums_ref[:, start : start + 128], 0.0)
            block = base + jnp.where(row == 6, mine, 0.0)
            high = block.astype(BF16)
            rest = block - high.astype(F32)
            sent_ref[place, wide : wide + 16, :] = jnp.concatenate(
                [high.astype(F32), rest], axis=0
            ).astype(BF16)


def branch_back(spot, own, others, resid, unit, inv_std, gain, mat_out, early, up_sums, squares,
                seqs, heads_here, repeats, devices):
    rows, width = own.shape
    vmem = pl.BlockSpec(memory_space=pltpu.VMEM)
    return pl.pallas_call(
        functools.partial(branch_back_kernel, seqs, heads_here, repeats),
        in_specs=[pl.BlockSpec(memory_space=pltpu.SMEM)] + [vmem] * (9 + len(others)),
        out_specs=[vmem] * 3,
        out_shape=[
            jax.ShapeDtypeStruct((devices, rows // seqs // 2 + 16, 128), BF16),
            jax.ShapeDtypeStruct((rows, width), F32),
            jax.ShapeDtypeStruct((rows, width), BF16),
        ],
        compiler_params=pltpu.CompilerParams(vmem_limit_bytes=32 * 1024 * 1024),
    )(spot, own, resid, unit, inv_std, gain, mat_out, early, up_sums, squares, *others)


def project_kernel(groups, heads_here, repeats, spot_ref, *refs):
    tokens, (mine_ref, other_ref, sent_ref, all_ref, mat_ref, values) = refs[:groups], refs[groups:]
    my_block, my_group = spot_ref[0], spot_ref[1]
    halves, chip_rows, _ = mine_ref.shape
    blocks = 2 * halves
    dim_rows = chip_rows // groups
    rows, width = all_ref.shape[0] // groups, all_ref.shape[1]
    width_here = heads_here * HEAD_DIM
    seqs = sent_ref.shape[0] // (repeats * heads_here)
    span = rows // seqs
    block_rows = span * groups
    each = 16 // groups
    row = lax.broadcasted_iota(jnp.int32, (16, 128), 0)
    short = jnp.zeros((16, 128), F32)
    for k in range(groups):
        all_ref[k * rows : (k + 1) * rows, :] = tokens[k][0:rows, :]
        vectors = tokens[k][rows : rows + 16, :].astype(F32)
        for i in range(each):
            piece = vectors[0:1, i * 128 : (i + 1) * 128]
            short = short + jnp.where(row == (my_group ^ k) * each + i, piece, 0.0)
    for place in range(sent_ref.shape[0]):
        sent_ref[place, block_rows * 3 // 2 :, :] = short.astype(BF16)
    for b in range(blocks):
        place = my_block ^ b
        spot = slice(b * chip_rows, (b + 1) * chip_rows)

        @pl.when(place % 2 == 0)
        def _():
            mat_ref[spot, :] = mine_ref[place // 2, :, 0 : 3 * width_here]

        @pl.when(place % 2 == 1)
        def _():
            mat_ref[spot, :] = other_ref[place // 2, :, 0 : 3 * width_here]

    lane = lax.broadcasted_iota(jnp.int32, (1, 128), 1)
    tiles = width_here // 128
    biases = [[jnp.zeros((1, 128), F32) for _ in range(tiles)] for _ in range(2)]
    for t in range(blocks):
        place = my_block ^ (my_group * (blocks // groups) + t // groups)
        piece = jnp.where(
            place % 2 == 0,
            mine_ref[place // 2, :, 3 * width_here :].astype(F32),
            other_ref[place // 2, :, 3 * width_here :].astype(F32),
        )
        piece = piece[t % groups * dim_rows : t % groups * dim_rows + 1]
        tile, start = t * dim_rows // 128, t * dim_rows % 128
        inside = (lane >= start) & (lane < start + dim_rows)
        for which in range(2):
            shift = (start - which * dim_rows) % 128
            moved = pltpu.roll(piece, shift, 1) if shift else piece
            biases[which][tile] = biases[which][tile] + jnp.where(inside, moved, 0.0)
    query_bias, value_bias = [jnp.concatenate(item, axis=1) for item in biases]
    result = matmul(all_ref[...], mat_ref[...])
    query = (result[:, :width_here] + query_bias) * HEAD_DIM ** (-0.5)
    key = result[:, width_here : 2 * width_here]
    values[...] = result[:, 2 * width_here :] + value_bias
    half_parts = groups // 2
    for pair in range(seqs * heads_here):
        which, head = pair // heads_here, pair % heads_here
        columns = slice(head * HEAD_DIM, (head + 1) * HEAD_DIM)
        for k in range(groups):
            spot = slice(k * rows + which * span, k * rows + (which + 1) * span)
            block = jnp.concatenate([query[spot, columns], key[spot, columns]], axis=1)
            for copy in range(repeats):
                sent_ref[pair * repeats + copy, k * span : (k + 1) * span, :] = block.astype(BF16)
        for k in range(half_parts):
            upper = slice(k * rows + which * span, k * rows + (which + 1) * span)
            lower = slice(upper.start + half_parts * rows, upper.stop + half_parts * rows)
            block = jnp.concatenate([values[upper, columns], values[lower, columns]], axis=1)
            for copy in range(repeats):
                sent_ref[
                    pair * repeats + copy, block_rows + k * span : block_rows + (k + 1) * span, :
                ] = block.astype(BF16)


def project(spot, token_parts, mine, other, seqs, heads_here, repeats):
    groups = len(token_parts)
    rows, width = token_parts[0].shape
    rows -= 16
    blocks = seqs * heads_here * repeats
    block_rows = rows // seqs * groups
    vmem = pl.BlockSpec(memory_space=pltpu.VMEM)
    return pl.pallas_call(
        functools.partial(project_kernel, groups, heads_here, repeats),
        in_specs=[pl.BlockSpec(memory_space=pltpu.SMEM)] + [vmem] * (groups + 2),
        out_specs=[vmem] * 3,
        out_shape=[
            jax.ShapeDtypeStruct((blocks, block_rows * 3 // 2 + 16, 128), BF16),
            jax.ShapeDtypeStruct((groups * rows, width), BF16),
            jax.ShapeDtypeStruct((width, 3 * heads_here * HEAD_DIM), BF16),
        ],
        scratch_shapes=[pltpu.VMEM((groups * rows, heads_here * HEAD_DIM), F32)],
        compiler_params=pltpu.CompilerParams(vmem_limit_bytes=40 * 1024 * 1024),
    )(spot, *token_parts, mine, other)


def input_kernel(
    groups, heads_here, repeats, spot_ref, got_ref, mat_ref, all_ref,
    own_ref, others_ref, keep_ref, send_ref, grads, mat_grads,
):
    my_block, my_group = spot_ref[0], spot_ref[1]
    blocks = got_ref.shape[0]
    seqs = blocks // (repeats * heads_here)
    rows = all_ref.shape[0] // groups
    span = rows // seqs
    block_rows = span * groups
    width_here = heads_here * HEAD_DIM
    chip_rows = keep_ref.shape[1] - 16
    half_parts = groups // 2

    def received(pair, start):
        spot = slice(start, start + span)
        total = got_ref[pair * repeats, spot, :].astype(F32)
        for copy in range(1, repeats):
            total = total + got_ref[pair * repeats + copy, spot, :].astype(F32)
        return total

    for which in range(seqs):
        for head in range(0, heads_here, 2):
            pair = which * heads_here + head
            start = head * HEAD_DIM
            for k in range(groups):
                spot = slice(k * rows + which * span, k * rows + (which + 1) * span)
                first, second = received(pair, k * span), received(pair + 1, k * span)
                grads[spot, start : start + 128] = (
                    left_pair(first, second) * HEAD_DIM ** (-0.5)
                ).astype(BF16)
                grads[spot, width_here + start : width_here + start + 128] = right_pair(
                    first, second
                ).astype(BF16)
                inner = block_rows + k % half_parts * span
                first, second = received(pair, inner), received(pair + 1, inner)
                grads[spot, 2 * width_here + start : 2 * width_here + start + 128] = (
                    left_pair(first, second) if k < half_parts else right_pair(first, second)
                ).astype(BF16)
    back = matmul_nt(grads[...], mat_ref[...])
    own_ref[...] = back[:rows]
    for k in range(1, groups):
        others_ref[k - 1] = back[k * rows : (k + 1) * rows].astype(BF16)
    mat_grads[...] = matmul_tn(all_ref[...], grads[...])
    query_sums = jnp.sum(grads[:, :width_here].astype(F32), axis=0, keepdims=True)
    value_sums = jnp.sum(grads[:, 2 * width_here :].astype(F32), axis=0, keepdims=True)
    chunks = blocks // groups
    chunk = width_here // chunks
    row = lax.broadcasted_iota(jnp.int32, (16, 128), 0)
    for k in range(blocks):
        owner = my_block ^ k
        spot = pl.ds(pl.multiple_of(owner * chip_rows, chip_rows), chip_rows)
        block = mat_grads[spot, :]
        sums = []
        for total in (query_sums, value_sums):
            chosen = jnp.zeros((1, chunk), F32)
            for i in range(chunks):
                piece = total[:, i * chunk : (i + 1) * chunk]
                chosen = chosen + jnp.where(owner == my_group * chunks + i, piece, 0.0)
            sums.append(jnp.concatenate([chosen, jnp.zeros((1, 128 - chunk), F32)], axis=1) if chunk < 128 else chosen)
        if k % 2 == 0:
            keep_ref[k // 2, 0:chip_rows, :] = block
        else:
            send_ref[k // 2, 0:chip_rows, :] = block.astype(BF16)
        for i in range(3 * width_here // 128):
            value = jnp.where(row == 0, sums[i], 0.0) if i < 2 else jnp.zeros((16, 128), F32)
            columns = slice(i * 128, (i + 1) * 128)
            if k % 2 == 0:
                keep_ref[k // 2, chip_rows : chip_rows + 16, columns] = value
            else:
                send_ref[k // 2, chip_rows : chip_rows + 16, columns] = value.astype(BF16)


def input_grads(spot, got, mat_three, token_all, heads_here, groups, repeats):
    blocks = got.shape[0]
    total_rows, width = token_all.shape
    rows = total_rows // groups
    chip_rows = width // blocks
    columns = mat_three.shape[1]
    vmem = pl.BlockSpec(memory_space=pltpu.VMEM)
    shape = (blocks // 2, chip_rows + 16, columns)
    return pl.pallas_call(
        functools.partial(input_kernel, groups, heads_here, repeats),
        in_specs=[pl.BlockSpec(memory_space=pltpu.SMEM)] + [vmem] * 3,
        out_specs=[vmem] * 4,
        out_shape=[
            jax.ShapeDtypeStruct((rows, width), F32),
            jax.ShapeDtypeStruct((groups - 1, rows, width), BF16),
            jax.ShapeDtypeStruct(shape, F32),
            jax.ShapeDtypeStruct(shape, BF16),
        ],
        scratch_shapes=[
            pltpu.VMEM((total_rows, columns), BF16),
            pltpu.VMEM((width, columns), F32),
        ],
        compiler_params=pltpu.CompilerParams(vmem_limit_bytes=40 * 1024 * 1024),
    )(spot, got, mat_three, token_all)


def whole_call(kernel, out_shape, arguments, scratch=(), megabytes=40):
    vmem = pl.BlockSpec(memory_space=pltpu.VMEM)
    return pl.pallas_call(
        kernel,
        in_specs=[vmem] * len(arguments),
        out_specs=[vmem] * len(out_shape),
        out_shape=out_shape,
        scratch_shapes=list(scratch),
        compiler_params=pltpu.CompilerParams(vmem_limit_bytes=megabytes * 1024 * 1024),
    )(*arguments)


def ffn_kernel(sent_ref, up_ref, down_ref, bias_ref, out_ref, act_ref, slope_ref):
    hidden = matmul(sent_ref[:, : up_ref.shape[0]], up_ref[...]) + bias_ref[...]
    cdf_part = 0.5 * (1.0 + lax.erf(hidden * 0.7071067811865476))
    act = (hidden * cdf_part).astype(BF16)
    act_ref[...] = act
    slope_ref[...] = cdf_part + hidden * (
        jnp.exp(-0.5 * hidden * hidden) * 0.3989422804014327
    )
    out_ref[...] = matmul(act, down_ref[...]).astype(out_ref.dtype)


def ffn_part(sent, mat_up, mat_down, vec_up, kind):
    rows = sent.shape[0]
    units, width = mat_down.shape
    return whole_call(
        ffn_kernel,
        [
            jax.ShapeDtypeStruct((rows, width), kind),
            jax.ShapeDtypeStruct((rows, units), BF16),
            jax.ShapeDtypeStruct((rows, units), F32),
        ],
        (sent, mat_up, mat_down, vec_up),
    )


def ffn_back_kernel(grad_ref, slope_ref, up_ref, down_ref, out_ref, hidden_ref):
    grad_hidden = (matmul_nt(grad_ref[...], down_ref[...]) * slope_ref[...]).astype(BF16)
    hidden_ref[...] = grad_hidden
    out_ref[...] = matmul_nt(grad_hidden, up_ref[...]).astype(out_ref.dtype)


def ffn_back_part(grad, slope, mat_up, mat_down, kind):
    rows, width = grad.shape
    return whole_call(
        ffn_back_kernel,
        [
            jax.ShapeDtypeStruct((rows, width), kind),
            jax.ShapeDtypeStruct(slope.shape, BF16),
        ],
        (grad, slope, mat_up, mat_down),
    )


def ffn_grads_kernel(groups, blocks, *refs):
    acts, grads, sents, hiddens = [refs[i * groups : (i + 1) * groups] for i in range(4)]
    *outs, sums_ref, left, right = refs[4 * groups :]
    rows, width = grads[0].shape
    units = acts[0].shape[1]
    for k in range(groups):
        spot = slice(k * rows, (k + 1) * rows)
        left[spot, 0:units] = acts[k][...]
        right[spot, 0:width] = grads[k][...]
    result = matmul_tn(left[:, 0:units], right[:, 0:width])
    chunk = units // blocks
    for b in range(blocks):
        outs[0][b, 0:chunk, :] = result[b * chunk : (b + 1) * chunk].astype(BF16)
    for k in range(groups):
        spot = slice(k * rows, (k + 1) * rows)
        left[spot, 0:width] = sents[k][:, 0:width]
        right[spot, 0:units] = hiddens[k][...]
    result = matmul_tn(left[:, 0:width], right[:, 0:units])
    chunk = width // blocks
    for b in range(blocks):
        block = result[b * chunk : (b + 1) * chunk].astype(BF16)
        if len(outs) == 1:
            outs[0][b, units // blocks :, :] = block
        else:
            outs[1][b] = block
    sums_ref[...] = jnp.sum(right[:, 0:units].astype(F32), axis=0, keepdims=True)


def ffn_grads_call(acts, grads, sents, hiddens, blocks):
    groups = len(acts)
    rows, width = grads[0].shape
    units = acts[0].shape[1]
    big = pltpu.VMEM((groups * rows, max(units, width)), BF16)
    if units == width:
        shapes = [jax.ShapeDtypeStruct((blocks, (units + width) // blocks, width), BF16)]
    else:
        shapes = [
            jax.ShapeDtypeStruct((blocks, units // blocks, width), BF16),
            jax.ShapeDtypeStruct((blocks, width // blocks, units), BF16),
        ]
    return whole_call(
        functools.partial(ffn_grads_kernel, groups, blocks),
        shapes + [jax.ShapeDtypeStruct((1, units), F32)],
        (*acts, *grads, *sents, *hiddens),
        (big, big),
    )


def split_kernel(own_ref, *outs):
    groups = own_ref.shape[0]
    dim_rows = outs[0].shape[0]
    columns = own_ref.shape[2] // 3
    total = jnp.zeros(outs[3].shape, F32)
    for group in range(groups):
        block = own_ref[group].astype(F32)
        for which in range(3):
            outs[which][:, group * columns : (group + 1) * columns] = block[
                :dim_rows, which * columns : (which + 1) * columns
            ]
        total = total + block[dim_rows : dim_rows + 8, 0:128]
    outs[3][...] = total


def split_columns(own, dim_rows):
    groups, _, columns = own.shape
    matrix = jax.ShapeDtypeStruct((dim_rows, groups * columns // 3), F32)
    return whole_call(split_kernel, [matrix] * 3 + [jax.ShapeDtypeStruct((8, 128), F32)], (own,))


def place_kernel(groups, blocks, spot_ref, *refs):
    parts, out_ref = refs[:groups], refs[groups]
    chunk = parts[0].shape[1] // blocks
    for k in range(groups):
        for group in range(groups):

            @pl.when((spot_ref[1] ^ k) == group)
            def _():
                for b in range(blocks):
                    start = (b * groups + group) * chunk
                    out_ref[:, start : start + chunk] = parts[k][
                        :, b * chunk : (b + 1) * chunk
                    ].astype(F32)


def place_columns(spot, parts, blocks):
    groups = len(parts)
    rows, columns = parts[0].shape
    chunk = columns // blocks
    if chunk % 128:
        whole = xor_order(jnp.stack(parts), 0, spot[1]).reshape(groups, rows, blocks, chunk)
        return jnp.transpose(whole, (1, 2, 0, 3)).reshape(rows, groups * columns).astype(F32)
    vmem = pl.BlockSpec(memory_space=pltpu.VMEM)
    return pl.pallas_call(
        functools.partial(place_kernel, groups, blocks),
        in_specs=[pl.BlockSpec(memory_space=pltpu.SMEM)] + [vmem] * groups,
        out_specs=vmem,
        out_shape=jax.ShapeDtypeStruct((rows, groups * columns), F32),
    )(spot, *parts)


def out_grads_kernel(groups, *refs):
    sents, grads, (out_ref, left, right) = refs[:groups], refs[groups : 2 * groups], refs[2 * groups :]
    rows, width = grads[0].shape
    for k in range(groups):
        spot = slice(k * rows, (k + 1) * rows)
        left[spot, :] = sents[k][...]
        right[spot, :] = grads[k][...]
    out_ref[...] = matmul_tn(left[...], right[...]).astype(BF16)


def out_grads_call(sents, grads):
    groups = len(sents)
    rows, width = grads[0].shape
    columns = sents[0].shape[1]
    return whole_call(
        functools.partial(out_grads_kernel, groups),
        [jax.ShapeDtypeStruct((columns, width), BF16)],
        (*sents, *grads),
        (
            pltpu.VMEM((groups * rows, columns), BF16),
            pltpu.VMEM((groups * rows, width), BF16),
        ),
    )[0]


def per_device(
    tokens,
    cotangent,
    doc_offsets,
    valid_flags,
    w_query,
    w_key,
    w_value,
    w_out,
    w_fc1,
    w_fc2,
    b_query,
    b_value,
    b_out,
    b_fc1,
    b_fc2,
    gain_attn,
    bias_attn,
    gain_ffn,
    bias_ffn,
):
    seqs, span, width = tokens.shape
    groups = lax.axis_size("heads")
    blocks = lax.axis_size("blk")
    devices = groups * blocks
    my_group = lax.axis_index("heads")
    my_block = lax.axis_index("blk")
    rows = seqs * span
    block_rows = span * groups
    length = block_rows * blocks
    heads = width // HEAD_DIM
    heads_here = heads // groups
    pairs = seqs * heads_here
    repeats = blocks // pairs
    parts_length = length // repeats
    width_here = heads_here * HEAD_DIM
    dim_rows = w_query.shape[0]
    unit_rows = w_fc2.shape[0]
    hidden_size = w_fc1.shape[1]
    units_here = hidden_size // groups
    qk_scale = HEAD_DIM ** (-0.5)
    half = block_rows // 2
    wide = span // 2

    token_rows = tokens.reshape(rows, width)
    short = jnp.concatenate(
        [b_out, b_fc2, gain_attn, bias_attn, gain_ffn, bias_ffn, b_fc1]
    )
    short_size = short.shape[0]
    short = jnp.pad(short, (0, 16 * width - short_size)).reshape(16, width)
    token_parts = gather_parts(jnp.concatenate([token_rows, short]), "heads")
    w_three = jnp.concatenate(
        [w.reshape(dim_rows, groups, width_here) for w in (w_query, w_key, w_value)], axis=-1
    )
    w_three = jnp.transpose(w_three, (1, 0, 2))
    def lanes_of(pieces):
        flat = jnp.concatenate(pieces)
        return jnp.pad(flat, (0, dim_rows * 128 - flat.shape[0])).reshape(dim_rows, 128)

    vectors = lanes_of([b_query, b_value])
    w_up = w_fc1.reshape(dim_rows, blocks, groups, unit_rows)
    w_up = jnp.transpose(w_up, (2, 0, 1, 3)).reshape(groups, dim_rows, units_here)
    first = jnp.concatenate(
        [w_three, jnp.broadcast_to(vectors[None], (groups,) + vectors.shape), w_up], axis=-1
    )
    first = lax.all_to_all(first, "heads", split_axis=0, concat_axis=0, tiled=True)
    first = first.reshape(groups * dim_rows, first.shape[-1])
    second = first[:, 3 * width_here + 128 :].reshape(-1, width)
    second = jnp.concatenate([second, w_fc2])
    mat_out = lax.all_gather(w_out, ALL, axis=0, tiled=True)

    first = first[:, : 3 * width_here + 128]
    for part in token_parts[1:]:
        second = after(second, part)
    mine, other = gather_blk_parts(first, second)
    part_blocks = blocks // repeats
    first_turn = my_block % repeats * (parts_length // QUERY_ROWS)
    spot = jnp.stack([my_block, my_group, first_turn, my_block // part_blocks]).astype(jnp.int32)
    sent, token_all, mat_three = project(
        spot, token_parts, mine, other, seqs, heads_here, repeats
    )
    qkv = lax.all_to_all(sent, "blk", split_axis=0, concat_axis=0, tiled=True)


    vectors = qkv[:, block_rows * 3 // 2 :, :].reshape(devices, 16 // groups * 128)[:, :short_size]
    vec_up = vectors[:, 6 * dim_rows : 6 * dim_rows + unit_rows]
    vec_up = vec_up.reshape(blocks, groups, unit_rows)
    vec_up = lax.dynamic_index_in_dim(vec_up, my_group, 1, False).reshape(units_here).astype(F32)
    short = jnp.transpose(vectors[:, : 6 * dim_rows].reshape(devices, 6, dim_rows), (1, 0, 2))
    short = short.reshape(6, width).astype(F32)
    vec_out, vec_down, gain_one, bias_one, gain_two, bias_two = [short[i] for i in range(6)]

    second = after(second, sent)
    if units_here == width:
        second = lax.all_gather(second.reshape(2, unit_rows, width), "blk", axis=1, tiled=True)
        mat_up, mat_down = second[0], second[1]
    else:
        second = lax.all_gather(second, "blk", axis=0, tiled=False)
        up_rows = groups * dim_rows * units_here // width
        mat_up = second[:, :up_rows].reshape(width, units_here)
        mat_down = second[:, up_rows:].reshape(units_here, width)

    my_pair = my_block // repeats
    my_part = my_block % repeats
    my_seq = my_pair // heads_here
    inner = jnp.arange(length, dtype=jnp.int32)
    place = (inner // block_rows) * block_rows + inner % span
    place = place + (((inner // span) % groups) ^ my_group) * span
    offsets = lax.dynamic_index_in_dim(doc_offsets, my_seq, 0, False)
    flags = lax.dynamic_index_in_dim(valid_flags, my_seq, 0, False)
    flags = xor_order(flags.reshape(blocks, groups, span), 1, my_group).reshape(length)
    segment = jnp.sum((offsets[None, :] <= place[:, None]).astype(jnp.int32), axis=1) - 1
    seg_row = segment.reshape(length // QUERY_ROWS, 1, QUERY_ROWS)
    seg_key = jnp.where(flags > 0, segment, -1)
    seg_key = jnp.broadcast_to(seg_key[:, None], (length, 128))
    attn_low, attn_t, lse = attend(spot, seg_row, seg_key, qkv, wide, parts_length)

    sent = jnp.concatenate([attn_low] * repeats, axis=0) if repeats > 1 else attn_low
    got = lax.all_to_all(sent, ALL, split_axis=0, concat_axis=0, tiled=True)
    my_span = my_block * groups + my_group
    local_flags = lax.dynamic_slice_in_dim(valid_flags, my_span * span, span, 1)
    local_flags = local_flags.reshape(rows, 1).astype(F32)
    *attn_sent, normed_low, normed_one, unit_one, inv_one, squares = join(
        spot, got, token_rows, local_flags, mat_out, short, seqs, heads_here, repeats
    )
    joint_parts = gather_parts(normed_low, "heads")
    ffn_results = [
        ffn_part(part, mat_up, mat_down, vec_up[None], F32 if k == 0 else BF16)
        for k, part in enumerate(joint_parts)
    ]
    ffn_others = [swapped(ffn_results[k][0], "heads", k) for k in range(1, groups)]
    output, grad_resid_two, grad_ffn, early, squares = middle(
        ffn_results[0][0], ffn_others, normed_one, short, local_flags,
        cotangent.reshape(rows, width), squares,
    )
    output = output.reshape(tokens.shape)
    grad_ffn_parts = gather_parts(grad_ffn, "heads")
    grad_results = [
        ffn_back_part(part, item[2], mat_up, mat_down, F32 if k == 0 else BF16)
        for k, (part, item) in enumerate(zip(grad_ffn_parts, ffn_results))
    ]
    grad_normed_parts = [item[0] for item in grad_results]
    grad_normed_others = [swapped(grad_normed_parts[k], "heads", k) for k in range(1, groups)]
    *ffn_grads, grad_vec_up = ffn_grads_call(
        [item[1] for item in ffn_results],
        grad_ffn_parts,
        joint_parts,
        [after(grad_results[0][1], grad_normed_others[-1])] + [item[1] for item in grad_results[1:]],
        blocks,
    )
    ffn_grads = [
        lax.psum_scatter(
            item.reshape(-1, item.shape[-1]), "blk", scatter_dimension=0, tiled=True
        )
        for item in ffn_grads
    ]
    if units_here == width:
        shard_down, shard_up = ffn_grads[0][:unit_rows], ffn_grads[0][unit_rows:]
    else:
        shard_down, shard_up = ffn_grads
    shard_down = shard_down.astype(F32)

    sent, grad_resid_one, grad_branch = branch_back(
        spot, grad_normed_parts[0], grad_normed_others, grad_resid_two, unit_one, inv_one,
        gain_one[None], mat_out, early,
        grad_vec_up, squares, seqs, heads_here, repeats, devices,
    )
    got = lax.all_to_all(sent, ALL, split_axis=0, concat_axis=0, tiled=True)
    small = jnp.sum(got[:, wide:].astype(F32), axis=0)
    small = small[:8] + small[8:]
    vector_sums = lax.dynamic_slice_in_dim(small[:6], my_span * dim_rows % 128, dim_rows, 1)
    shard_vec_up = lax.dynamic_slice_in_dim(small[6], my_block * unit_rows % 128, unit_rows, 0)
    real_count = jnp.maximum(jnp.sum(valid_flags.astype(F32)), 1.0)
    rms = jnp.sqrt(small[7, :4] / (real_count * width))

    attn_parts = [attn_sent[0]] + [
        swapped(after(attn_sent[k], grad_branch), "heads", k) for k in range(1, groups)
    ]
    got = after(got, attn_parts[-1])
    grads = attend_back(spot, seg_row, seg_key, qkv, got, attn_t, lse)
    branch_parts = gather_parts(after(grad_branch, grads), "heads")
    grad_mat_out = out_grads_call(attn_parts, branch_parts)
    got = lax.all_to_all(grads, "blk", split_axis=0, concat_axis=0, tiled=True)
    shard_up = after(shard_up, grads).reshape(groups, dim_rows, units_here)
    shard_up = xor_order(shard_up, 0, my_group)
    up_parts = [shard_up[0]] + [swapped(shard_up[k], "heads", k) for k in range(1, groups)]
    got = after(got, up_parts[-1])
    shard_out = scatter_blk(after(grad_mat_out, got).reshape(blocks, dim_rows, width)).astype(BF16)
    route = [(j, j % groups * blocks + j // groups) for j in range(devices)]
    shard_out = lax.ppermute(shard_out, ("heads", "blk"), route)
    own_input, other_input, keep, send = input_grads(
        spot, got, mat_three, token_all, heads_here, groups, repeats
    )
    grad_input = grad_resid_one + own_input
    for k in range(1, groups):
        grad_input = grad_input + swapped(other_input[k - 1], "heads", k).astype(F32)
    grad_input = grad_input.reshape(tokens.shape)
    chip_sums = keep + swapped(send, "blk", 1).astype(F32)
    chip_low = chip_sums.astype(BF16)
    three_grads = chip_sums[0]
    for k in range(1, blocks // 2):
        three_grads = three_grads + swapped(chip_low[k], "blk", 2 * k).astype(F32)
    own_rows = three_grads[: groups * dim_rows].reshape(groups, dim_rows, 3 * width_here)
    own_sums = three_grads[groups * dim_rows, :256].reshape(2, 128)[:, : groups * dim_rows]
    own_sums = jnp.transpose(own_sums.reshape(2, groups, dim_rows), (1, 0, 2))
    row = lax.broadcasted_iota(jnp.int32, (1, 16, 1), 1)
    own_sums = jnp.concatenate(
        [
            own_sums.reshape(groups, 2 * dim_rows),
            jnp.zeros((groups, 3 * width_here - 2 * dim_rows), F32),
        ],
        axis=1,
    )
    own_sums = jnp.where(row == 0, own_sums[:, None, :], 0.0)
    own = jnp.concatenate([own_rows, own_sums], axis=1).astype(BF16)
    shard_up = place_columns(after(spot, own), up_parts, blocks)
    own = lax.all_to_all(own, "heads", split_axis=0, concat_axis=0, tiled=True)
    shards_three = split_columns(own, dim_rows)
    shard_sums = shards_three[3][0]

    return (
        output,
        grad_input,
        shards_three[0],
        shards_three[1],
        shards_three[2],
        shard_out.astype(F32),
        shard_up,
        shard_down,
        shard_sums[:dim_rows],
        shard_sums[dim_rows : 2 * dim_rows],
        vector_sums[0],
        shard_vec_up,
        vector_sums[3],
        vector_sums[1],
        vector_sums[2],
        vector_sums[4],
        vector_sums[5],
        rms,
    )


def solution(mesh):
    token_spec = P(None, ALL, None)
    matrix_spec = P(ALL, None)
    vector_spec = P(ALL)
    return jax.shard_map(
        per_device,
        mesh=mesh,
        in_specs=(token_spec,) * 2 + (P(),) * 2 + (matrix_spec,) * 6 + (vector_spec,) * 9,
        out_specs=(token_spec,) * 2 + (matrix_spec,) * 6 + (vector_spec,) * 9 + (P(),),
        check_vma=False,
    )
```
